256 devices in a mesh: grp: 16 (over z, core), dom: 16 (over x, y).
Axes of the slice: x: 4, y: 4, z: 8, core: 2. Of those that a mesh axis runs over, the one named last changes fastest.
Arguments:
- query: bfloat16 [65536, 512], P(('grp', 'dom')), may hold values from -9 to 9
- key: bfloat16 [65536, 512], P(('grp', 'dom')), may hold values from -6 to 6
- value: bfloat16 [65536, 512], P(('grp', 'dom')), may hold values from -6 to 6
- cotangent: bfloat16 [65536, 512], P(('grp', 'dom')), may hold values from -6 to 6
- tile_index: int32 [256, 8, 3], P(('grp', 'dom')), may hold values from 0 to 15, as said below
- tile_mask: int32 [256, 8, 128, 128], P(('grp', 'dom')), may hold values 0 or 1
- tile_count: int32 [256], P(('grp', 'dom')), may hold values from 1 to 8, as said below
- partner: int32 [256, 4], P(('grp', 'dom')), may hold values from 0 to 255, as said below
- pair_edges: int32 [256, 4, 64, 2], P(('grp', 'dom')), may hold values from 0 to 255, as said below
Outputs:
- attended: bfloat16 [65536, 512], P(('grp', 'dom'))
- grad_query: bfloat16 [65536, 512], P(('grp', 'dom'))
- grad_key: bfloat16 [65536, 512], P(('grp', 'dom'))
- grad_value: bfloat16 [65536, 512], P(('grp', 'dom'))
The draws below stay inside these ranges and needn't reach their ends.
Inputs may be any that keep to these rules, and one draw needn't show every extreme that they name: `tile_index`: the slots of one partition name distinct triples (a, c, b) with a and b below 2 and c below 16. Slots at or beyond tile_count[P] are padding; one partition uses all 8 slots. partner[P, m] has P's domain index, and its group index is P's group index XOR a nonzero code that depends on m only; the 4 codes are distinct and one of them is 8. pair_edges[partner[P, m], m, e] is pair_edges[P, m, e] with its two entries swapped.
All inputs are finite; a program needn't handle non-finite values. No bound on the sum of `tile_mask` on one device may be relied on, other than what follows from the above.
Results may differ from the reference program's by a relative error of at most 0.0075.
The reference program's roundings to bfloat16 on the way count: a program that leaves them out, or rounds other values in their place, can miss the bound.
Values may be sent and summed in bfloat16 or wider, within the bound.
No kernel may reach another device: no remote copies, remote signals or barrier semaphores. Data moves between devices by JAX's collectives and lax.ppermute only.
A program may use at most 128 MiB of HBM per device.

```python
import math
import jax
import jax.numpy as jnp
from jax import lax

D = 512
HEADS = 8
HEAD_DIM = 64
NODE_DEV = 256
TILE = 128
MATCH = 4
GROUPS = 16
DOMAINS = 16
PARTS_SIZE = 256
NODES = 65536
ROW_BLOCKS = 2
TILE_SLOTS = 8
EXPANDER = 64


def draw_key(key, part):
    noise = jax.random.normal(jax.random.fold_in(key, 31), (NODES, D), jnp.float32)
    values = jnp.clip(noise, -6.0, 6.0)
    return values.astype(jnp.bfloat16)


def draw_query(key, part):
    noise = jax.random.normal(jax.random.fold_in(key, 37), (NODES, D), jnp.float32)
    values = jnp.clip(noise, -6.0, 6.0)
    return values.astype(jnp.bfloat16)


def draw_tile_index(key, part):
    combos = DOMAINS * ROW_BLOCKS * ROW_BLOCKS

    def one_part(part_id):
        ordering = jax.random.permutation(jax.random.fold_in(jax.random.fold_in(key, 17), part_id), combos)[:TILE_SLOTS]
        return jnp.stack([ordering // (DOMAINS * ROW_BLOCKS), ordering // ROW_BLOCKS % DOMAINS, ordering % ROW_BLOCKS], axis=1)
    return jax.vmap(one_part)(jnp.arange(PARTS_SIZE, dtype=jnp.int32)).astype(jnp.int32)


def draw_tile_count(key, part):
    base_count = 1 + jax.random.randint(jax.random.fold_in(key, 19), (PARTS_SIZE,), 0, TILE_SLOTS // 2)
    heaviest = jax.random.randint(jax.random.fold_in(key, 23), (), 0, PARTS_SIZE)
    return jnp.where(jnp.arange(PARTS_SIZE, dtype=jnp.int32) == heaviest, TILE_SLOTS, base_count).astype(jnp.int32)


def matching_codes(key):
    half_code = GROUPS // 2
    others = jax.random.permutation(jax.random.fold_in(key, 11), GROUPS - 2)[:MATCH - 1] + 1
    others = jnp.where(others >= half_code, others + 1, others)
    codes = jnp.concatenate([jnp.full((1,), half_code, jnp.int32), others.astype(jnp.int32)])
    return jax.random.permutation(jax.random.fold_in(key, 7), codes).astype(jnp.int32)


def draw_partner(key, part):
    match_codes = matching_codes(key)
    part_ids = jnp.arange(PARTS_SIZE, dtype=jnp.int32)
    group_ids = part_ids // DOMAINS
    domain_ids = part_ids % DOMAINS
    return (jnp.bitwise_xor(group_ids[:, None], match_codes[None, :]) * DOMAINS + domain_ids[:, None]).astype(jnp.int32)


def draw_pair_edges(key, part):
    partners = draw_partner(key, part)
    part_ids = jnp.arange(PARTS_SIZE, dtype=jnp.int32)
    lower = jnp.minimum(part_ids[:, None], partners)
    identity = jnp.arange(MATCH, dtype=jnp.int32)[None, :] * PARTS_SIZE + lower

    def one_pair(pair_id):
        return jax.random.randint(jax.random.fold_in(jax.random.fold_in(key, 13), pair_id), (EXPANDER, 2), 0, NODE_DEV)
    pairs = jax.vmap(jax.vmap(one_pair))(identity)
    is_lower = (part_ids[:, None] < partners)[:, :, None, None]
    return jnp.where(is_lower, pairs, pairs[..., ::-1]).astype(jnp.int32)


def plant(array, rng, low, high):
    spot = [jax.random.randint(jax.random.fold_in(rng, axis), (), 0, length) for axis, length in enumerate(array.shape)]
    main_axis = array.shape.index(max(array.shape))
    beside = spot[:main_axis] + [(spot[main_axis] + 1) % array.shape[main_axis]] + spot[main_axis + 1:]
    return array.at[tuple(spot)].set(low).at[tuple(beside)].set(high)


def shard_levels(stream_key, dims, pieces, smallest, largest):
    gain = 1.0
    for axis_at, parts in pieces:
        heights = jax.random.uniform(jax.random.fold_in(jax.random.fold_in(stream_key, 6), axis_at), (parts,), jnp.float32, smallest / len(pieces), largest / len(pieces))
        gain = gain * jnp.repeat(jnp.exp(heights), dims[axis_at] // parts).reshape((-1,) + (1,) * (len(dims) - 1 - axis_at))
    return gain


def centred(key, shape, spread, limit, shards=(), held_as=jnp.bfloat16):
    values = spread * jax.random.normal(key, shape, jnp.float32)
    if shards:
        values = values * shard_levels(key, shape, shards, -0.22, 0.18)
    return jnp.clip(values, -limit, limit).astype(held_as)


def setup_inputs(seed: int = 0) -> dict:
    key_list = jax.random.split(jax.random.key(seed), 10)
    query = draw_query(jax.random.fold_in(key_list[9], 71), 0)
    key = draw_key(jax.random.fold_in(key_list[9], 71), 0)
    value = centred(key_list[2], (NODES, D), 1.0, 6.0, ((0, 256),))
    cotangent = centred(key_list[3], (NODES, D), 1.0, 6.0, ((0, 256),))
    tile_index = draw_tile_index(jax.random.fold_in(key_list[9], 71), 0)
    tile_mask = plant((jax.random.randint(key_list[5], (PARTS_SIZE, TILE_SLOTS, TILE, TILE), 0, TILE // 2) < 1).astype(jnp.int32), jax.random.fold_in(key_list[5], 1), 0, 1)
    tile_count = draw_tile_count(jax.random.fold_in(key_list[9], 71), 0)
    partner = draw_partner(jax.random.fold_in(key_list[9], 71), 0)
    pair_edges = draw_pair_edges(jax.random.fold_in(key_list[9], 71), 0)
    return dict(query=query, key=key, value=value, cotangent=cotangent, tile_index=tile_index, tile_mask=tile_mask, tile_count=tile_count, partner=partner, pair_edges=pair_edges)


def rounded(values):
    return lax.optimization_barrier(values.astype(jnp.bfloat16)).astype(jnp.float32)

def split_heads(values):
    return values.astype(jnp.float32).reshape(values.shape[0], HEADS, HEAD_DIM)

def reference(query, key, value, cotangent, tile_index, tile_mask, tile_count, partner, pair_edges):
    score_scale = 1.0 / math.sqrt(HEAD_DIM)
    group_size = DOMAINS * NODE_DEV
    lane_ids = jnp.arange(TILE, dtype=jnp.int32)
    slot_ids = jnp.arange(TILE_SLOTS, dtype=jnp.int32)

    def part_step(carried, part_id):
        key_acc, value_acc = carried
        own_start = (part_id * NODE_DEV).astype(jnp.int32)
        group_start = (part_id // DOMAINS * group_size).astype(jnp.int32)
        own_query = split_heads(lax.dynamic_slice_in_dim(query, own_start, NODE_DEV, 0))
        own_key = split_heads(lax.dynamic_slice_in_dim(key, own_start, NODE_DEV, 0))
        own_value = split_heads(lax.dynamic_slice_in_dim(value, own_start, NODE_DEV, 0))
        own_grad = split_heads(lax.dynamic_slice_in_dim(cotangent, own_start, NODE_DEV, 0))
        group_key = split_heads(lax.dynamic_slice_in_dim(key, group_start, group_size, 0))
        group_value = split_heads(lax.dynamic_slice_in_dim(value, group_start, group_size, 0))
        entries = tile_index[part_id]
        live_mask = (tile_mask[part_id] != 0) & (slot_ids < tile_count[part_id])[:, None, None]
        row_ids = entries[:, 0:1] * TILE + lane_ids[None, :]
        col_ids = entries[:, 1:2] * NODE_DEV + entries[:, 2:3] * TILE + lane_ids[None, :]
        flat_rows = row_ids.reshape(-1)
        flat_cols = col_ids.reshape(-1)
        tile_query = own_query[row_ids]
        tile_grad = own_grad[row_ids]
        tile_key = group_key[col_ids]
        tile_value = group_value[col_ids]
        tile_score = jnp.einsum('sihe,sjhe->shij', tile_query, tile_key) * score_scale
        tile_score = jnp.where(live_mask[:, None], tile_score, -jnp.inf)
        self_score = lax.optimization_barrier(jnp.sum(own_query * own_key, axis=2)) * score_scale
        partner_ids = partner[part_id]
        near_rows = pair_edges[part_id, :, :, 0].reshape(-1)
        far_rows = (partner_ids[:, None] * NODE_DEV + pair_edges[part_id, :, :, 1]).reshape(-1)
        far_key = split_heads(key[far_rows])
        far_value = split_heads(value[far_rows])
        near_query = own_query[near_rows]
        near_grad = own_grad[near_rows]
        pair_score = lax.optimization_barrier(jnp.sum(near_query * far_key, axis=2)) * score_scale

        def per_row(values):
            return values.transpose(0, 2, 1).reshape(-1, HEADS)

        def tile_rows(values):
            return values[row_ids].transpose(0, 2, 1)[:, :, :, None]
        row_top = self_score.at[flat_rows].max(per_row(lax.optimization_barrier(jnp.max(tile_score, axis=3))))
        row_top = row_top.at[near_rows].max(pair_score)
        tile_exp = jnp.exp(tile_score - tile_rows(row_top))
        self_exp = jnp.exp(self_score - row_top)
        pair_exp = jnp.exp(pair_score - row_top[near_rows])
        row_total = self_exp.at[flat_rows].add(per_row(lax.optimization_barrier(jnp.sum(tile_exp, axis=3))))
        row_total = row_total.at[near_rows].add(pair_exp)
        tile_weight = tile_exp / tile_rows(row_total)
        self_weight = self_exp / row_total
        pair_weight = pair_exp / row_total[near_rows]
        tile_wb = rounded(tile_weight)
        self_wb = rounded(self_weight)
        pair_wb = rounded(pair_weight)
        outcome = self_wb[:, :, None] * own_value
        outcome = outcome.at[flat_rows].add(jnp.einsum('shij,sjhe->sihe', tile_wb, tile_value).reshape(-1, HEADS, HEAD_DIM))
        outcome = outcome.at[near_rows].add(pair_wb[:, :, None] * far_value)
        row_delta = lax.optimization_barrier(jnp.sum(own_grad * outcome, axis=2))
        tile_drops = jnp.einsum('sihe,sjhe->shij', tile_grad, tile_value)
        tile_ds = rounded(tile_weight * (tile_drops - tile_rows(row_delta)))
        self_ds = rounded(self_weight * (lax.optimization_barrier(jnp.sum(own_grad * own_value, axis=2)) - row_delta))
        pair_ds = rounded(pair_weight * (lax.optimization_barrier(jnp.sum(near_grad * far_value, axis=2)) - row_delta[near_rows]))
        query_total = self_ds[:, :, None] * own_key
        query_total = query_total.at[flat_rows].add(jnp.einsum('shij,sjhe->sihe', tile_ds, tile_key).reshape(-1, HEADS, HEAD_DIM))
        query_total = query_total.at[near_rows].add(pair_ds[:, :, None] * far_key)
        empty_rows = jnp.zeros((group_size, HEADS, HEAD_DIM), jnp.float32)
        group_dk = empty_rows.at[flat_cols].add(jnp.einsum('shij,sihe->sjhe', tile_ds, tile_query).reshape(-1, HEADS, HEAD_DIM))
        group_dv = empty_rows.at[flat_cols].add(jnp.einsum('shij,sihe->sjhe', tile_wb, tile_grad).reshape(-1, HEADS, HEAD_DIM))
        group_dk = rounded(score_scale * group_dk).reshape(group_size, D)
        group_dv = rounded(group_dv).reshape(group_size, D)
        key_acc = lax.dynamic_update_slice_in_dim(key_acc, lax.dynamic_slice_in_dim(key_acc, group_start, group_size, 0) + group_dk, group_start, 0)
        value_acc = lax.dynamic_update_slice_in_dim(value_acc, lax.dynamic_slice_in_dim(value_acc, group_start, group_size, 0) + group_dv, group_start, 0)
        self_dk = (score_scale * self_ds[:, :, None] * own_query).reshape(NODE_DEV, D)
        self_dv = (self_wb[:, :, None] * own_grad).reshape(NODE_DEV, D)
        key_acc = lax.dynamic_update_slice_in_dim(key_acc, lax.dynamic_slice_in_dim(key_acc, own_start, NODE_DEV, 0) + self_dk, own_start, 0)
        value_acc = lax.dynamic_update_slice_in_dim(value_acc, lax.dynamic_slice_in_dim(value_acc, own_start, NODE_DEV, 0) + self_dv, own_start, 0)
        key_acc = key_acc.at[far_rows].add(rounded(score_scale * pair_ds[:, :, None] * near_query).reshape(-1, D))
        value_acc = value_acc.at[far_rows].add(rounded(pair_wb[:, :, None] * near_grad).reshape(-1, D))
        results = (outcome.reshape(NODE_DEV, D).astype(jnp.bfloat16), (score_scale * query_total).reshape(NODE_DEV, D).astype(jnp.bfloat16))
        return ((key_acc, value_acc), results)
    start_acc = jnp.zeros((NODES, D), jnp.float32)
    (key_acc, value_acc), (outcome, query_grad) = lax.scan(part_step, (start_acc, start_acc), jnp.arange(PARTS_SIZE, dtype=jnp.int32))
    return (outcome.reshape(NODES, D), query_grad.reshape(NODES, D), key_acc.astype(jnp.bfloat16), value_acc.astype(jnp.bfloat16))
```

```python
import jax
import jax.numpy as jnp
from jax import lax
from jax.experimental import pallas as pl
from jax.experimental.pallas import tpu as pltpu
from jax.sharding import PartitionSpec as P

F32 = jnp.float32
BF16 = jnp.bfloat16
LOW = -1e30
SCALE = 0.125
ROWS = 256
WIDTH = 512
TILE = 128
PAIRS = 4
SLOTS = 8
MATCH = 4
EDGES = 64
DOMAINS = 16
GROUPS = 16
VMEM_LIMIT = 48 * 2**20


def dot(a, b, da=1, db=0):
    return lax.dot_general(a, b, (((da,), (db,)), ((), ())), preferred_element_type=F32)


def one_hot(near_col):
    e, r = near_col.shape[0], ROWS
    return lax.broadcasted_iota(jnp.int32, (e, r), 1) == near_col


def one_hot_t(near_row):
    e, r = near_row.shape[1], ROWS
    return lax.broadcasted_iota(jnp.int32, (r, e), 0) == near_row


def as_bf16(flags):
    return jnp.where(flags, 1.0, 0.0).astype(BF16)


def head_rows():
    s = lax.broadcasted_iota(jnp.int32, (16, WIDTH), 0)
    c = lax.broadcasted_iota(jnp.int32, (16, WIDTH), 1)
    return as_bf16((c >> 6) == 2 * (s & 7) + (s >> 3))


def halves(x):
    hi = x.astype(BF16)
    return hi, (x - hi.astype(F32)).astype(BF16)


def thirds(x):
    hi = x.astype(BF16)
    rest = x - hi.astype(F32)
    mid = rest.astype(BF16)
    return jnp.concatenate([hi, mid, (rest - mid.astype(F32)).astype(BF16)], axis=0)


def select_sum(x, matrix):
    y = dot(thirds(x), matrix)
    return y[0:16] + y[16:32] + y[32:48]


def to_blocks(x, a):
    lanes = slice(a * TILE, (a + 1) * TILE)
    return jnp.concatenate([x[0:8, lanes], x[8:16, lanes]], axis=1)


def from_blocks(x0, x1):
    even = jnp.concatenate([x0[:, :TILE], x1[:, :TILE]], axis=1)
    odd = jnp.concatenate([x0[:, TILE:], x1[:, TILE:]], axis=1)
    return jnp.concatenate([even, odd], axis=0)


def pick_kernel(near_ref, k_ref, v_ref, *outs):
    hot = as_bf16(one_hot(near_ref[...]))
    rows_k = dot(hot, k_ref[...]).astype(BF16)
    rows_v = dot(hot, v_ref[...]).astype(BF16)
    for m, out in enumerate(outs):
        part = slice(m * EDGES, (m + 1) * EDGES)
        out[:, :WIDTH] = rows_k[part]
        out[:, WIDTH:] = rows_v[part]


def prep_kernel(nc_ref, nr_ref, q_ref, k_ref, v_ref, g_ref, mask_ref, f0, f1, f2, f3,
                qs_ref, gs_ref, qt_ref, gt_ref, bias_ref, nq_ref, ng_ref, st_ref, top_ref):
    hot = one_hot(nc_ref[...])
    hot_b = as_bf16(hot)
    hot_t = as_bf16(one_hot_t(nr_ref[...]))
    heads = head_rows()
    low_rows = lax.broadcasted_iota(jnp.int32, (TILE, TILE), 0) < 64
    low_lanes = lax.broadcasted_iota(jnp.int32, (TILE, TILE), 1) < 64

    for t in range(SLOTS):
        bias_ref[t] = jnp.where(mask_ref[t].astype(F32).T != 0, 0.0, LOW)

    qs = q_ref[...].astype(F32) * SCALE
    g = g_ref[...].astype(F32)
    for source, by_col, by_row in ((qs, qs_ref, qt_ref), (g, gs_ref, gt_ref)):
        for a in range(2):
            for p in range(PAIRS):
                x = source[a * TILE:(a + 1) * TILE, p * TILE:(p + 1) * TILE]
                xt = x.T
                by_col[a, p] = jnp.concatenate(
                    [jnp.where(low_rows, xt, 0.0), jnp.where(low_rows, 0.0, xt)], axis=1).astype(BF16)
                by_row[a, p] = jnp.concatenate(
                    [jnp.where(low_lanes, x, 0.0), jnp.where(low_lanes, 0.0, x)], axis=0).astype(BF16)

    far = jnp.concatenate([f0[...], f1[...], f2[...], f3[...]], axis=0).astype(F32)
    far_k, far_v = far[:, :WIDTH], far[:, WIDTH:]
    near_q = dot(hot_b, qs.astype(BF16))
    near_g = dot(hot_b, g_ref[...])
    nq_ref[...] = near_q.astype(BF16)
    ng_ref[...] = near_g.astype(BF16)

    def head_sum(x):
        hi, lo = halves(x)
        return dot(heads, hi, 1, 1) + dot(heads, lo, 1, 1)

    self_score = head_sum(qs * k_ref[...].astype(F32))
    self_drop = head_sum(g * v_ref[...].astype(F32))
    product = near_q * far_k
    hi, lo = halves(product)
    pair_score = dot(heads, hi, 1, 1) + dot(heads, lo, 1, 1)
    by_edge = dot(hi, heads, 1, 1) + dot(lo, heads, 1, 1)
    pair_drop = head_sum(near_g * far_v)
    top_ref[...] = self_score
    for s in (0, 1, 2, 3, 8, 9, 10, 11):
        best = jnp.max(jnp.where(hot, by_edge[:, s:s + 1], LOW), axis=0, keepdims=True)
        top_ref[s:s + 1, :] = jnp.maximum(top_ref[s:s + 1, :], best)
    top = top_ref[...]
    self_exp = jnp.exp(self_score - top)
    pair_exp = jnp.exp(pair_score - select_sum(top, hot_t))
    st_ref[0:16] = top
    st_ref[16:32] = self_exp + select_sum(pair_exp, hot_b)
    st_ref[32:48] = self_exp
    st_ref[48:64] = pair_exp
    st_ref[64:80] = self_drop
    st_ref[80:96] = pair_drop


def tile_kernel(info, nc_ref, nr_ref, kv_ref, zero_ref, qs_ref, gs_ref, qt_ref, gt_ref, bias_ref, st_ref,
                terms_ref, out_ref, gq_ref, wd_ref,
                kb, vb, eb, mt, lt, ft, top2, sum2, del2, dk, dv, sk, sv, in_sem, out_sem):
    count = info[SLOTS, 0]

    def load(t, part):
        start = pl.multiple_of(info[t, 1] * (2 * ROWS) + part * ROWS + info[t, 2] * TILE, TILE)
        buf = kb if part == 0 else vb
        return pltpu.make_async_copy(kv_ref.at[pl.ds(start, TILE)], buf.at[t], in_sem.at[part, t])

    @pl.loop(0, count)
    def _(t):
        load(t, 0).start()
        load(t, 1).start()

    top1, sum1 = st_ref[0:16], st_ref[16:32]
    self_exp, pair_exp = st_ref[32:48], st_ref[48:64]
    self_drop, pair_drop = st_ref[64:80], st_ref[80:96]
    hot_b = as_bf16(one_hot(nc_ref[...]))
    hot_t = as_bf16(one_hot_t(nr_ref[...]))
    for a in range(2):
        top2[a] = to_blocks(top1, a)

    @pl.loop(0, count)
    def _(t):
        a = info[t, 0]
        load(t, 0).wait()
        bias = bias_ref[t]
        bias = jnp.concatenate([bias, bias], axis=1)
        for p in range(PAIRS):
            s = dot(kb[t, :, p * TILE:(p + 1) * TILE], qs_ref[a, p]) + bias
            m = jnp.max(s, axis=0, keepdims=True)
            e = jnp.exp(s - m)
            eb[t, p] = e
            mt[t, p:p + 1] = m
            lt[t, p:p + 1] = jnp.sum(e, axis=0, keepdims=True)
        top2[a, 0:PAIRS] = jnp.maximum(top2[a, 0:PAIRS], mt[t, 0:PAIRS])

    for a in range(2):
        sum2[a] = to_blocks(sum1, a) * jnp.exp(to_blocks(top1, a) - top2[a])

    @pl.loop(0, count)
    def _(t):
        a = info[t, 0]
        shrink = jnp.exp(mt[t, 0:PAIRS] - top2[a, 0:PAIRS])
        ft[t, 0:PAIRS] = shrink
        sum2[a, 0:PAIRS] += lt[t, 0:PAIRS] * shrink

    @pl.loop(0, count)
    def _(t):
        a = info[t, 0]
        ft[t, 0:PAIRS] = ft[t, 0:PAIRS] / sum2[a, 0:PAIRS]

    factor = jnp.exp(top1 - from_blocks(top2[0], top2[1])) / from_blocks(sum2[0], sum2[1])
    self_w = self_exp * factor
    pair_w = pair_exp * select_sum(factor, hot_t)
    self_wb = self_w.astype(BF16).astype(F32)
    pair_wb = pair_w.astype(BF16).astype(F32)
    wd_ref[0:16] = self_wb
    wd_ref[16:32] = pair_wb
    delta = self_wb * self_drop + select_sum(pair_wb * pair_drop, hot_b)

    out_ref[...] = jnp.zeros_like(out_ref)
    gq_ref[...] = jnp.zeros_like(gq_ref)

    def add_term(acc, t, p, term):
        f = info[t, 3]
        cols = slice(p * TILE, (p + 1) * TILE)
        acc[f, :, cols] = jnp.where(f == t, 0.0, acc[f, :, cols]) + term

    @pl.loop(0, count)
    def _(t):
        a = info[t, 0]
        load(t, 1).wait()
        for p in range(PAIRS):
            wb = (eb[t, p] * ft[t, p:p + 1]).astype(BF16)
            out_ref[a, p] += dot(vb[t, :, p * TILE:(p + 1) * TILE], wb, 0, 0)
            add_term(dv, t, p, dot(wb, gt_ref[a, p]))

    for a in range(2):
        base = to_blocks(delta, a)
        for p in range(PAIRS):
            del2[a, p:p + 1] = base[p:p + 1] + jnp.sum(
                gs_ref[a, p].astype(F32) * out_ref[a, p], axis=0, keepdims=True)
        del2[a, PAIRS:8] = jnp.zeros((8 - PAIRS, 2 * TILE), F32)
    delta = from_blocks(del2[0], del2[1])
    wd_ref[32:48] = self_w * (self_drop - delta)
    wd_ref[48:64] = pair_w * (pair_drop - select_sum(delta, hot_t))

    @pl.loop(0, count)
    def _(t):
        a = info[t, 0]
        for p in range(PAIRS):
            cols = slice(p * TILE, (p + 1) * TILE)
            drop = dot(vb[t, :, cols], gs_ref[a, p])
            ds = (eb[t, p] * ft[t, p:p + 1] * (drop - del2[a, p:p + 1])).astype(BF16)
            gq_ref[a, p] += dot(kb[t, :, cols], ds, 0, 0)
            add_term(dk, t, p, dot(ds, qt_ref[a, p]))

    def store(t, part):
        buf = sk if part == 0 else sv
        rows = pl.ds(pl.multiple_of(part * ROWS + info[t, 2] * TILE, TILE), TILE)
        return pltpu.make_async_copy(buf.at[t], terms_ref.at[info[t, 1], rows], out_sem.at[part, t])

    @pl.loop(0, count)
    def _(t):
        @pl.when(info[t, 3] == t)
        def _():
            sk[t] = dk[t].astype(BF16)
            sv[t] = dv[t].astype(BF16)
            store(t, 0).start()
            store(t, 1).start()

    @pl.loop(0, count)
    def _(t):
        @pl.when(info[t, 3] == t)
        def _():
            store(t, 0).wait()
            store(t, 1).wait()


def rest_kernel(nr_ref, q_ref, k_ref, v_ref, g_ref, f0, f1, f2, f3, nq_ref, ng_ref, acc_ref, gacc_ref, wd_ref,
                out_ref, gq_ref, own_ref, b0, b1, b2, b3):
    hot_t = as_bf16(one_hot_t(nr_ref[...]))
    heads = head_rows()

    def expand(x):
        return dot(x.astype(BF16), heads, 0, 0)

    far = jnp.concatenate([f0[...], f1[...], f2[...], f3[...]], axis=0).astype(F32)
    self_wb, pair_wb = expand(wd_ref[0:16]), expand(wd_ref[16:32])
    self_ds, pair_ds = expand(wd_ref[32:48]), expand(wd_ref[48:64])
    back_k = (pair_ds * nq_ref[...].astype(F32)).astype(BF16)
    back_v = (pair_wb * ng_ref[...].astype(F32)).astype(BF16)
    for m, out in enumerate((b0, b1, b2, b3)):
        part = slice(m * EDGES, (m + 1) * EDGES)
        out[:, :WIDTH] = back_k[part]
        out[:, WIDTH:] = back_v[part]
    own_ref[0:ROWS] = self_ds * (q_ref[...].astype(F32) * SCALE)
    own_ref[ROWS:2 * ROWS] = self_wb * g_ref[...].astype(F32)

    def finish(own, pair, acc, scale, out):
        hi, lo = halves(pair)
        total = own + dot(hot_t, hi) + dot(hot_t, lo)
        for a in range(2):
            for p in range(PAIRS):
                x = acc[a, p]
                x = jnp.concatenate([x[0:64, :TILE], x[64:TILE, TILE:]], axis=0).T
                rows, cols = slice(a * TILE, (a + 1) * TILE), slice(p * TILE, (p + 1) * TILE)
                out[rows, cols] = ((total[rows, cols] + x) * scale).astype(BF16)

    finish(self_wb * v_ref[...].astype(F32), pair_wb * far[:, WIDTH:], acc_ref, 1.0, out_ref)
    finish(self_ds * k_ref[...].astype(F32), pair_ds * far[:, :WIDTH], gacc_ref, SCALE, gq_ref)


def last_kernel(nr_ref, sum_ref, own_ref, b0, b1, b2, b3, gk_ref, gv_ref):
    hot_t = as_bf16(one_hot_t(nr_ref[...]))
    back = jnp.concatenate([b0[...], b1[...], b2[...], b3[...]], axis=0)
    gk_ref[...] = (sum_ref[0:ROWS].astype(F32) + own_ref[0:ROWS] + dot(hot_t, back[:, :WIDTH])).astype(BF16)
    gv_ref[...] = (sum_ref[ROWS:].astype(F32) + own_ref[ROWS:] + dot(hot_t, back[:, WIDTH:])).astype(BF16)


def call(kernel, outs, ins, args, cost=(1e8, 4e6), scratch=(), out_specs=None, **more):
    vmem = pl.BlockSpec(memory_space=pltpu.VMEM)
    return pl.pallas_call(
        kernel,
        out_shape=[jax.ShapeDtypeStruct(s, d) for s, d in outs],
        in_specs=[vmem] * len(args) if ins is None else ins,
        out_specs=[vmem] * len(outs) if out_specs is None else out_specs,
        scratch_shapes=list(scratch),
        compiler_params=pltpu.CompilerParams(vmem_limit_bytes=VMEM_LIMIT),
        cost_estimate=pl.CostEstimate(flops=int(cost[0]), bytes_accessed=int(cost[1]), transcendentals=0),
        **more,
    )(*args)


def exchange(blocks, codes):
    def route(code):
        pairs = [(i, i ^ code) for i in range(GROUPS)]
        return lambda block: lax.ppermute(block, "grp", pairs)

    routes = [route(code) for code in range(1, GROUPS)]
    return [lax.switch(codes[m] - 1, routes, block) for m, block in enumerate(blocks)]


def body(query, key, value, cotangent, tile_index, tile_mask, tile_count, partner, pair_edges):
    vmem = pl.BlockSpec(memory_space=pltpu.VMEM)
    anywhere = pl.BlockSpec(memory_space=pl.ANY)
    smem = pl.BlockSpec(memory_space=pltpu.SMEM)

    near = pair_edges[0, :, :, 0].reshape(-1)
    near_col, near_row = near.reshape(-1, 1), near.reshape(1, -1)
    codes = jnp.bitwise_xor(partner[0] // DOMAINS, lax.axis_index("grp"))
    entries = tile_index[0]
    place = entries[:, 1] * 2 + entries[:, 2]
    slot = jnp.arange(SLOTS, dtype=jnp.int32)
    first = jnp.min(jnp.where(place[:, None] == place[None, :], slot[None, :], SLOTS), axis=1)
    info = jnp.concatenate([entries, first[:, None].astype(jnp.int32)], axis=1)
    info = jnp.concatenate([info, jnp.broadcast_to(tile_count[:, None], (1, 4))], axis=0)

    group_kv = lax.all_gather(jnp.concatenate([key, value], axis=0), "dom", axis=0, tiled=True)

    block = ((EDGES, 2 * WIDTH), BF16)
    sent = call(pick_kernel, [block] * MATCH, None, (near_col, key, value))
    far = exchange(sent, codes)

    node = ((ROWS, WIDTH), BF16)
    by_col = ((2, PAIRS, TILE, 2 * TILE), BF16)
    by_row = ((2, PAIRS, 2 * TILE, TILE), BF16)
    qs, gs, qt, gt, bias, near_q, near_g, stats = call(
        prep_kernel,
        [by_col, by_col, by_row, by_row, ((SLOTS, TILE, TILE), F32), node, node, ((96, ROWS), F32)],
        None,
        (near_col, near_row, query, key, value, cotangent, tile_mask[0], *far),
        scratch=[pltpu.VMEM((16, ROWS), F32)],
    )

    zeros = jnp.zeros((DOMAINS, 2 * ROWS, WIDTH), BF16)
    acc = ((2, PAIRS, TILE, 2 * TILE), F32)
    row_stat = pltpu.VMEM((SLOTS, 8, 2 * TILE), F32)
    block_stat = pltpu.VMEM((2, 8, 2 * TILE), F32)
    tiles_b = pltpu.VMEM((SLOTS, TILE, WIDTH), BF16)
    tiles_f = pltpu.VMEM((SLOTS, TILE, WIDTH), F32)
    terms, out_acc, gq_acc, grads = call(
        tile_kernel,
        [((DOMAINS, 2 * ROWS, WIDTH), BF16), acc, acc, ((64, ROWS), F32)],
        [smem, vmem, vmem, anywhere, anywhere] + [vmem] * 6,
        (info, near_col, near_row, group_kv, zeros, qs, gs, qt, gt, bias, stats),
        cost=(1e9, 2e7),
        scratch=[
            tiles_b, tiles_b, pltpu.VMEM((SLOTS, PAIRS, TILE, 2 * TILE), F32),
            row_stat, row_stat, row_stat, block_stat, block_stat, block_stat,
            tiles_f, tiles_f, tiles_b, tiles_b,
            pltpu.SemaphoreType.DMA((2, SLOTS)), pltpu.SemaphoreType.DMA((2, SLOTS)),
        ],
        out_specs=[anywhere, vmem, vmem, vmem],
        input_output_aliases={4: 0},
    )

    sums = lax.psum_scatter(terms.reshape(DOMAINS * 2 * ROWS, WIDTH), "dom", scatter_dimension=0, tiled=True)

    attended, grad_query, own, *back = call(
        rest_kernel,
        [node, node, ((2 * ROWS, WIDTH), F32)] + [block] * MATCH,
        None,
        (near_row, query, key, value, cotangent, *far, near_q, near_g, out_acc, gq_acc, grads),
    )
    back = exchange(back, codes)
    grad_key, grad_value = call(last_kernel, [node, node], None, (near_row, sums, own, *back))
    return attended, grad_query, grad_key, grad_value


def solution(mesh):
    rows = P(("grp", "dom"), None)
    return jax.shard_map(
        body,
        mesh=mesh,
        in_specs=(
            rows, rows, rows, rows,
            P(("grp", "dom"), None, None),
            P(("grp", "dom"), None, None, None),
            P(("grp", "dom")),
            rows,
            P(("grp", "dom"), None, None, None),
        ),
        out_specs=(rows, rows, rows, rows),
        check_vma=False,
    )
```

```python
import jax
import jax.numpy as jnp
from jax import lax
from jax.experimental import pallas as pl
from jax.experimental.pallas import tpu as pltpu
from jax.sharding import PartitionSpec as P

F32 = jnp.float32
BF16 = jnp.bfloat16
LOW = -1e30
SCALE = 0.125
ROWS = 256
WIDTH = 512
TILE = 128
PAIRS = 4
SLOTS = 8
MATCH = 4
EDGES = 64
DOMAINS = 16
GROUPS = 16
VMEM_LIMIT = 34 * 2**20
ROUTE = ((4, 12, 1, 3), (12, 4, 3, 1), (1, 3, 4, 12), (3, 1, 12, 4))


def dot(a, b, da=1, db=0):
    return lax.dot_general(a, b, (((da,), (db,)), ((), ())), preferred_element_type=F32)


def one_hot(near_col):
    e, r = near_col.shape[0], ROWS
    return lax.broadcasted_iota(jnp.int32, (e, r), 1) == near_col


def one_hot_t(near_row):
    e, r = near_row.shape[1], ROWS
    return lax.broadcasted_iota(jnp.int32, (r, e), 0) == near_row


def as_bf16(flags):
    return jnp.where(flags, 1.0, 0.0).astype(BF16)


def head_rows():
    s = lax.broadcasted_iota(jnp.int32, (16, WIDTH), 0)
    c = lax.broadcasted_iota(jnp.int32, (16, WIDTH), 1)
    return as_bf16((c >> 6) == 2 * (s & 7) + (s >> 3))


def halves(x):
    hi = x.astype(BF16)
    return hi, (x - hi.astype(F32)).astype(BF16)


def thirds(x):
    hi = x.astype(BF16)
    rest = x - hi.astype(F32)
    mid = rest.astype(BF16)
    return jnp.concatenate([hi, mid, (rest - mid.astype(F32)).astype(BF16)], axis=0)


def select_sum(x, matrix):
    y = dot(thirds(x), matrix)
    return y[0:16] + y[16:32] + y[32:48]


def to_blocks(x, a):
    lanes = slice(a * TILE, (a + 1) * TILE)
    return jnp.concatenate([x[0:8, lanes], x[8:16, lanes]], axis=1)


def from_blocks(x0, x1):
    even = jnp.concatenate([x0[:, :TILE], x1[:, :TILE]], axis=1)
    odd = jnp.concatenate([x0[:, TILE:], x1[:, TILE:]], axis=1)
    return jnp.concatenate([even, odd], axis=0)


def pick_kernel(near_ref, k_ref, v_ref, *outs):
    hot = as_bf16(one_hot(near_ref[...]))
    rows_k = dot(hot, k_ref[...]).astype(BF16)
    rows_v = dot(hot, v_ref[...]).astype(BF16)
    for m, out in enumerate(outs):
        part = slice(m * EDGES, (m + 1) * EDGES)
        out[:, :WIDTH] = rows_k[part]
        out[:, WIDTH:] = rows_v[part]


def layout_kernel(q_ref, g_ref, mask_ref, qs_ref, gs_ref, qt_ref, gt_ref, bias_ref):
    low_rows = lax.broadcasted_iota(jnp.int32, (TILE, TILE), 0) < 64
    low_lanes = lax.broadcasted_iota(jnp.int32, (TILE, TILE), 1) < 64

    for t in range(SLOTS):
        bias_ref[t] = jnp.where(mask_ref[t].astype(F32).T != 0, 0.0, LOW)

    qs = q_ref[...].astype(F32) * SCALE
    g = g_ref[...].astype(F32)
    for source, by_col, by_row in ((qs, qs_ref, qt_ref), (g, gs_ref, gt_ref)):
        for a in range(2):
            for p in range(PAIRS):
                x = source[a * TILE:(a + 1) * TILE, p * TILE:(p + 1) * TILE]
                xt = x.T
                by_col[a, p] = jnp.concatenate(
                    [jnp.where(low_rows, xt, 0.0), jnp.where(low_rows, 0.0, xt)], axis=1).astype(BF16)
                by_row[a, p] = jnp.concatenate(
                    [jnp.where(low_lanes, x, 0.0), jnp.where(low_lanes, 0.0, x)], axis=0).astype(BF16)


def pair_kernel(nc_ref, nr_ref, q_ref, k_ref, v_ref, g_ref, f0, f1, f2, f3, nq_ref, ng_ref, st_ref, top_ref):
    hot = one_hot(nc_ref[...])
    hot_b = as_bf16(hot)
    hot_t = as_bf16(one_hot_t(nr_ref[...]))
    heads = head_rows()
    qs = q_ref[...].astype(F32) * SCALE
    g = g_ref[...].astype(F32)

    far = jnp.concatenate([f0[...], f1[...], f2[...], f3[...]], axis=0).astype(F32)
    far_k, far_v = far[:, :WIDTH], far[:, WIDTH:]
    near_q = dot(hot_b, qs.astype(BF16))
    near_g = dot(hot_b, g_ref[...])
    nq_ref[...] = near_q.astype(BF16)
    ng_ref[...] = near_g.astype(BF16)

    def head_sum(x):
        hi, lo = halves(x)
        return dot(heads, hi, 1, 1) + dot(heads, lo, 1, 1)

    self_score = head_sum(qs * k_ref[...].astype(F32))
    self_drop = head_sum(g * v_ref[...].astype(F32))
    product = near_q * far_k
    hi, lo = halves(product)
    pair_score = dot(heads, hi, 1, 1) + dot(heads, lo, 1, 1)
    by_edge = dot(hi, heads, 1, 1) + dot(lo, heads, 1, 1)
    pair_drop = head_sum(near_g * far_v)
    top_ref[...] = self_score
    for s in (0, 1, 2, 3, 8, 9, 10, 11):
        best = jnp.max(jnp.where(hot, by_edge[:, s:s + 1], LOW), axis=0, keepdims=True)
        top_ref[s:s + 1, :] = jnp.maximum(top_ref[s:s + 1, :], best)
    top = top_ref[...]
    self_exp = jnp.exp(self_score - top)
    pair_exp = jnp.exp(pair_score - select_sum(top, hot_t))
    st_ref[0:16] = top
    st_ref[16:32] = self_exp + select_sum(pair_exp, hot_b)
    st_ref[32:48] = self_exp
    st_ref[48:64] = pair_exp
    st_ref[64:80] = self_drop
    st_ref[80:96] = pair_drop


def tile_kernel(info, nc_ref, nr_ref, n0, n1, n2, n3, r0, r1, r2, r3, qs_ref, gs_ref, qt_ref, gt_ref, bias_ref, st_ref,
                s0, s1, s2, s3, sk, sv, out_ref, gq_ref, wd_ref,
                kb, vb, eb, mt, lt, ft, top2, sum2, del2, dk, dv, in_sem):
    count = info[SLOTS, 0]
    near_half, far_half = (n0, n1, n2, n3), (r0, r1, r2, r3)

    def load(t, part, source=n0, index=0):
        buf = kb if part == 0 else vb
        return pltpu.make_async_copy(source.at[index], buf.at[t], in_sem.at[part, t])

    @pl.loop(0, count)
    def _(t):
        for part in range(2):
            index = info[t, 4 + part]
            for b in range(2):
                @pl.when((info[t, 2] == b) & (index < 8))
                def _():
                    load(t, part, near_half[2 * part + b], index).start()

                @pl.when((info[t, 2] == b) & (index >= 8))
                def _():
                    load(t, part, far_half[2 * part + b], index - 8).start()

    top1, sum1 = st_ref[0:16], st_ref[16:32]
    self_exp, pair_exp = st_ref[32:48], st_ref[48:64]
    self_drop, pair_drop = st_ref[64:80], st_ref[80:96]
    hot_b = as_bf16(one_hot(nc_ref[...]))
    hot_t = as_bf16(one_hot_t(nr_ref[...]))
    for a in range(2):
        top2[a] = to_blocks(top1, a)

    @pl.loop(0, count)
    def _(t):
        a = info[t, 0]
        load(t, 0).wait()
        bias = bias_ref[t]
        bias = jnp.concatenate([bias, bias], axis=1)
        for p in range(PAIRS):
            s = dot(kb[t, :, p * TILE:(p + 1) * TILE], qs_ref[a, p]) + bias
            m = jnp.max(s, axis=0, keepdims=True)
            e = jnp.exp(s - m)
            eb[t, p] = e
            mt[t, p:p + 1] = m
            lt[t, p:p + 1] = jnp.sum(e, axis=0, keepdims=True)
        top2[a, 0:PAIRS] = jnp.maximum(top2[a, 0:PAIRS], mt[t, 0:PAIRS])

    for a in range(2):
        sum2[a] = to_blocks(sum1, a) * jnp.exp(to_blocks(top1, a) - top2[a])

    @pl.loop(0, count)
    def _(t):
        a = info[t, 0]
        shrink = jnp.exp(mt[t, 0:PAIRS] - top2[a, 0:PAIRS])
        ft[t, 0:PAIRS] = shrink
        sum2[a, 0:PAIRS] += lt[t, 0:PAIRS] * shrink

    @pl.loop(0, count)
    def _(t):
        a = info[t, 0]
        ft[t, 0:PAIRS] = ft[t, 0:PAIRS] / sum2[a, 0:PAIRS]

    factor = jnp.exp(top1 - from_blocks(top2[0], top2[1])) / from_blocks(sum2[0], sum2[1])
    self_w = self_exp * factor
    pair_w = pair_exp * select_sum(factor, hot_t)
    self_wb = self_w.astype(BF16).astype(F32)
    pair_wb = pair_w.astype(BF16).astype(F32)
    wd_ref[0:16] = self_wb
    wd_ref[16:32] = pair_wb
    delta = self_wb * self_drop + select_sum(pair_wb * pair_drop, hot_b)

    out_ref[...] = jnp.zeros_like(out_ref)
    gq_ref[...] = jnp.zeros_like(gq_ref)

    def add_term(acc, t, p, term):
        f = info[t, 3]
        cols = slice(p * TILE, (p + 1) * TILE)
        acc[f, :, cols] = jnp.where(f == t, 0.0, acc[f, :, cols]) + term

    @pl.loop(0, count)
    def _(t):
        a = info[t, 0]
        load(t, 1).wait()
        for p in range(PAIRS):
            wb = (eb[t, p] * ft[t, p:p + 1]).astype(BF16)
            out_ref[a, p] += dot(vb[t, :, p * TILE:(p + 1) * TILE], wb, 0, 0)
            add_term(dv, t, p, dot(wb, gt_ref[a, p]))

    for a in range(2):
        base = to_blocks(delta, a)
        for p in range(PAIRS):
            del2[a, p:p + 1] = base[p:p + 1] + jnp.sum(
                gs_ref[a, p].astype(F32) * out_ref[a, p], axis=0, keepdims=True)
        del2[a, PAIRS:8] = jnp.zeros((8 - PAIRS, 2 * TILE), F32)
    delta = from_blocks(del2[0], del2[1])
    wd_ref[32:48] = self_w * (self_drop - delta)
    wd_ref[48:64] = pair_w * (pair_drop - select_sum(delta, hot_t))

    @pl.loop(0, count)
    def _(t):
        a = info[t, 0]
        for p in range(PAIRS):
            cols = slice(p * TILE, (p + 1) * TILE)
            drop = dot(vb[t, :, cols], gs_ref[a, p])
            ds = (eb[t, p] * ft[t, p:p + 1] * (drop - del2[a, p:p + 1])).astype(BF16)
            gq_ref[a, p] += dot(kb[t, :, cols], ds, 0, 0)
            add_term(dk, t, p, dot(ds, qt_ref[a, p]))

    sends = (s0, s1, s2, s3)
    for out in sends:
        out[...] = jnp.zeros_like(out)

    @pl.loop(0, count)
    def _(t):
        @pl.when(info[t, 3] == t)
        def _():
            for part, (acc, stage) in enumerate(((dk, sk), (dv, sv))):
                term = acc[t].astype(BF16)
                stage[t] = term
                index = info[t, 4 + part]
                for b in range(2):
                    @pl.when((info[t, 2] == b) & (index >= 8))
                    def _():
                        sends[2 * part + b][index - 8] = term


def each_term(info, sk, sv, low, high, add):
    @pl.loop(0, info[SLOTS, 0])
    def _(t):
        for part, stage in enumerate((sk, sv)):
            index = info[t, 4 + part]
            for b in range(2):
                @pl.when((info[t, 3] == t) & (info[t, 2] == b) & (index >= low) & (index < high))
                def _():
                    add(2 * part + b, index, stage[t].astype(F32))


def second_kernel(info, sk, sv, g0, g1, g2, g3, o0, o1, o2, o3):
    got, outs = (g0, g1, g2, g3), (o0, o1, o2, o3)
    for q in range(4):
        outs[q][...] = got[q][4:8]

    def add(q, index, term):
        outs[q][index - 4] = (got[q][index].astype(F32) + term).astype(BF16)

    each_term(info, sk, sv, 4, 8, add)


def third_kernel(info, sk, sv, a0, a1, a2, a3, g0, g1, g2, g3, o0, o1, o2, o3, k0, k1, k2, k3, total):
    had, got, outs, kept = (a0, a1, a2, a3), (g0, g1, g2, g3), (o0, o1, o2, o3), (k0, k1, k2, k3)
    for q in range(4):
        total[q] = had[q][0:4].astype(F32) + got[q][...].astype(F32)

    def add(q, index, term):
        total[q, index] += term

    each_term(info, sk, sv, 0, 4, add)
    for q in range(4):
        kept[q][...] = total[q, 0:2]
        outs[q][...] = total[q, 2:4].astype(BF16)


def fourth_kernel(a0, a1, a2, a3, g0, g1, g2, g3, o0, o1, o2, o3, k0, k1, k2, k3):
    had, got, outs, kept = (a0, a1, a2, a3), (g0, g1, g2, g3), (o0, o1, o2, o3), (k0, k1, k2, k3)
    for q in range(4):
        kept[q][...] = had[q][0:1] + got[q][0:1].astype(F32)
        outs[q][...] = (had[q][1:2] + got[q][1:2].astype(F32)).astype(BF16)


def rest_kernel(nr_ref, q_ref, k_ref, v_ref, g_ref, f0, f1, f2, f3, nq_ref, ng_ref, acc_ref, gacc_ref, wd_ref,
                out_ref, gq_ref, own_ref, b0, b1, b2, b3):
    hot_t = as_bf16(one_hot_t(nr_ref[...]))
    heads = head_rows()

    def expand(x):
        return dot(x.astype(BF16), heads, 0, 0)

    far = jnp.concatenate([f0[...], f1[...], f2[...], f3[...]], axis=0).astype(F32)
    self_wb, pair_wb = expand(wd_ref[0:16]), expand(wd_ref[16:32])
    self_ds, pair_ds = expand(wd_ref[32:48]), expand(wd_ref[48:64])
    back_k = (pair_ds * nq_ref[...].astype(F32)).astype(BF16)
    back_v = (pair_wb * ng_ref[...].astype(F32)).astype(BF16)
    for m, out in enumerate((b0, b1, b2, b3)):
        part = slice(m * EDGES, (m + 1) * EDGES)
        out[:, :WIDTH] = back_k[part]
        out[:, WIDTH:] = back_v[part]
    own_ref[0:ROWS] = self_ds * (q_ref[...].astype(F32) * SCALE)
    own_ref[ROWS:2 * ROWS] = self_wb * g_ref[...].astype(F32)

    def finish(own, pair, acc, scale, out):
        hi, lo = halves(pair)
        total = own + dot(hot_t, hi) + dot(hot_t, lo)
        for a in range(2):
            for p in range(PAIRS):
                x = acc[a, p]
                x = jnp.concatenate([x[0:64, :TILE], x[64:TILE, TILE:]], axis=0).T
                rows, cols = slice(a * TILE, (a + 1) * TILE), slice(p * TILE, (p + 1) * TILE)
                out[rows, cols] = ((total[rows, cols] + x) * scale).astype(BF16)

    finish(self_wb * v_ref[...].astype(F32), pair_wb * far[:, WIDTH:], acc_ref, 1.0, out_ref)
    finish(self_ds * k_ref[...].astype(F32), pair_ds * far[:, :WIDTH], gacc_ref, SCALE, gq_ref)


def last_kernel(nr_ref, a0, a1, a2, a3, g0, g1, g2, g3, own_ref, b0, b1, b2, b3, gk_ref, gv_ref):
    had, got = (a0, a1, a2, a3), (g0, g1, g2, g3)
    hot_t = as_bf16(one_hot_t(nr_ref[...]))
    back = jnp.concatenate([b0[...], b1[...], b2[...], b3[...]], axis=0)
    for part, out in enumerate((gk_ref, gv_ref)):
        pairs = dot(hot_t, back[:, part * WIDTH:(part + 1) * WIDTH])
        for b in range(2):
            q, rows = 2 * part + b, slice(b * TILE, (b + 1) * TILE)
            own = own_ref[part * ROWS + b * TILE:part * ROWS + (b + 1) * TILE]
            out[rows] = (had[q][0] + got[q][0].astype(F32) + own + pairs[rows]).astype(BF16)


def call(kernel, outs, ins, args, cost=(1e8, 4e6), scratch=(), out_specs=None, **more):
    vmem = pl.BlockSpec(memory_space=pltpu.VMEM)
    return pl.pallas_call(
        kernel,
        out_shape=[jax.ShapeDtypeStruct(s, d) for s, d in outs],
        in_specs=[vmem] * len(args) if ins is None else ins,
        out_specs=[vmem] * len(outs) if out_specs is None else out_specs,
        scratch_shapes=list(scratch),
        compiler_params=pltpu.CompilerParams(vmem_limit_bytes=VMEM_LIMIT),
        cost_estimate=pl.CostEstimate(flops=int(cost[0]), bytes_accessed=int(cost[1]), transcendentals=0),
        **more,
    )(*args)


def cross(blocks, step):
    return [
        lax.ppermute(block, "dom", [(i, i ^ ROUTE[q][step]) for i in range(DOMAINS)])
        for q, block in enumerate(blocks)
    ]


def to_group(code):
    pairs = [(i, i ^ code) for i in range(GROUPS)]
    return lambda block: lax.ppermute(block, "grp", pairs)


def switched(block, code):
    return lax.switch(code - 1, [to_group(c) for c in range(1, GROUPS)], block)


def halfway_first(rows, at):
    return jnp.stack([
        sum(jnp.where(at == m, rows[m], 0) for m in range(MATCH)),
        *(jnp.where(m - 1 < at, rows[m - 1], rows[m]) for m in range(1, MATCH)),
    ])


def body(query, key, value, cotangent, tile_index, tile_mask, tile_count, partner, pair_edges):
    vmem = pl.BlockSpec(memory_space=pltpu.VMEM)
    anywhere = pl.BlockSpec(memory_space=pl.ANY)
    smem = pl.BlockSpec(memory_space=pltpu.SMEM)
    tied = lax.optimization_barrier

    own = [x[None, b * TILE:(b + 1) * TILE] for x in (key, value) for b in range(2)]
    held = own
    for step in range(2):
        got = cross(held, step)
        if step == 0:
            held = [jnp.concatenate([h, g], axis=0) for h, g in zip(held, tied(got))]

    codes = jnp.bitwise_xor(partner[0] // DOMAINS, lax.axis_index("grp"))
    slot4 = jnp.arange(MATCH, dtype=jnp.int32)
    at = jnp.sum(jnp.where(codes == GROUPS // 2, slot4, 0))
    codes = halfway_first(codes, at)
    near = halfway_first(pair_edges[0, :, :, 0], at).reshape(-1)
    near_col, near_row = near.reshape(-1, 1), near.reshape(1, -1)

    entries = tile_index[0]
    place = entries[:, 1] * 2 + entries[:, 2]
    slot = jnp.arange(SLOTS, dtype=jnp.int32)
    first = jnp.min(jnp.where(place[:, None] == place[None, :], slot[None, :], SLOTS), axis=1)
    apart = jnp.bitwise_xor(entries[:, 1], lax.axis_index("dom"))
    links = {}
    for low, base in ((1, 0), (4, 2)):
        pair = (apart >> base) & 3
        links[low * 3] = pair >> 1
        links[low] = (pair ^ (pair >> 1)) & 1
    index = [sum(links[link] << step for step, link in enumerate(order)) for order in ROUTE]
    second = entries[:, 2] == 1
    info = jnp.stack(
        [entries[:, 0], entries[:, 1], entries[:, 2], first.astype(jnp.int32),
         jnp.where(second, index[1], index[0]), jnp.where(second, index[3], index[2])], axis=1)
    info = jnp.concatenate([info, jnp.broadcast_to(tile_count[:, None], (1, 6))], axis=0)

    block = ((EDGES, 2 * WIDTH), BF16)
    sent = call(pick_kernel, [block] * MATCH, None, (near_col, key, value))
    far0 = to_group(GROUPS // 2)(sent[0])

    node = ((ROWS, WIDTH), BF16)
    by_col = ((2, PAIRS, TILE, 2 * TILE), BF16)
    by_row = ((2, PAIRS, 2 * TILE, TILE), BF16)
    qs, gs, qt, gt, bias = call(
        layout_kernel, [by_col, by_col, by_row, by_row, ((SLOTS, TILE, TILE), F32)],
        None, (query, cotangent, tile_mask[0]))

    got, sent1 = tied((got, sent[1]))
    held = [jnp.concatenate([h, g], axis=0) for h, g in zip(held, got)]
    got = cross(held, 2)
    far1 = switched(sent1, codes[1])
    got, far1, sent2, sent3 = tied((got, far1, sent[2], sent[3]))
    held = [jnp.concatenate([h, g], axis=0) for h, g in zip(held, got)]
    held, sent2, sent3 = tied((held, sent2, sent3))
    got = cross(held, 3)
    far2, far3 = switched(sent2, codes[2]), switched(sent3, codes[3])
    far = [far0, far1, far2, far3]

    near_q, near_g, stats = call(
        pair_kernel, [node, node, ((96, ROWS), F32)], None,
        (near_col, near_row, query, key, value, cotangent, *far),
        scratch=[pltpu.VMEM((16, ROWS), F32)],
    )

    acc = ((2, PAIRS, TILE, 2 * TILE), F32)
    row_stat = pltpu.VMEM((SLOTS, 8, 2 * TILE), F32)
    block_stat = pltpu.VMEM((2, 8, 2 * TILE), F32)
    tiles_b = pltpu.VMEM((SLOTS, TILE, WIDTH), BF16)
    tiles_f = pltpu.VMEM((SLOTS, TILE, WIDTH), F32)
    terms = ((SLOTS, TILE, WIDTH), BF16)
    *send, own_k, own_v, out_acc, gq_acc, grads = call(
        tile_kernel,
        [terms] * 6 + [acc, acc, ((64, ROWS), F32)],
        [smem, vmem, vmem] + [anywhere] * 8 + [vmem] * 6,
        (info, near_col, near_row, *held, *got, qs, gs, qt, gt, bias, stats),
        cost=(1e9, 2e7),
        scratch=[
            tiles_b, tiles_b, pltpu.VMEM((SLOTS, PAIRS, TILE, 2 * TILE), F32),
            row_stat, row_stat, row_stat, block_stat, block_stat, block_stat,
            tiles_f, tiles_f, pltpu.SemaphoreType.DMA((2, SLOTS)),
        ],
    )

    got = cross(send, 3)
    attended, grad_query, own, *back = call(
        rest_kernel,
        [node, node, ((2 * ROWS, WIDTH), F32)] + [block] * MATCH,
        None,
        (near_row, query, key, value, cotangent, *far, near_q, near_g, out_acc, gq_acc, grads),
    )
    back0 = to_group(GROUPS // 2)(back[0])
    back1, back2 = switched(back[1], codes[1]), switched(back[2], codes[2])
    got, back1, back2, back3 = tied((got, back1, back2, back[3]))

    def some(n, kind):
        return [((n, TILE, WIDTH), kind)] * 4

    send = call(second_kernel, some(4, BF16), [smem] + [vmem] * 6, (info, own_k, own_v, *got))
    more = cross(send, 2)
    back3 = switched(back3, codes[3])
    more, back3 = tied((more, back3))
    result = call(
        third_kernel, some(2, BF16) + some(2, F32), [smem] + [vmem] * 10, (info, own_k, own_v, *got, *more),
        scratch=[pltpu.VMEM((4, 4, TILE, WIDTH), F32)])
    send, kept = result[:4], result[4:]
    got = tied(cross(send, 1))
    result = call(fourth_kernel, some(1, BF16) + some(1, F32), None, (*kept, *got))
    send, kept = result[:4], result[4:]
    got = cross(send, 0)
    grad_key, grad_value = call(
        last_kernel, [node, node], None, (near_row, *kept, *got, own, back0, back1, back2, back3))
    return attended, grad_query, grad_key, grad_value


def solution(mesh):
    rows = P(("grp", "dom"), None)
    return jax.shard_map(
        body,
        mesh=mesh,
        in_specs=(
            rows, rows, rows, rows,
            P(("grp", "dom"), None, None),
            P(("grp", "dom"), None, None, None),
            P(("grp", "dom")),
            rows,
            P(("grp", "dom"), None, None, None),
        ),
        out_specs=(rows, rows, rows, rows),
        check_vma=False,
    )
```

```python
import jax
import jax.numpy as jnp
from jax import lax
from jax.experimental import pallas as pl
from jax.experimental.pallas import tpu as pltpu
from jax.sharding import PartitionSpec as P

F32 = jnp.float32
BF16 = jnp.bfloat16
LOW = -1e30
SCALE = 0.125
ROWS = 256
WIDTH = 512
TILE = 128
PAIRS = 4
SLOTS = 8
MATCH = 4
EDGES = 64
DOMAINS = 16
GROUPS = 16
VMEM_LIMIT = 50 * 2**20
HALF = WIDTH // 2
TAIL = 16
LINKS = (1, 3, 4, 12)
THIRD = (1, 3, 4, 12)
FOURTH = (3, 1, 12, 4)
A, B, FIRST, BITS = 0, 1, 2, 3
LIST = 2 * SLOTS

def dot(a, b, da=1, db=0):
    return lax.dot_general(a, b, (((da,), (db,)), ((), ())), preferred_element_type=F32)


def one_hot(near_col):
    e, r = near_col.shape[0], ROWS
    return lax.broadcasted_iota(jnp.int32, (e, r), 1) == near_col


def one_hot_t(near_row):
    e, r = near_row.shape[1], ROWS
    return lax.broadcasted_iota(jnp.int32, (r, e), 0) == near_row


def as_bf16(flags):
    return jnp.where(flags, 1.0, 0.0).astype(BF16)


def head_rows():
    s = lax.broadcasted_iota(jnp.int32, (16, WIDTH), 0)
    c = lax.broadcasted_iota(jnp.int32, (16, WIDTH), 1)
    return as_bf16((c >> 6) == 2 * (s & 7) + (s >> 3))


def halves(x):
    hi = x.astype(BF16)
    return hi, (x - hi.astype(F32)).astype(BF16)


def thirds(x):
    hi = x.astype(BF16)
    rest = x - hi.astype(F32)
    mid = rest.astype(BF16)
    return jnp.concatenate([hi, mid, (rest - mid.astype(F32)).astype(BF16)], axis=0)


def select_sum(x, matrix):
    y = dot(thirds(x), matrix)
    return y[0:16] + y[16:32] + y[32:48]


def to_blocks(x, a):
    lanes = slice(a * TILE, (a + 1) * TILE)
    return jnp.concatenate([x[0:8, lanes], x[8:16, lanes]], axis=1)


def from_blocks(x0, x1):
    even = jnp.concatenate([x0[:, :TILE], x1[:, :TILE]], axis=1)
    odd = jnp.concatenate([x0[:, TILE:], x1[:, TILE:]], axis=1)
    return jnp.concatenate([even, odd], axis=0)


def pick_kernel(near_ref, k_ref, v_ref, *outs):
    hot = as_bf16(one_hot(near_ref[...]))
    rows_k = dot(hot, k_ref[...]).astype(BF16)
    rows_v = dot(hot, v_ref[...]).astype(BF16)
    for m, out in enumerate(outs):
        part = slice(m * EDGES, (m + 1) * EDGES)
        out[:, :WIDTH] = rows_k[part]
        out[:, WIDTH:] = rows_v[part]


def layout_kernel(q_ref, g_ref, mask_ref, qs_ref, gs_ref, qt_ref, gt_ref, bias_ref):
    low_rows = lax.broadcasted_iota(jnp.int32, (TILE, TILE), 0) < 64
    low_lanes = lax.broadcasted_iota(jnp.int32, (TILE, TILE), 1) < 64

    for t in range(SLOTS):
        bias_ref[t] = jnp.where(mask_ref[t].astype(F32).T != 0, 0.0, LOW)

    qs = q_ref[...].astype(F32) * SCALE
    g = g_ref[...].astype(F32)
    for source, by_col, by_row in ((qs, qs_ref, qt_ref), (g, gs_ref, gt_ref)):
        for a in range(2):
            for p in range(PAIRS):
                x = source[a * TILE:(a + 1) * TILE, p * TILE:(p + 1) * TILE]
                xt = x.T
                by_col[a, p] = jnp.concatenate(
                    [jnp.where(low_rows, xt, 0.0), jnp.where(low_rows, 0.0, xt)], axis=1).astype(BF16)
                by_row[a, p] = jnp.concatenate(
                    [jnp.where(low_lanes, x, 0.0), jnp.where(low_lanes, 0.0, x)], axis=0).astype(BF16)


def pair_kernel(nc_ref, nr_ref, q_ref, k_ref, v_ref, g_ref, f0, f1, f2, f3, nq_ref, ng_ref, st_ref, top_ref):
    hot = one_hot(nc_ref[...])
    hot_b = as_bf16(hot)
    hot_t = as_bf16(one_hot_t(nr_ref[...]))
    heads = head_rows()
    qs = q_ref[...].astype(F32) * SCALE
    g = g_ref[...].astype(F32)

    far = jnp.concatenate([f0[...], f1[...], f2[...], f3[...]], axis=0).astype(F32)
    far_k, far_v = far[:, :WIDTH], far[:, WIDTH:]
    near_q = dot(hot_b, qs.astype(BF16))
    near_g = dot(hot_b, g_ref[...])
    nq_ref[...] = near_q.astype(BF16)
    ng_ref[...] = near_g.astype(BF16)

    def head_sum(x):
        hi, lo = halves(x)
        return dot(heads, hi, 1, 1) + dot(heads, lo, 1, 1)

    self_score = head_sum(qs * k_ref[...].astype(F32))
    self_drop = head_sum(g * v_ref[...].astype(F32))
    product = near_q * far_k
    hi, lo = halves(product)
    pair_score = dot(heads, hi, 1, 1) + dot(heads, lo, 1, 1)
    by_edge = dot(hi, heads, 1, 1) + dot(lo, heads, 1, 1)
    pair_drop = head_sum(near_g * far_v)
    top_ref[...] = self_score
    for s in (0, 1, 2, 3, 8, 9, 10, 11):
        best = jnp.max(jnp.where(hot, by_edge[:, s:s + 1], LOW), axis=0, keepdims=True)
        top_ref[s:s + 1, :] = jnp.maximum(top_ref[s:s + 1, :], best)
    top = top_ref[...]
    self_exp = jnp.exp(self_score - top)
    pair_exp = jnp.exp(pair_score - select_sum(top, hot_t))
    st_ref[0:16] = top
    st_ref[16:32] = self_exp + select_sum(pair_exp, hot_b)
    st_ref[32:48] = self_exp
    st_ref[48:64] = pair_exp
    st_ref[64:80] = self_drop
    st_ref[80:96] = pair_drop


def bit(info, row, link):
    return info[row, BITS + LINKS.index(link)]


def ring_index(info, row, part):
    low, high = ((4, 12), (1, 3))[part]
    return bit(info, row, low) + 2 * bit(info, row, high)


def split_kernel(me, tail_ref, k0, k1, k2, k3, v0, v1, v2, v3, ka, kb, va, vb, info_ref, tails, sem):
    copies = []
    for p, (sources, outs) in enumerate((((k0, k1, k2, k3), (ka, kb)), ((v0, v1, v2, v3), (va, vb)))):
        for i, source in enumerate(sources):
            for h, out in enumerate(outs):
                copies.append(pltpu.make_async_copy(
                    source.at[0:ROWS, h * HALF:(h + 1) * HALF], out.at[i], sem.at[p * 8 + i * 2 + h]))
    for i, source in enumerate((v1, v2, k1, k2)):
        copies.append(pltpu.make_async_copy(source.at[ROWS:ROWS + TAIL, 0:TILE], tails.at[i], sem.at[16 + i]))
    for copy in copies:
        copy.start()
    for copy in copies[16:]:
        copy.wait()
    lane = lax.broadcasted_iota(jnp.int32, (SLOTS, TILE), 1)
    for i in range(5):
        tail = tail_ref[:, 0:TILE] if i == 0 else tails[i - 1]
        tail = tail[0:SLOTS].astype(F32).astype(jnp.int32)
        block, owner, rows, count = (tail[:, c:c + 1] for c in range(4))
        place = owner * 2 + rows
        first = jnp.full((SLOTS, 1), SLOTS, jnp.int32)
        for t in range(SLOTS):
            first = jnp.minimum(first, jnp.where(place == place[t:t + 1], t, SLOTS))
        apart = owner ^ me[0, 0]
        x, y = apart >> 2, apart & 3
        columns = (block, rows, first, (y ^ (y >> 1)) & 1, y >> 1, (x ^ (x >> 1)) & 1, x >> 1)
        table = jnp.zeros((SLOTS, TILE), jnp.int32)
        for c, column in enumerate(columns):
            table = jnp.where(lane == c, column, table)
        info_ref[i * LIST:i * LIST + SLOTS] = table
        info_ref[i * LIST + SLOTS:(i + 1) * LIST] = jnp.where(lane == 0, count, 0)
    for copy in copies[:16]:
        copy.wait()


def pack_kernel(info, h0, h1, h2, h3, g0, g1, g2, g3, o0, o1, o2, o3, sem):
    held, got, outs = (h0, h1, h2, h3), (g0, g1, g2, g3), (o0, o1, o2, o3)

    def copies(act):
        for q in range(4):
            base = (1 + LINKS.index(FOURTH[q])) * LIST

            @pl.loop(0, info[base + SLOTS, 0])
            def _(t):
                row = base + t
                index = ring_index(info, row, q // 2)
                rows = pl.ds(pl.multiple_of(info[row, B] * TILE, TILE), TILE)
                here = bit(info, row, FOURTH[q]) == 0
                for other, source in enumerate((held[q], got[q])):
                    @pl.when(here & (bit(info, row, THIRD[q]) == other))
                    def _():
                        act(pltpu.make_async_copy(source.at[index, rows], outs[q].at[t], sem.at[q, t]))

    copies(lambda copy: copy.start())
    copies(lambda copy: copy.wait())


def tile_kernel(info, nc_ref, nr_ref, h0, h1, h2, h3, g0, g1, g2, g3, p0, p1, p2, p3,
                qs_ref, gs_ref, qt_ref, gt_ref, bias_ref, st_ref,
                s0, s1, s2, s3, out_ref, gq_ref, wd_ref,
                kb, vb, eb, mt, lt, ft, top2, sum2, del2, dk, dv, in_sem):
    count = info[SLOTS, 0]
    held, got, packed = (h0, h1, h2, h3), (g0, g1, g2, g3), (p0, p1, p2, p3)

    def into(t, q):
        return (kb, kb, vb, vb)[q].at[t, :, pl.ds((q % 2) * HALF, HALF)]

    @pl.loop(0, count)
    def _(t):
        rows = pl.ds(pl.multiple_of(info[t, B] * TILE, TILE), TILE)
        for q in range(4):
            index = ring_index(info, t, q // 2)
            third, fourth = bit(info, t, THIRD[q]), bit(info, t, FOURTH[q])

            def fetch(source):
                pltpu.make_async_copy(source, into(t, q), in_sem.at[q, t]).start()

            @pl.when(fourth == 1)
            def _():
                fetch(packed[q].at[t])

            @pl.when((fourth == 0) & (third == 1))
            def _():
                fetch(got[q].at[index, rows])

            @pl.when((fourth == 0) & (third == 0))
            def _():
                fetch(held[q].at[index, rows])

    def arrived(t, part):
        for q in (2 * part, 2 * part + 1):
            pltpu.make_async_copy(packed[q].at[0], into(t, q), in_sem.at[q, t]).wait()

    top1, sum1 = st_ref[0:16], st_ref[16:32]
    self_exp, pair_exp = st_ref[32:48], st_ref[48:64]
    self_drop, pair_drop = st_ref[64:80], st_ref[80:96]
    hot_b = as_bf16(one_hot(nc_ref[...]))
    hot_t = as_bf16(one_hot_t(nr_ref[...]))
    for a in range(2):
        top2[a] = to_blocks(top1, a)

    @pl.loop(0, count)
    def _(t):
        a = info[t, 0]
        arrived(t, 0)
        bias = bias_ref[t]
        bias = jnp.concatenate([bias, bias], axis=1)
        for p in range(PAIRS):
            s = dot(kb[t, :, p * TILE:(p + 1) * TILE], qs_ref[a, p]) + bias
            m = jnp.max(s, axis=0, keepdims=True)
            e = jnp.exp(s - m)
            eb[t, p] = e
            mt[t, p:p + 1] = m
            lt[t, p:p + 1] = jnp.sum(e, axis=0, keepdims=True)
        top2[a, 0:PAIRS] = jnp.maximum(top2[a, 0:PAIRS], mt[t, 0:PAIRS])

    for a in range(2):
        sum2[a] = to_blocks(sum1, a) * jnp.exp(to_blocks(top1, a) - top2[a])

    @pl.loop(0, count)
    def _(t):
        a = info[t, 0]
        shrink = jnp.exp(mt[t, 0:PAIRS] - top2[a, 0:PAIRS])
        ft[t, 0:PAIRS] = shrink
        sum2[a, 0:PAIRS] += lt[t, 0:PAIRS] * shrink

    @pl.loop(0, count)
    def _(t):
        a = info[t, 0]
        ft[t, 0:PAIRS] = ft[t, 0:PAIRS] / sum2[a, 0:PAIRS]

    factor = jnp.exp(top1 - from_blocks(top2[0], top2[1])) / from_blocks(sum2[0], sum2[1])
    self_w = self_exp * factor
    pair_w = pair_exp * select_sum(factor, hot_t)
    self_wb = self_w.astype(BF16).astype(F32)
    pair_wb = pair_w.astype(BF16).astype(F32)
    wd_ref[0:16] = self_wb
    wd_ref[16:32] = pair_wb
    delta = self_wb * self_drop + select_sum(pair_wb * pair_drop, hot_b)

    out_ref[...] = jnp.zeros_like(out_ref)
    gq_ref[...] = jnp.zeros_like(gq_ref)

    def add_term(acc, t, p, term):
        f = info[t, FIRST]
        cols = slice(p * TILE, (p + 1) * TILE)
        acc[f, :, cols] = jnp.where(f == t, 0.0, acc[f, :, cols]) + term

    @pl.loop(0, count)
    def _(t):
        a = info[t, 0]
        arrived(t, 1)
        for p in range(PAIRS):
            wb = (eb[t, p] * ft[t, p:p + 1]).astype(BF16)
            out_ref[a, p] += dot(vb[t, :, p * TILE:(p + 1) * TILE], wb, 0, 0)
            add_term(dv, t, p, dot(wb, gt_ref[a, p]))

    for a in range(2):
        base = to_blocks(delta, a)
        for p in range(PAIRS):
            del2[a, p:p + 1] = base[p:p + 1] + jnp.sum(
                gs_ref[a, p].astype(F32) * out_ref[a, p], axis=0, keepdims=True)
        del2[a, PAIRS:8] = jnp.zeros((8 - PAIRS, 2 * TILE), F32)
    delta = from_blocks(del2[0], del2[1])
    wd_ref[32:48] = self_w * (self_drop - delta)
    wd_ref[48:64] = pair_w * (pair_drop - select_sum(delta, hot_t))

    @pl.loop(0, count)
    def _(t):
        a = info[t, 0]
        for p in range(PAIRS):
            cols = slice(p * TILE, (p + 1) * TILE)
            drop = dot(vb[t, :, cols], gs_ref[a, p])
            ds = (eb[t, p] * ft[t, p:p + 1] * (drop - del2[a, p:p + 1])).astype(BF16)
            gq_ref[a, p] += dot(kb[t, :, cols], ds, 0, 0)
            add_term(dk, t, p, dot(ds, qt_ref[a, p]))

    @pl.loop(0, count)
    def _(t):
        @pl.when(info[t, FIRST] == t)
        def _():
            s0[t] = dk[t, :, 0:HALF].astype(BF16)
            s1[t] = dk[t, :, HALF:WIDTH].astype(BF16)
            s2[t] = dv[t, :, 0:HALF].astype(BF16)
            s3[t] = dv[t, :, HALF:WIDTH].astype(BF16)


def each_term(info, q, third, mine, theirs, add):
    for base, terms in ((0, mine), ((1 + LINKS.index(FOURTH[q])) * LIST, theirs)):
        @pl.loop(0, info[base + SLOTS, 0])
        def _(t):
            row = base + t

            @pl.when((info[row, FIRST] == t) & (bit(info, row, FOURTH[q]) == 0) & (bit(info, row, THIRD[q]) == third))
            def _():
                rows = pl.ds(pl.multiple_of(info[row, B] * TILE, TILE), TILE)
                add(ring_index(info, row, q // 2), rows, terms[t].astype(F32))


def second_kernel(info, m0, m1, m2, m3, g0, g1, g2, g3, o0, o1, o2, o3):
    for q, (mine, theirs, out) in enumerate(zip((m0, m1, m2, m3), (g0, g1, g2, g3), (o0, o1, o2, o3))):
        out[...] = jnp.zeros_like(out)

        def add(index, rows, term):
            out[index, rows] = (out[index, rows].astype(F32) + term).astype(BF16)

        each_term(info, q, 1, mine, theirs, add)


def third_kernel(info, m0, m1, m2, m3, g0, g1, g2, g3, n0, n1, n2, n3,
                 k1, k2, k3, v1, v2, v3, kk, kv, total):
    got = (n0, n1, n2, n3)
    for q, (mine, theirs) in enumerate(zip((m0, m1, m2, m3), (g0, g1, g2, g3))):
        total[q] = got[q][...].astype(F32)

        def add(index, rows, term):
            total[q, index, rows] += term

        each_term(info, q, 0, mine, theirs, add)
        cols = slice((q % 2) * HALF, (q % 2 + 1) * HALF)
        (kk, kv)[q // 2][:, cols] = total[q, 0]
        for i, out in enumerate(((k1, k2, k3), (v1, v2, v3))[q // 2]):
            out[:, cols] = total[q, i + 1].astype(BF16)


def rest_kernel(nr_ref, q_ref, k_ref, v_ref, g_ref, f0, f1, f2, f3, nq_ref, ng_ref, acc_ref, gacc_ref, wd_ref,
                out_ref, gq_ref, own_ref, b0, b1, b2, b3):
    hot_t = as_bf16(one_hot_t(nr_ref[...]))
    heads = head_rows()

    def expand(x):
        return dot(x.astype(BF16), heads, 0, 0)

    far = jnp.concatenate([f0[...], f1[...], f2[...], f3[...]], axis=0).astype(F32)
    self_wb, pair_wb = expand(wd_ref[0:16]), expand(wd_ref[16:32])
    self_ds, pair_ds = expand(wd_ref[32:48]), expand(wd_ref[48:64])
    back_k = (pair_ds * nq_ref[...].astype(F32)).astype(BF16)
    back_v = (pair_wb * ng_ref[...].astype(F32)).astype(BF16)
    for m, out in enumerate((b0, b1, b2, b3)):
        part = slice(m * EDGES, (m + 1) * EDGES)
        out[:, :WIDTH] = back_k[part]
        out[:, WIDTH:] = back_v[part]
    own_ref[0:ROWS] = self_ds * (q_ref[...].astype(F32) * SCALE)
    own_ref[ROWS:2 * ROWS] = self_wb * g_ref[...].astype(F32)

    def finish(own, pair, acc, scale, out):
        hi, lo = halves(pair)
        total = own + dot(hot_t, hi) + dot(hot_t, lo)
        for a in range(2):
            for p in range(PAIRS):
                x = acc[a, p]
                x = jnp.concatenate([x[0:64, :TILE], x[64:TILE, TILE:]], axis=0).T
                rows, cols = slice(a * TILE, (a + 1) * TILE), slice(p * TILE, (p + 1) * TILE)
                out[rows, cols] = ((total[rows, cols] + x) * scale).astype(BF16)

    finish(self_wb * v_ref[...].astype(F32), pair_wb * far[:, WIDTH:], acc_ref, 1.0, out_ref)
    finish(self_ds * k_ref[...].astype(F32), pair_ds * far[:, :WIDTH], gacc_ref, SCALE, gq_ref)


def last_kernel(nr_ref, kk, kv, k1, k2, k3, v1, v2, v3, own_ref, b0, b1, b2, b3, gk_ref, gv_ref):
    hot_t = as_bf16(one_hot_t(nr_ref[...]))
    back = jnp.concatenate([b0[...], b1[...], b2[...], b3[...]], axis=0)
    for part, (kept, terms, out) in enumerate(((kk, (k1, k2, k3), gk_ref), (kv, (v1, v2, v3), gv_ref))):
        total = kept[...] + own_ref[part * ROWS:(part + 1) * ROWS]
        for term in terms:
            total += term[...].astype(F32)
        out[...] = (total + dot(hot_t, back[:, part * WIDTH:(part + 1) * WIDTH])).astype(BF16)


def staged(kernel, scalars, raw, n_in, n_out):
    def run(*refs):
        *refs, sem = refs
        moved = [i for i in range(scalars, n_in) if i not in raw]
        ins, outs = list(refs[:n_in]), refs[n_in:n_in + n_out]
        buffers, scratch = refs[n_in + n_out:n_in + n_out + len(moved)], refs[n_in + n_out + len(moved):]
        copies = [pltpu.make_async_copy(ins[i], buf, sem.at[j]) for j, (i, buf) in enumerate(zip(moved, buffers))]
        for copy in copies:
            copy.start()
        for copy in copies:
            copy.wait()
        for i, buf in zip(moved, buffers):
            ins[i] = buf
        kernel(*ins, *outs, *scratch)
    return run


def call(kernel, outs, args, scalars=0, raw=(), scratch=(), cost=(1e8, 4e6)):
    smem, anywhere = pl.BlockSpec(memory_space=pltpu.SMEM), pl.BlockSpec(memory_space=pl.ANY)
    moved = [x for i, x in enumerate(args) if i >= scalars and i not in raw]
    return pl.pallas_call(
        staged(kernel, scalars, raw, len(args), len(outs)),
        out_shape=[jax.ShapeDtypeStruct(s, d) for s, d in outs],
        in_specs=[smem] * scalars + [anywhere] * (len(args) - scalars),
        out_specs=[pl.BlockSpec(memory_space=pltpu.VMEM)] * len(outs),
        scratch_shapes=[pltpu.VMEM(x.shape, x.dtype) for x in moved] + list(scratch)
        + [pltpu.SemaphoreType.DMA((max(len(moved), 1),))],
        compiler_params=pltpu.CompilerParams(vmem_limit_bytes=VMEM_LIMIT),
        cost_estimate=pl.CostEstimate(flops=int(cost[0]), bytes_accessed=int(cost[1]), transcendentals=0),
    )(*args)


def over(block, link):
    return lax.ppermute(block, "dom", [(i, i ^ link) for i in range(DOMAINS)])


def to_group(code):
    pairs = [(i, i ^ code) for i in range(GROUPS)]
    return lambda block: lax.ppermute(block, "grp", pairs)


def switched(block, code):
    return lax.switch(code - 1, [to_group(c) for c in range(1, GROUPS)], block)


def halfway_first(rows, at):
    return jnp.stack([
        sum(jnp.where(at == m, rows[m], 0) for m in range(MATCH)),
        *(jnp.where(m - 1 < at, rows[m - 1], rows[m]) for m in range(1, MATCH)),
    ])


def body(query, key, value, cotangent, tile_index, tile_mask, tile_count, partner, pair_edges):
    tied = lax.optimization_barrier
    node = ((ROWS, WIDTH), BF16)
    half = ((4, ROWS, HALF), BF16)
    slots = ((SLOTS, TILE, HALF), BF16)
    block = ((EDGES, 2 * WIDTH), BF16)

    tail = jnp.concatenate([tile_index[0], jnp.broadcast_to(tile_count[:, None], (SLOTS, 1))], axis=1)
    tail = jnp.pad(tail.astype(BF16), ((0, TAIL - SLOTS), (0, WIDTH - 4)))
    keys, values = (jnp.concatenate([x, tail], axis=0) for x in (key, value))
    ring_k = [over(keys, link) for link in (8, 4, 12)]
    ring_v = [over(values, link) for link in (2, 1, 3)]

    codes = jnp.bitwise_xor(partner[0] // DOMAINS, lax.axis_index("grp"))
    slot4 = jnp.arange(MATCH, dtype=jnp.int32)
    at = jnp.sum(jnp.where(codes == GROUPS // 2, slot4, 0))
    codes = halfway_first(codes, at)
    near = halfway_first(pair_edges[0, :, :, 0], at).reshape(-1)
    near_col, near_row = near.reshape(-1, 1), near.reshape(1, -1)
    sent = call(pick_kernel, [block] * MATCH, (near_col, key, value))

    by_col = ((2, PAIRS, TILE, 2 * TILE), BF16)
    by_row = ((2, PAIRS, 2 * TILE, TILE), BF16)
    layouts = call(
        layout_kernel, [by_col, by_col, by_row, by_row, ((SLOTS, TILE, TILE), F32)],
        (query, cotangent, tile_mask[0]))
    ring_k, ring_v, layouts, sent = tied((ring_k, ring_v, layouts, sent))

    me = lax.axis_index("dom").reshape(1, 1)
    *held, info = call(
        split_kernel, [half] * 4 + [((5 * LIST, TILE), jnp.int32)],
        (me, tail, keys, ring_k[1], ring_k[2], ring_k[0], values, ring_v[1], ring_v[2], ring_v[0]),
        scalars=1, raw=range(2, 10),
        scratch=[pltpu.VMEM((4, TAIL, TILE), BF16), pltpu.SemaphoreType.DMA((20,))])
    held, info, sent = tied((held, info, sent))
    far0 = to_group(GROUPS // 2)(sent[0])
    got = [over(x, link) for x, link in zip(held, THIRD)]
    far1 = switched(sent[1], codes[1])
    got, far1, sent2, sent3 = tied((got, far1, sent[2], sent[3]))
    packs = call(
        pack_kernel, [slots] * 4, (info, *held, *got), scalars=1, raw=range(1, 9),
        scratch=[pltpu.SemaphoreType.DMA((4, SLOTS))])
    packs, sent2, sent3 = tied((packs, sent2, sent3))
    packed = [over(x, link) for x, link in zip(packs, FOURTH)]
    far = [far0, far1, switched(sent2, codes[2]), switched(sent3, codes[3])]
    near_q, near_g, stats = call(
        pair_kernel, [node, node, ((96, ROWS), F32)], (near_col, near_row, query, key, value, cotangent, *far),
        scratch=[pltpu.VMEM((16, ROWS), F32)])

    acc = ((2, PAIRS, TILE, 2 * TILE), F32)
    row_stat = pltpu.VMEM((SLOTS, 8, 2 * TILE), F32)
    block_stat = pltpu.VMEM((2, 8, 2 * TILE), F32)
    tiles_b = pltpu.VMEM((SLOTS, TILE, WIDTH), BF16)
    tiles_f = pltpu.VMEM((SLOTS, TILE, WIDTH), F32)
    *terms, out_acc, gq_acc, grads = call(
        tile_kernel,
        [slots] * 4 + [acc, acc, ((64, ROWS), F32)],
        (info, near_col, near_row, *held, *got, *packed, *layouts, stats),
        scalars=1, raw=range(3, 15), cost=(1e9, 2e7),
        scratch=[
            tiles_b, tiles_b, pltpu.VMEM((SLOTS, PAIRS, TILE, 2 * TILE), F32),
            row_stat, row_stat, row_stat, block_stat, block_stat, block_stat,
            tiles_f, tiles_f, pltpu.SemaphoreType.DMA((4, SLOTS)),
        ],
    )

    theirs = [over(x, link) for x, link in zip(terms, FOURTH)]
    attended, grad_query, own, *back = call(
        rest_kernel,
        [node, node, ((2 * ROWS, WIDTH), F32)] + [block] * MATCH,
        (near_row, query, key, value, cotangent, *far, near_q, near_g, out_acc, gq_acc, grads))
    back0 = to_group(GROUPS // 2)(back[0])
    back1, back2 = switched(back[1], codes[1]), switched(back[2], codes[2])
    theirs, back1, back2, back3 = tied((theirs, back1, back2, back[3]))
    sums = call(second_kernel, [half] * 4, (info, *terms, *theirs), scalars=1)
    sums, back3 = tied((sums, back3))
    more = [over(x, link) for x, link in zip(sums, THIRD)]
    back3 = switched(back3, codes[3])
    more, back0, back3 = tied((more, back0, back3))
    *ring, kept_k, kept_v = call(
        third_kernel, [node] * 6 + [((ROWS, WIDTH), F32)] * 2, (info, *terms, *theirs, *more), scalars=1,
        scratch=[pltpu.VMEM((4, 4, ROWS, HALF), F32)])
    order = ((2, 8), (5, 2), (0, 4), (3, 1), (1, 12), (4, 3))
    arrived = {i: over(ring[i], link) for i, link in order}
    grad_key, grad_value = call(
        last_kernel, [node, node],
        (near_row, kept_k, kept_v, *(arrived[i] for i in range(6)), own, back0, back1, back2, back3))
    return attended, grad_query, grad_key, grad_value


def solution(mesh):
    rows = P(("grp", "dom"), None)
    return jax.shard_map(
        body,
        mesh=mesh,
        in_specs=(
            rows, rows, rows, rows,
            P(("grp", "dom"), None, None),
            P(("grp", "dom"), None, None, None),
            P(("grp", "dom")),
            rows,
            P(("grp", "dom"), None, None, None),
        ),
        out_specs=(rows, rows, rows, rows),
        check_vma=False,
    )
```

```python
import jax
import jax.numpy as jnp
from jax import lax
from jax.experimental import pallas as pl
from jax.experimental.pallas import tpu as pltpu
from jax.sharding import PartitionSpec as P

F32 = jnp.float32
BF16 = jnp.bfloat16
LOW = -1e30
SCALE = 0.125
ROWS = 256
WIDTH = 512
TILE = 128
PAIRS = 4
SLOTS = 8
MATCH = 4
EDGES = 64
DOMAINS = 16
GROUPS = 16
VMEM_LIMIT = 63 * 2**20
HALF = WIDTH // 2
TAIL = 16
LINKS = (1, 3, 4, 12)
THIRD = (1, 3, 4, 12)
FOURTH = (3, 1, 12, 4)
A, B, FIRST, BITS = 0, 1, 2, 3
LIST = 2 * SLOTS

def dot(a, b, da=1, db=0):
    return lax.dot_general(a, b, (((da,), (db,)), ((), ())), preferred_element_type=F32)


def one_hot(near_col):
    e, r = near_col.shape[0], ROWS
    return lax.broadcasted_iota(jnp.int32, (e, r), 1) == near_col


def one_hot_t(near_row):
    e, r = near_row.shape[1], ROWS
    return lax.broadcasted_iota(jnp.int32, (r, e), 0) == near_row


def as_bf16(flags):
    return jnp.where(flags, 1.0, 0.0).astype(BF16)


def head_rows():
    s = lax.broadcasted_iota(jnp.int32, (16, WIDTH), 0)
    c = lax.broadcasted_iota(jnp.int32, (16, WIDTH), 1)
    return as_bf16((c >> 6) == 2 * (s & 7) + (s >> 3))


def halves(x):
    hi = x.astype(BF16)
    return hi, (x - hi.astype(F32)).astype(BF16)


def thirds(x):
    hi = x.astype(BF16)
    rest = x - hi.astype(F32)
    mid = rest.astype(BF16)
    return jnp.concatenate([hi, mid, (rest - mid.astype(F32)).astype(BF16)], axis=0)


def select_sum(x, matrix):
    y = dot(thirds(x), matrix)
    return y[0:16] + y[16:32] + y[32:48]


def to_blocks(x, a):
    lanes = slice(a * TILE, (a + 1) * TILE)
    return jnp.concatenate([x[0:8, lanes], x[8:16, lanes]], axis=1)


def from_blocks(x0, x1):
    even = jnp.concatenate([x0[:, :TILE], x1[:, :TILE]], axis=1)
    odd = jnp.concatenate([x0[:, TILE:], x1[:, TILE:]], axis=1)
    return jnp.concatenate([even, odd], axis=0)


def pick_kernel(near_ref, k_ref, v_ref, *outs):
    hot = as_bf16(one_hot(near_ref[...]))
    rows_k = dot(hot, k_ref[...]).astype(BF16)
    rows_v = dot(hot, v_ref[...]).astype(BF16)
    for m, out in enumerate(outs):
        part = slice(m * EDGES, (m + 1) * EDGES)
        out[:, :WIDTH] = rows_k[part]
        out[:, WIDTH:] = rows_v[part]


def pair_kernel(nc_ref, nr_ref, q_ref, k_ref, v_ref, g_ref, f0, f1, f2, f3, nq_ref, ng_ref, st_ref, top_ref):
    hot = one_hot(nc_ref[...])
    hot_b = as_bf16(hot)
    hot_t = as_bf16(one_hot_t(nr_ref[...]))
    heads = head_rows()
    qs = q_ref[...].astype(F32) * SCALE
    g = g_ref[...].astype(F32)

    far = jnp.concatenate([f0[...], f1[...], f2[...], f3[...]], axis=0).astype(F32)
    far_k, far_v = far[:, :WIDTH], far[:, WIDTH:]
    near_q = dot(hot_b, qs.astype(BF16))
    near_g = dot(hot_b, g_ref[...])
    nq_ref[...] = near_q.astype(BF16)
    ng_ref[...] = near_g.astype(BF16)

    def head_sum(x):
        hi, lo = halves(x)
        return dot(heads, hi, 1, 1) + dot(heads, lo, 1, 1)

    self_score = head_sum(qs * k_ref[...].astype(F32))
    self_drop = head_sum(g * v_ref[...].astype(F32))
    product = near_q * far_k
    hi, lo = halves(product)
    pair_score = dot(heads, hi, 1, 1) + dot(heads, lo, 1, 1)
    by_edge = dot(hi, heads, 1, 1) + dot(lo, heads, 1, 1)
    pair_drop = head_sum(near_g * far_v)
    top_ref[...] = self_score
    for s in (0, 1, 2, 3, 8, 9, 10, 11):
        best = jnp.max(jnp.where(hot, by_edge[:, s:s + 1], LOW), axis=0, keepdims=True)
        top_ref[s:s + 1, :] = jnp.maximum(top_ref[s:s + 1, :], best)
    top = top_ref[...]
    self_exp = jnp.exp(self_score - top)
    pair_exp = jnp.exp(pair_score - select_sum(top, hot_t))
    st_ref[0:16] = top
    st_ref[16:32] = self_exp + select_sum(pair_exp, hot_b)
    st_ref[32:48] = self_exp
    st_ref[48:64] = pair_exp
    st_ref[64:80] = self_drop
    st_ref[80:96] = pair_drop


def bit(info, row, link):
    return info[row, BITS + LINKS.index(link)]


def ring_index(info, row, part):
    low, high = ((4, 12), (1, 3))[part]
    return bit(info, row, low) + 2 * bit(info, row, high)


def split_kernel(me, tail_ref, k0, k1, k2, k3, v0, v1, v2, v3, ka, kb, va, vb, info_ref, tails, sem):
    copies = []
    for p, (sources, outs) in enumerate((((k0, k1, k2, k3), (ka, kb)), ((v0, v1, v2, v3), (va, vb)))):
        for i, source in enumerate(sources):
            for h, out in enumerate(outs):
                copies.append(pltpu.make_async_copy(
                    source.at[0:ROWS, h * HALF:(h + 1) * HALF], out.at[i], sem.at[p * 8 + i * 2 + h]))
    for i, source in enumerate((v1, v2, k1, k2)):
        copies.append(pltpu.make_async_copy(source.at[ROWS:ROWS + TAIL, 0:TILE], tails.at[i], sem.at[16 + i]))
    for copy in copies:
        copy.start()
    for copy in copies[16:]:
        copy.wait()
    lane = lax.broadcasted_iota(jnp.int32, (SLOTS, TILE), 1)
    for i in range(5):
        tail = tail_ref[:, 0:TILE] if i == 0 else tails[i - 1]
        tail = tail[0:SLOTS].astype(F32).astype(jnp.int32)
        block, owner, rows, count = (tail[:, c:c + 1] for c in range(4))
        place = owner * 2 + rows
        first = jnp.full((SLOTS, 1), SLOTS, jnp.int32)
        for t in range(SLOTS):
            first = jnp.minimum(first, jnp.where(place == place[t:t + 1], t, SLOTS))
        apart = owner ^ me[0, 0]
        x, y = apart >> 2, apart & 3
        columns = (block, rows, first, (y ^ (y >> 1)) & 1, y >> 1, (x ^ (x >> 1)) & 1, x >> 1)
        table = jnp.zeros((SLOTS, TILE), jnp.int32)
        for c, column in enumerate(columns):
            table = jnp.where(lane == c, column, table)
        info_ref[i * LIST:i * LIST + SLOTS] = table
        info_ref[i * LIST + SLOTS:(i + 1) * LIST] = jnp.where(lane == 0, count, 0)
    for copy in copies[:16]:
        copy.wait()


def pack_kernel(info, h0, h1, h2, h3, g0, g1, g2, g3, o0, o1, o2, o3, sem):
    held, got, outs = (h0, h1, h2, h3), (g0, g1, g2, g3), (o0, o1, o2, o3)

    def copies(act):
        for q in range(4):
            base = (1 + LINKS.index(FOURTH[q])) * LIST

            @pl.loop(0, info[base + SLOTS, 0])
            def _(t):
                row = base + t
                index = ring_index(info, row, q // 2)
                rows = pl.ds(pl.multiple_of(info[row, B] * TILE, TILE), TILE)
                here = bit(info, row, FOURTH[q]) == 0
                for other, source in enumerate((held[q], got[q])):
                    @pl.when(here & (bit(info, row, THIRD[q]) == other))
                    def _():
                        act(pltpu.make_async_copy(source.at[index, rows], outs[q].at[t], sem.at[q, t]))

    copies(lambda copy: copy.start())
    copies(lambda copy: copy.wait())


def tile_kernel(info, nc_ref, nr_ref, h0, h1, h2, h3, g0, g1, g2, g3, p0, p1, p2, p3,
                mask_ref, q_ref, g_ref, st_ref,
                s0, s1, s2, s3, out_ref, gq_ref, wd_ref,
                kb, vb, eb, mt, lt, ft, top2, sum2, del2, dk, dv,
                qs_ref, gs_ref, qt_ref, gt_ref, mask_buf, in_sem, mask_sem, ready):
    count = info[SLOTS, 0]
    held, got, packed = (h0, h1, h2, h3), (g0, g1, g2, g3), (p0, p1, p2, p3)

    def mask_copy(t):
        return pltpu.make_async_copy(mask_ref.at[t], mask_buf.at[t], mask_sem.at[t])

    def into(t, q):
        return (kb, kb, vb, vb)[q].at[t, :, pl.ds((q % 2) * HALF, HALF)]

    @pl.loop(0, count)
    def _(t):
        mask_copy(t).start()
        rows = pl.ds(pl.multiple_of(info[t, B] * TILE, TILE), TILE)
        for q in range(4):
            index = ring_index(info, t, q // 2)
            third, fourth = bit(info, t, THIRD[q]), bit(info, t, FOURTH[q])

            def fetch(source):
                pltpu.make_async_copy(source, into(t, q), in_sem.at[q, t]).start()

            @pl.when(fourth == 1)
            def _():
                fetch(packed[q].at[t])

            @pl.when((fourth == 0) & (third == 1))
            def _():
                fetch(got[q].at[index, rows])

            @pl.when((fourth == 0) & (third == 0))
            def _():
                fetch(held[q].at[index, rows])

    def arrived(t, part):
        for q in (2 * part, 2 * part + 1):
            pltpu.make_async_copy(packed[q].at[0], into(t, q), in_sem.at[q, t]).wait()

    ready()
    low_rows = lax.broadcasted_iota(jnp.int32, (TILE, TILE), 0) < 64
    low_lanes = lax.broadcasted_iota(jnp.int32, (TILE, TILE), 1) < 64
    qs = q_ref[...].astype(F32) * SCALE
    g = g_ref[...].astype(F32)
    for source, by_col, by_row in ((qs, qs_ref, qt_ref), (g, gs_ref, gt_ref)):
        for a in range(2):
            for p in range(PAIRS):
                x = source[a * TILE:(a + 1) * TILE, p * TILE:(p + 1) * TILE]
                xt = x.T
                by_col[a, p] = jnp.concatenate(
                    [jnp.where(low_rows, xt, 0.0), jnp.where(low_rows, 0.0, xt)], axis=1).astype(BF16)
                by_row[a, p] = jnp.concatenate(
                    [jnp.where(low_lanes, x, 0.0), jnp.where(low_lanes, 0.0, x)], axis=0).astype(BF16)

    top1, sum1 = st_ref[0:16], st_ref[16:32]
    self_exp, pair_exp = st_ref[32:48], st_ref[48:64]
    self_drop, pair_drop = st_ref[64:80], st_ref[80:96]
    hot_b = as_bf16(one_hot(nc_ref[...]))
    hot_t = as_bf16(one_hot_t(nr_ref[...]))
    for a in range(2):
        top2[a] = to_blocks(top1, a)

    @pl.loop(0, count)
    def _(t):
        a = info[t, 0]
        arrived(t, 0)
        mask_copy(t).wait()
        bias = jnp.where(mask_buf[t].astype(F32).T != 0, 0.0, LOW)
        bias = jnp.concatenate([bias, bias], axis=1)
        for p in range(PAIRS):
            s = dot(kb[t, :, p * TILE:(p + 1) * TILE], qs_ref[a, p]) + bias
            m = jnp.max(s, axis=0, keepdims=True)
            e = jnp.exp(s - m)
            eb[t, p] = e
            mt[t, p:p + 1] = m
            lt[t, p:p + 1] = jnp.sum(e, axis=0, keepdims=True)
        top2[a, 0:PAIRS] = jnp.maximum(top2[a, 0:PAIRS], mt[t, 0:PAIRS])

    for a in range(2):
        sum2[a] = to_blocks(sum1, a) * jnp.exp(to_blocks(top1, a) - top2[a])

    @pl.loop(0, count)
    def _(t):
        a = info[t, 0]
        shrink = jnp.exp(mt[t, 0:PAIRS] - top2[a, 0:PAIRS])
        ft[t, 0:PAIRS] = shrink
        sum2[a, 0:PAIRS] += lt[t, 0:PAIRS] * shrink

    @pl.loop(0, count)
    def _(t):
        a = info[t, 0]
        ft[t, 0:PAIRS] = ft[t, 0:PAIRS] / sum2[a, 0:PAIRS]

    factor = jnp.exp(top1 - from_blocks(top2[0], top2[1])) / from_blocks(sum2[0], sum2[1])
    self_w = self_exp * factor
    pair_w = pair_exp * select_sum(factor, hot_t)
    self_wb = self_w.astype(BF16).astype(F32)
    pair_wb = pair_w.astype(BF16).astype(F32)
    wd_ref[0:16] = self_wb
    wd_ref[16:32] = pair_wb
    delta = self_wb * self_drop + select_sum(pair_wb * pair_drop, hot_b)

    out_ref[...] = jnp.zeros_like(out_ref)
    gq_ref[...] = jnp.zeros_like(gq_ref)

    def add_term(acc, t, p, term):
        f = info[t, FIRST]
        cols = slice(p * TILE, (p + 1) * TILE)
        acc[f, :, cols] = jnp.where(f == t, 0.0, acc[f, :, cols]) + term

    @pl.loop(0, count)
    def _(t):
        a = info[t, 0]
        arrived(t, 1)
        for p in range(PAIRS):
            wb = (eb[t, p] * ft[t, p:p + 1]).astype(BF16)
            out_ref[a, p] += dot(vb[t, :, p * TILE:(p + 1) * TILE], wb, 0, 0)
            add_term(dv, t, p, dot(wb, gt_ref[a, p]))

    for a in range(2):
        base = to_blocks(delta, a)
        for p in range(PAIRS):
            del2[a, p:p + 1] = base[p:p + 1] + jnp.sum(
                gs_ref[a, p].astype(F32) * out_ref[a, p], axis=0, keepdims=True)
        del2[a, PAIRS:8] = jnp.zeros((8 - PAIRS, 2 * TILE), F32)
    delta = from_blocks(del2[0], del2[1])
    wd_ref[32:48] = self_w * (self_drop - delta)
    wd_ref[48:64] = pair_w * (pair_drop - select_sum(delta, hot_t))

    @pl.loop(0, count)
    def _(t):
        a = info[t, 0]
        for p in range(PAIRS):
            cols = slice(p * TILE, (p + 1) * TILE)
            drop = dot(vb[t, :, cols], gs_ref[a, p])
            ds = (eb[t, p] * ft[t, p:p + 1] * (drop - del2[a, p:p + 1])).astype(BF16)
            gq_ref[a, p] += dot(kb[t, :, cols], ds, 0, 0)
            add_term(dk, t, p, dot(ds, qt_ref[a, p]))

    @pl.loop(0, count)
    def _(t):
        @pl.when(info[t, FIRST] == t)
        def _():
            s0[t] = dk[t, :, 0:HALF].astype(BF16)
            s1[t] = dk[t, :, HALF:WIDTH].astype(BF16)
            s2[t] = dv[t, :, 0:HALF].astype(BF16)
            s3[t] = dv[t, :, HALF:WIDTH].astype(BF16)


def each_term(info, q, third, mine, theirs, add):
    for base, terms in ((0, mine), ((1 + LINKS.index(FOURTH[q])) * LIST, theirs)):
        @pl.loop(0, info[base + SLOTS, 0])
        def _(t):
            row = base + t

            @pl.when((info[row, FIRST] == t) & (bit(info, row, FOURTH[q]) == 0) & (bit(info, row, THIRD[q]) == third))
            def _():
                rows = pl.ds(pl.multiple_of(info[row, B] * TILE, TILE), TILE)
                add(ring_index(info, row, q // 2), rows, terms[t].astype(F32))


def second_kernel(info, m0, m1, m2, m3, g0, g1, g2, g3, o0, o1, o2, o3):
    for q, (mine, theirs, out) in enumerate(zip((m0, m1, m2, m3), (g0, g1, g2, g3), (o0, o1, o2, o3))):
        out[...] = jnp.zeros_like(out)

        def add(index, rows, term):
            out[index, rows] = (out[index, rows].astype(F32) + term).astype(BF16)

        each_term(info, q, 1, mine, theirs, add)


def third_kernel(info, m0, m1, m2, m3, g0, g1, g2, g3, n0, n1, n2, n3,
                 k1, k2, k3, v1, v2, v3, kk, kv, total):
    got = (n0, n1, n2, n3)
    for q, (mine, theirs) in enumerate(zip((m0, m1, m2, m3), (g0, g1, g2, g3))):
        total[q] = got[q][...].astype(F32)

        def add(index, rows, term):
            total[q, index, rows] += term

        each_term(info, q, 0, mine, theirs, add)
        cols = slice((q % 2) * HALF, (q % 2 + 1) * HALF)
        (kk, kv)[q // 2][:, cols] = total[q, 0]
        for i, out in enumerate(((k1, k2, k3), (v1, v2, v3))[q // 2]):
            out[:, cols] = total[q, i + 1].astype(BF16)


def rest_kernel(nr_ref, q_ref, k_ref, v_ref, g_ref, f0, f1, f2, f3, nq_ref, ng_ref, acc_ref, gacc_ref, wd_ref,
                out_ref, gq_ref, own_ref, b0, b1, b2, b3):
    hot_t = as_bf16(one_hot_t(nr_ref[...]))
    heads = head_rows()

    def expand(x):
        return dot(x.astype(BF16), heads, 0, 0)

    far = jnp.concatenate([f0[...], f1[...], f2[...], f3[...]], axis=0).astype(F32)
    self_wb, pair_wb = expand(wd_ref[0:16]), expand(wd_ref[16:32])
    self_ds, pair_ds = expand(wd_ref[32:48]), expand(wd_ref[48:64])
    back_k = (pair_ds * nq_ref[...].astype(F32)).astype(BF16)
    back_v = (pair_wb * ng_ref[...].astype(F32)).astype(BF16)
    for m, out in enumerate((b0, b1, b2, b3)):
        part = slice(m * EDGES, (m + 1) * EDGES)
        out[:, :WIDTH] = back_k[part]
        out[:, WIDTH:] = back_v[part]
    own_ref[0:ROWS] = self_ds * (q_ref[...].astype(F32) * SCALE)
    own_ref[ROWS:2 * ROWS] = self_wb * g_ref[...].astype(F32)

    def finish(own, pair, acc, scale, out):
        hi, lo = halves(pair)
        total = own + dot(hot_t, hi) + dot(hot_t, lo)
        for a in range(2):
            for p in range(PAIRS):
                x = acc[a, p]
                x = jnp.concatenate([x[0:64, :TILE], x[64:TILE, TILE:]], axis=0).T
                rows, cols = slice(a * TILE, (a + 1) * TILE), slice(p * TILE, (p + 1) * TILE)
                out[rows, cols] = ((total[rows, cols] + x) * scale).astype(BF16)

    finish(self_wb * v_ref[...].astype(F32), pair_wb * far[:, WIDTH:], acc_ref, 1.0, out_ref)
    finish(self_ds * k_ref[...].astype(F32), pair_ds * far[:, :WIDTH], gacc_ref, SCALE, gq_ref)


def last_kernel(nr_ref, kk, kv, k1, k2, k3, v1, v2, v3, own_ref, b0, b1, b2, b3, gk_ref, gv_ref):
    hot_t = as_bf16(one_hot_t(nr_ref[...]))
    back = jnp.concatenate([b0[...], b1[...], b2[...], b3[...]], axis=0)
    for part, (kept, terms, out) in enumerate(((kk, (k1, k2, k3), gk_ref), (kv, (v1, v2, v3), gv_ref))):
        total = kept[...] + own_ref[part * ROWS:(part + 1) * ROWS]
        for term in terms:
            total += term[...].astype(F32)
        out[...] = (total + dot(hot_t, back[:, part * WIDTH:(part + 1) * WIDTH])).astype(BF16)


def staged(kernel, scalars, raw, n_in, n_out, late):
    def run(*refs):
        *refs, sem = refs
        moved = [i for i in range(scalars, n_in) if i not in raw]
        ins, outs = list(refs[:n_in]), refs[n_in:n_in + n_out]
        buffers, scratch = refs[n_in + n_out:n_in + n_out + len(moved)], refs[n_in + n_out + len(moved):]
        copies = [pltpu.make_async_copy(ins[i], buf, sem.at[j]) for j, (i, buf) in enumerate(zip(moved, buffers))]
        for copy in copies:
            copy.start()
        for i, buf in zip(moved, buffers):
            ins[i] = buf

        def ready():
            for copy in copies:
                copy.wait()

        if late:
            kernel(*ins, *outs, *scratch, ready)
        else:
            ready()
            kernel(*ins, *outs, *scratch)
    return run


def call(kernel, outs, args, scalars=0, raw=(), scratch=(), cost=(1e8, 4e6), late=False, loose=()):
    smem, anywhere = pl.BlockSpec(memory_space=pltpu.SMEM), pl.BlockSpec(memory_space=pl.ANY)
    moved = [x for i, x in enumerate(args) if i >= scalars and i not in raw]
    return pl.pallas_call(
        staged(kernel, scalars, raw, len(args), len(outs), late),
        out_shape=[jax.ShapeDtypeStruct(s, d) for s, d in outs],
        in_specs=[smem] * scalars + [anywhere] * (len(args) - scalars),
        out_specs=[anywhere if i in loose else pl.BlockSpec(memory_space=pltpu.VMEM) for i in range(len(outs))],
        scratch_shapes=[pltpu.VMEM(x.shape, x.dtype) for x in moved] + list(scratch)
        + [pltpu.SemaphoreType.DMA((max(len(moved), 1),))],
        compiler_params=pltpu.CompilerParams(vmem_limit_bytes=VMEM_LIMIT),
        cost_estimate=pl.CostEstimate(flops=int(cost[0]), bytes_accessed=int(cost[1]), transcendentals=0),
    )(*args)


def over(block, link):
    return lax.ppermute(block, "dom", [(i, i ^ link) for i in range(DOMAINS)])


def to_group(code):
    pairs = [(i, i ^ code) for i in range(GROUPS)]
    return lambda block: lax.ppermute(block, "grp", pairs)


def chained(one, two):
    def run(x, y):
        x, y = lax.optimization_barrier((to_group(one)(x), y))
        return x, to_group(two)(y)

    return run


def first_exchange(blocks, codes):
    def route(code):
        return chained(GROUPS // 2, code)

    return lax.switch(codes[1] - 1, [route(code) for code in range(1, GROUPS)], *blocks)


def second_exchange(blocks, codes):
    routes = [to_group(code) for code in range(1, GROUPS)]
    return [lax.switch(codes[2 + m] - 1, routes, block) for m, block in enumerate(blocks)]


def ranked(rows, rank):
    return jnp.stack([sum(jnp.where(rank[m] == r, rows[m], 0) for m in range(MATCH)) for r in range(MATCH)])


def body(query, key, value, cotangent, tile_index, tile_mask, tile_count, partner, pair_edges):
    tied = lax.optimization_barrier
    node = ((ROWS, WIDTH), BF16)
    half = ((4, ROWS, HALF), BF16)
    slots = ((SLOTS, TILE, HALF), BF16)
    block = ((EDGES, 2 * WIDTH), BF16)

    tail = jnp.concatenate([tile_index[0], jnp.broadcast_to(tile_count[:, None], (SLOTS, 1))], axis=1)
    tail = jnp.pad(tail.astype(BF16), ((0, TAIL - SLOTS), (0, WIDTH - 4)))
    keys, values = (jnp.concatenate([x, tail], axis=0) for x in (key, value))
    ring_k = [over(keys, link) for link in (8, 4, 12)]
    ring_v = [over(values, link) for link in (2, 1, 3)]

    codes = jnp.bitwise_xor(partner[0] // DOMAINS, lax.axis_index("grp"))
    order = jnp.where(codes == GROUPS // 2, 0, codes)
    rank = jnp.sum((order[None, :] < order[:, None]).astype(jnp.int32), axis=1)
    codes = ranked(codes, rank)
    near = ranked(pair_edges[0, :, :, 0], rank).reshape(-1)
    near_col, near_row = near.reshape(-1, 1), near.reshape(1, -1)
    sent = call(pick_kernel, [block] * MATCH, (near_col, key, value))

    ring_k, ring_v, sent = tied((ring_k, ring_v, sent))

    me = lax.axis_index("dom").reshape(1, 1)
    *held, info = call(
        split_kernel, [half] * 4 + [((5 * LIST, TILE), jnp.int32)],
        (me, tail, keys, ring_k[1], ring_k[2], ring_k[0], values, ring_v[1], ring_v[2], ring_v[0]),
        scalars=1, raw=range(2, 10), loose=range(4),
        scratch=[pltpu.VMEM((4, TAIL, TILE), BF16), pltpu.SemaphoreType.DMA((20,))])
    held, info, sent = tied((held, info, sent))
    got = [over(x, link) for x, link in zip(held, THIRD)]
    far0, far1 = first_exchange(sent[:2], codes)
    got, far0, far1, later = tied((got, far0, far1, sent[2:]))
    packs = call(
        pack_kernel, [slots] * 4, (info, *held, *got), scalars=1, raw=range(1, 9), loose=range(4),
        scratch=[pltpu.SemaphoreType.DMA((4, SLOTS))])
    packs, later = tied((packs, later))
    packed = [over(x, link) for x, link in zip(packs, FOURTH)]
    far = [far0, far1, *second_exchange(later, codes)]
    near_q, near_g, stats = call(
        pair_kernel, [node, node, ((96, ROWS), F32)], (near_col, near_row, query, key, value, cotangent, *far),
        scratch=[pltpu.VMEM((16, ROWS), F32)])

    acc = ((2, PAIRS, TILE, 2 * TILE), F32)
    row_stat = pltpu.VMEM((SLOTS, 8, 2 * TILE), F32)
    block_stat = pltpu.VMEM((2, 8, 2 * TILE), F32)
    by_col = pltpu.VMEM((2, PAIRS, TILE, 2 * TILE), BF16)
    by_row = pltpu.VMEM((2, PAIRS, 2 * TILE, TILE), BF16)
    tiles_b = pltpu.VMEM((SLOTS, TILE, WIDTH), BF16)
    tiles_f = pltpu.VMEM((SLOTS, TILE, WIDTH), F32)
    *terms, out_acc, gq_acc, grads = call(
        tile_kernel,
        [slots] * 4 + [acc, acc, ((64, ROWS), F32)],
        (info, near_col, near_row, *held, *got, *packed, tile_mask[0], query, cotangent, stats),
        scalars=1, raw=range(3, 16), cost=(1e9, 2e7), late=True,
        scratch=[
            tiles_b, tiles_b, pltpu.VMEM((SLOTS, PAIRS, TILE, 2 * TILE), F32),
            row_stat, row_stat, row_stat, block_stat, block_stat, block_stat,
            tiles_f, tiles_f,
            by_col, by_col, by_row, by_row, pltpu.VMEM((SLOTS, TILE, TILE), jnp.int32),
            pltpu.SemaphoreType.DMA((4, SLOTS)), pltpu.SemaphoreType.DMA((SLOTS,)),
        ],
    )

    theirs = [over(x, link) for x, link in zip(terms, FOURTH)]
    attended, grad_query, own, *back = call(
        rest_kernel,
        [node, node, ((2 * ROWS, WIDTH), F32)] + [block] * MATCH,
        (near_row, query, key, value, cotangent, *far, near_q, near_g, out_acc, gq_acc, grads))
    back2, back3 = second_exchange(back[2:], codes)
    theirs, back2, back3, back = tied((theirs, back2, back3, back[:2]))
    sums = call(second_kernel, [half] * 4, (info, *terms, *theirs), scalars=1)
    sums, back = tied((sums, back))
    more = [over(x, link) for x, link in zip(sums, THIRD)]
    back0, back1 = first_exchange(back, codes)
    more, back0, back1 = tied((more, back0, back1))
    *ring, kept_k, kept_v = call(
        third_kernel, [node] * 6 + [((ROWS, WIDTH), F32)] * 2, (info, *terms, *theirs, *more), scalars=1,
        scratch=[pltpu.VMEM((4, 4, ROWS, HALF), F32)])
    order = ((2, 8), (5, 2), (0, 4), (3, 1), (1, 12), (4, 3))
    arrived = {i: over(ring[i], link) for i, link in order}
    grad_key, grad_value = call(
        last_kernel, [node, node],
        (near_row, kept_k, kept_v, *(arrived[i] for i in range(6)), own, back0, back1, back2, back3))
    return attended, grad_query, grad_key, grad_value


def solution(mesh):
    rows = P(("grp", "dom"), None)
    return jax.shard_map(
        body,
        mesh=mesh,
        in_specs=(
            rows, rows, rows, rows,
            P(("grp", "dom"), None, None),
            P(("grp", "dom"), None, None, None),
            P(("grp", "dom")),
            rows,
            P(("grp", "dom"), None, None, None),
        ),
        out_specs=(rows, rows, rows, rows),
        check_vma=False,
    )
```

```python
import jax
import jax.numpy as jnp
from jax import lax
from jax.experimental import pallas as pl
from jax.experimental.pallas import tpu as pltpu
from jax.sharding import PartitionSpec as P

F32 = jnp.float32
BF16 = jnp.bfloat16
LOW = -1e30
SCALE = 0.125
ROWS = 256
WIDTH = 512
TILE = 128
PAIRS = 4
SLOTS = 8
MATCH = 4
EDGES = 64
DOMAINS = 16
GROUPS = 16
VMEM_LIMIT = 50 * 2**20
WHOLE_VMEM = 63 * 2**20
HALF = WIDTH // 2
TAIL = 16
LINKS = (1, 3, 4, 12)
THIRD = (1, 3, 4, 12)
FOURTH = (3, 1, 12, 4)
A, B, FIRST, BITS = 0, 1, 2, 3
LIST = 2 * SLOTS

def dot(a, b, da=1, db=0):
    return lax.dot_general(a, b, (((da,), (db,)), ((), ())), preferred_element_type=F32)


def one_hot(near_col):
    e, r = near_col.shape[0], ROWS
    return lax.broadcasted_iota(jnp.int32, (e, r), 1) == near_col


def one_hot_t(near_row):
    e, r = near_row.shape[1], ROWS
    return lax.broadcasted_iota(jnp.int32, (r, e), 0) == near_row


def as_bf16(flags):
    return jnp.where(flags, 1.0, 0.0).astype(BF16)


def head_rows():
    s = lax.broadcasted_iota(jnp.int32, (16, WIDTH), 0)
    c = lax.broadcasted_iota(jnp.int32, (16, WIDTH), 1)
    return as_bf16((c >> 6) == 2 * (s & 7) + (s >> 3))


def halves(x):
    hi = x.astype(BF16)
    return hi, (x - hi.astype(F32)).astype(BF16)


def thirds(x):
    hi = x.astype(BF16)
    rest = x - hi.astype(F32)
    mid = rest.astype(BF16)
    return jnp.concatenate([hi, mid, (rest - mid.astype(F32)).astype(BF16)], axis=0)


def select_sum(x, matrix):
    y = dot(thirds(x), matrix)
    return y[0:16] + y[16:32] + y[32:48]


def to_blocks(x, a):
    lanes = slice(a * TILE, (a + 1) * TILE)
    return jnp.concatenate([x[0:8, lanes], x[8:16, lanes]], axis=1)


def from_blocks(x0, x1):
    even = jnp.concatenate([x0[:, :TILE], x1[:, :TILE]], axis=1)
    odd = jnp.concatenate([x0[:, TILE:], x1[:, TILE:]], axis=1)
    return jnp.concatenate([even, odd], axis=0)


def pick_kernel(near_ref, k_ref, v_ref, *outs):
    hot = as_bf16(one_hot(near_ref[...]))
    rows_k = dot(hot, k_ref[...]).astype(BF16)
    rows_v = dot(hot, v_ref[...]).astype(BF16)
    for m, out in enumerate(outs):
        part = slice(m * EDGES, (m + 1) * EDGES)
        out[:, :WIDTH] = rows_k[part]
        out[:, WIDTH:] = rows_v[part]


def pair_kernel(nc_ref, nr_ref, q_ref, k_ref, v_ref, g_ref, f0, f1, f2, f3, nq_ref, ng_ref, st_ref, top_ref):
    hot = one_hot(nc_ref[...])
    hot_b = as_bf16(hot)
    hot_t = as_bf16(one_hot_t(nr_ref[...]))
    heads = head_rows()
    qs = q_ref[...].astype(F32) * SCALE
    g = g_ref[...].astype(F32)

    far = jnp.concatenate([f0[...], f1[...], f2[...], f3[...]], axis=0).astype(F32)
    far_k, far_v = far[:, :WIDTH], far[:, WIDTH:]
    near_q = dot(hot_b, qs.astype(BF16))
    near_g = dot(hot_b, g_ref[...])
    nq_ref[...] = near_q.astype(BF16)
    ng_ref[...] = near_g.astype(BF16)

    def head_sum(x):
        hi, lo = halves(x)
        return dot(heads, hi, 1, 1) + dot(heads, lo, 1, 1)

    self_score = head_sum(qs * k_ref[...].astype(F32))
    self_drop = head_sum(g * v_ref[...].astype(F32))
    product = near_q * far_k
    hi, lo = halves(product)
    pair_score = dot(heads, hi, 1, 1) + dot(heads, lo, 1, 1)
    by_edge = dot(hi, heads, 1, 1) + dot(lo, heads, 1, 1)
    pair_drop = head_sum(near_g * far_v)
    top_ref[...] = self_score
    for s in (0, 1, 2, 3, 8, 9, 10, 11):
        best = jnp.max(jnp.where(hot, by_edge[:, s:s + 1], LOW), axis=0, keepdims=True)
        top_ref[s:s + 1, :] = jnp.maximum(top_ref[s:s + 1, :], best)
    top = top_ref[...]
    self_exp = jnp.exp(self_score - top)
    pair_exp = jnp.exp(pair_score - select_sum(top, hot_t))
    st_ref[0:16] = top
    st_ref[16:32] = self_exp + select_sum(pair_exp, hot_b)
    st_ref[32:48] = self_exp
    st_ref[48:64] = pair_exp
    st_ref[64:80] = self_drop
    st_ref[80:96] = pair_drop


def bit(info, row, link):
    return info[row, BITS + LINKS.index(link)]


def ring_index(info, row, part):
    low, high = ((4, 12), (1, 3))[part]
    return bit(info, row, low) + 2 * bit(info, row, high)


def split_kernel(me, tail_ref, k0, k1, k2, k3, v0, v1, v2, v3, ka, kb, va, vb, info_ref, tails, sem):
    copies = []
    for p, (sources, outs) in enumerate((((k0, k1, k2, k3), (ka, kb)), ((v0, v1, v2, v3), (va, vb)))):
        for i, source in enumerate(sources):
            for h, out in enumerate(outs):
                copies.append(pltpu.make_async_copy(
                    source.at[0:ROWS, h * HALF:(h + 1) * HALF], out.at[i], sem.at[p * 8 + i * 2 + h]))
    for i, source in enumerate((v1, v2, k1, k2)):
        copies.append(pltpu.make_async_copy(source.at[ROWS:ROWS + TAIL, 0:TILE], tails.at[i], sem.at[16 + i]))
    for copy in copies:
        copy.start()
    for copy in copies[16:]:
        copy.wait()
    lane = lax.broadcasted_iota(jnp.int32, (SLOTS, TILE), 1)
    for i in range(5):
        tail = tail_ref[:, 0:TILE] if i == 0 else tails[i - 1]
        tail = tail[0:SLOTS].astype(F32).astype(jnp.int32)
        block, owner, rows, count = (tail[:, c:c + 1] for c in range(4))
        place = owner * 2 + rows
        first = jnp.full((SLOTS, 1), SLOTS, jnp.int32)
        for t in range(SLOTS):
            first = jnp.minimum(first, jnp.where(place == place[t:t + 1], t, SLOTS))
        apart = owner ^ me[0, 0]
        x, y = apart >> 2, apart & 3
        columns = (block, rows, first, (y ^ (y >> 1)) & 1, y >> 1, (x ^ (x >> 1)) & 1, x >> 1)
        table = jnp.zeros((SLOTS, TILE), jnp.int32)
        for c, column in enumerate(columns):
            table = jnp.where(lane == c, column, table)
        info_ref[i * LIST:i * LIST + SLOTS] = table
        info_ref[i * LIST + SLOTS:(i + 1) * LIST] = jnp.where(lane == 0, count, 0)
    for copy in copies[:16]:
        copy.wait()


def pack_kernel(info, h0, h1, h2, h3, g0, g1, g2, g3, o0, o1, o2, o3, sem):
    held, got, outs = (h0, h1, h2, h3), (g0, g1, g2, g3), (o0, o1, o2, o3)

    def copies(act):
        for q in range(4):
            base = (1 + LINKS.index(FOURTH[q])) * LIST

            @pl.loop(0, info[base + SLOTS, 0])
            def _(t):
                row = base + t
                index = ring_index(info, row, q // 2)
                rows = pl.ds(pl.multiple_of(info[row, B] * TILE, TILE), TILE)
                here = bit(info, row, FOURTH[q]) == 0
                for other, source in enumerate((held[q], got[q])):
                    @pl.when(here & (bit(info, row, THIRD[q]) == other))
                    def _():
                        act(pltpu.make_async_copy(source.at[index, rows], outs[q].at[t], sem.at[q, t]))

    copies(lambda copy: copy.start())
    copies(lambda copy: copy.wait())


def tile_kernel(info, nc_ref, nr_ref, h0, h1, h2, h3, g0, g1, g2, g3, p0, p1, p2, p3,
                mask_ref, q_ref, g_ref, st_ref,
                s0, s1, s2, s3, out_ref, gq_ref, wd_ref,
                kb, vb, eb, mt, lt, ft, top2, sum2, del2, dk, dv,
                qs_ref, gs_ref, qt_ref, gt_ref, mask_buf, in_sem, mask_sem, ready):
    count = info[SLOTS, 0]
    held, got, packed = (h0, h1, h2, h3), (g0, g1, g2, g3), (p0, p1, p2, p3)

    def mask_copy(t):
        return pltpu.make_async_copy(mask_ref.at[t], mask_buf.at[t], mask_sem.at[t])

    def into(t, q):
        return (kb, kb, vb, vb)[q].at[t, :, pl.ds((q % 2) * HALF, HALF)]

    @pl.loop(0, count)
    def _(t):
        mask_copy(t).start()
        rows = pl.ds(pl.multiple_of(info[t, B] * TILE, TILE), TILE)
        for q in range(4):
            index = ring_index(info, t, q // 2)
            third, fourth = bit(info, t, THIRD[q]), bit(info, t, FOURTH[q])

            def fetch(source):
                pltpu.make_async_copy(source, into(t, q), in_sem.at[q, t]).start()

            @pl.when(fourth == 1)
            def _():
                fetch(packed[q].at[t])

            @pl.when((fourth == 0) & (third == 1))
            def _():
                fetch(got[q].at[index, rows])

            @pl.when((fourth == 0) & (third == 0))
            def _():
                fetch(held[q].at[index, rows])

    def arrived(t, part):
        for q in (2 * part, 2 * part + 1):
            pltpu.make_async_copy(packed[q].at[0], into(t, q), in_sem.at[q, t]).wait()

    ready()
    low_rows = lax.broadcasted_iota(jnp.int32, (TILE, TILE), 0) < 64
    low_lanes = lax.broadcasted_iota(jnp.int32, (TILE, TILE), 1) < 64
    qs = q_ref[...].astype(F32) * SCALE
    g = g_ref[...].astype(F32)
    for source, by_col, by_row in ((qs, qs_ref, qt_ref), (g, gs_ref, gt_ref)):
        for a in range(2):
            for p in range(PAIRS):
                x = source[a * TILE:(a + 1) * TILE, p * TILE:(p + 1) * TILE]
                xt = x.T
                by_col[a, p] = jnp.concatenate(
                    [jnp.where(low_rows, xt, 0.0), jnp.where(low_rows, 0.0, xt)], axis=1).astype(BF16)
                by_row[a, p] = jnp.concatenate(
                    [jnp.where(low_lanes, x, 0.0), jnp.where(low_lanes, 0.0, x)], axis=0).astype(BF16)

    top1, sum1 = st_ref[0:16], st_ref[16:32]
    self_exp, pair_exp = st_ref[32:48], st_ref[48:64]
    self_drop, pair_drop = st_ref[64:80], st_ref[80:96]
    hot_b = as_bf16(one_hot(nc_ref[...]))
    hot_t = as_bf16(one_hot_t(nr_ref[...]))
    for a in range(2):
        top2[a] = to_blocks(top1, a)

    @pl.loop(0, count)
    def _(t):
        a = info[t, 0]
        arrived(t, 0)
        mask_copy(t).wait()
        bias = jnp.where(mask_buf[t].astype(F32).T != 0, 0.0, LOW)
        bias = jnp.concatenate([bias, bias], axis=1)
        for p in range(PAIRS):
            s = dot(kb[t, :, p * TILE:(p + 1) * TILE], qs_ref[a, p]) + bias
            m = jnp.max(s, axis=0, keepdims=True)
            e = jnp.exp(s - m)
            eb[t, p] = e
            mt[t, p:p + 1] = m
            lt[t, p:p + 1] = jnp.sum(e, axis=0, keepdims=True)
        top2[a, 0:PAIRS] = jnp.maximum(top2[a, 0:PAIRS], mt[t, 0:PAIRS])

    for a in range(2):
        sum2[a] = to_blocks(sum1, a) * jnp.exp(to_blocks(top1, a) - top2[a])

    @pl.loop(0, count)
    def _(t):
        a = info[t, 0]
        shrink = jnp.exp(mt[t, 0:PAIRS] - top2[a, 0:PAIRS])
        ft[t, 0:PAIRS] = shrink
        sum2[a, 0:PAIRS] += lt[t, 0:PAIRS] * shrink

    @pl.loop(0, count)
    def _(t):
        a = info[t, 0]
        ft[t, 0:PAIRS] = ft[t, 0:PAIRS] / sum2[a, 0:PAIRS]

    factor = jnp.exp(top1 - from_blocks(top2[0], top2[1])) / from_blocks(sum2[0], sum2[1])
    self_w = self_exp * factor
    pair_w = pair_exp * select_sum(factor, hot_t)
    self_wb = self_w.astype(BF16).astype(F32)
    pair_wb = pair_w.astype(BF16).astype(F32)
    wd_ref[0:16] = self_wb
    wd_ref[16:32] = pair_wb
    delta = self_wb * self_drop + select_sum(pair_wb * pair_drop, hot_b)

    out_ref[...] = jnp.zeros_like(out_ref)
    gq_ref[...] = jnp.zeros_like(gq_ref)

    def add_term(acc, t, p, term):
        f = info[t, FIRST]
        cols = slice(p * TILE, (p + 1) * TILE)
        acc[f, :, cols] = jnp.where(f == t, 0.0, acc[f, :, cols]) + term

    @pl.loop(0, count)
    def _(t):
        a = info[t, 0]
        arrived(t, 1)
        for p in range(PAIRS):
            wb = (eb[t, p] * ft[t, p:p + 1]).astype(BF16)
            out_ref[a, p] += dot(vb[t, :, p * TILE:(p + 1) * TILE], wb, 0, 0)
            add_term(dv, t, p, dot(wb, gt_ref[a, p]))

    for a in range(2):
        base = to_blocks(delta, a)
        for p in range(PAIRS):
            del2[a, p:p + 1] = base[p:p + 1] + jnp.sum(
                gs_ref[a, p].astype(F32) * out_ref[a, p], axis=0, keepdims=True)
        del2[a, PAIRS:8] = jnp.zeros((8 - PAIRS, 2 * TILE), F32)
    delta = from_blocks(del2[0], del2[1])
    wd_ref[32:48] = self_w * (self_drop - delta)
    wd_ref[48:64] = pair_w * (pair_drop - select_sum(delta, hot_t))

    @pl.loop(0, count)
    def _(t):
        a = info[t, 0]
        for p in range(PAIRS):
            cols = slice(p * TILE, (p + 1) * TILE)
            drop = dot(vb[t, :, cols], gs_ref[a, p])
            ds = (eb[t, p] * ft[t, p:p + 1] * (drop - del2[a, p:p + 1])).astype(BF16)
            gq_ref[a, p] += dot(kb[t, :, cols], ds, 0, 0)
            add_term(dk, t, p, dot(ds, qt_ref[a, p]))

    @pl.loop(0, count)
    def _(t):
        @pl.when(info[t, FIRST] == t)
        def _():
            s0[t] = dk[t, :, 0:HALF].astype(BF16)
            s1[t] = dk[t, :, HALF:WIDTH].astype(BF16)
            s2[t] = dv[t, :, 0:HALF].astype(BF16)
            s3[t] = dv[t, :, HALF:WIDTH].astype(BF16)


def each_term(info, q, third, mine, theirs, add):
    for base, terms in ((0, mine), ((1 + LINKS.index(FOURTH[q])) * LIST, theirs)):
        @pl.loop(0, info[base + SLOTS, 0])
        def _(t):
            row = base + t

            @pl.when((info[row, FIRST] == t) & (bit(info, row, FOURTH[q]) == 0) & (bit(info, row, THIRD[q]) == third))
            def _():
                rows = pl.ds(pl.multiple_of(info[row, B] * TILE, TILE), TILE)
                add(ring_index(info, row, q // 2), rows, terms[t].astype(F32))


def second_kernel(info, m0, m1, m2, m3, g0, g1, g2, g3, o0, o1, o2, o3):
    for q, (mine, theirs, out) in enumerate(zip((m0, m1, m2, m3), (g0, g1, g2, g3), (o0, o1, o2, o3))):
        out[...] = jnp.zeros_like(out)

        def add(index, rows, term):
            out[index, rows] = (out[index, rows].astype(F32) + term).astype(BF16)

        each_term(info, q, 1, mine, theirs, add)


def third_kernel(info, m0, m1, m2, m3, g0, g1, g2, g3, n0, n1, n2, n3,
                 k1, k2, k3, v1, v2, v3, kk, kv, total):
    got = (n0, n1, n2, n3)
    for q, (mine, theirs) in enumerate(zip((m0, m1, m2, m3), (g0, g1, g2, g3))):
        total[q] = got[q][...].astype(F32)

        def add(index, rows, term):
            total[q, index, rows] += term

        each_term(info, q, 0, mine, theirs, add)
        cols = slice((q % 2) * HALF, (q % 2 + 1) * HALF)
        (kk, kv)[q // 2][:, cols] = total[q, 0]
        for i, out in enumerate(((k1, k2, k3), (v1, v2, v3))[q // 2]):
            out[:, cols] = total[q, i + 1].astype(BF16)


def rest_kernel(nr_ref, q_ref, k_ref, v_ref, g_ref, f0, f1, f2, f3, nq_ref, ng_ref, acc_ref, gacc_ref, wd_ref,
                out_ref, gq_ref, own_ref, b0, b1, b2, b3):
    hot_t = as_bf16(one_hot_t(nr_ref[...]))
    heads = head_rows()

    def expand(x):
        return dot(x.astype(BF16), heads, 0, 0)

    far = jnp.concatenate([f0[...], f1[...], f2[...], f3[...]], axis=0).astype(F32)
    self_wb, pair_wb = expand(wd_ref[0:16]), expand(wd_ref[16:32])
    self_ds, pair_ds = expand(wd_ref[32:48]), expand(wd_ref[48:64])
    back_k = (pair_ds * nq_ref[...].astype(F32)).astype(BF16)
    back_v = (pair_wb * ng_ref[...].astype(F32)).astype(BF16)
    for m, out in enumerate((b0, b1, b2, b3)):
        part = slice(m * EDGES, (m + 1) * EDGES)
        out[:, :WIDTH] = back_k[part]
        out[:, WIDTH:] = back_v[part]
    own_ref[0:ROWS] = self_ds * (q_ref[...].astype(F32) * SCALE)
    own_ref[ROWS:2 * ROWS] = self_wb * g_ref[...].astype(F32)

    def finish(own, pair, acc, scale, out):
        hi, lo = halves(pair)
        total = own + dot(hot_t, hi) + dot(hot_t, lo)
        for a in range(2):
            for p in range(PAIRS):
                x = acc[a, p]
                x = jnp.concatenate([x[0:64, :TILE], x[64:TILE, TILE:]], axis=0).T
                rows, cols = slice(a * TILE, (a + 1) * TILE), slice(p * TILE, (p + 1) * TILE)
                out[rows, cols] = ((total[rows, cols] + x) * scale).astype(BF16)

    finish(self_wb * v_ref[...].astype(F32), pair_wb * far[:, WIDTH:], acc_ref, 1.0, out_ref)
    finish(self_ds * k_ref[...].astype(F32), pair_ds * far[:, :WIDTH], gacc_ref, SCALE, gq_ref)


def last_kernel(nr_ref, kk, kv, k1, k2, k3, v1, v2, v3, own_ref, b0, b1, b2, b3, gk_ref, gv_ref):
    hot_t = as_bf16(one_hot_t(nr_ref[...]))
    back = jnp.concatenate([b0[...], b1[...], b2[...], b3[...]], axis=0)
    for part, (kept, terms, out) in enumerate(((kk, (k1, k2, k3), gk_ref), (kv, (v1, v2, v3), gv_ref))):
        total = kept[...] + own_ref[part * ROWS:(part + 1) * ROWS]
        for term in terms:
            total += term[...].astype(F32)
        out[...] = (total + dot(hot_t, back[:, part * WIDTH:(part + 1) * WIDTH])).astype(BF16)


def staged(kernel, scalars, raw, n_in, n_out, late):
    def run(*refs):
        *refs, sem = refs
        moved = [i for i in range(scalars, n_in) if i not in raw]
        ins, outs = list(refs[:n_in]), refs[n_in:n_in + n_out]
        buffers, scratch = refs[n_in + n_out:n_in + n_out + len(moved)], refs[n_in + n_out + len(moved):]
        copies = [pltpu.make_async_copy(ins[i], buf, sem.at[j]) for j, (i, buf) in enumerate(zip(moved, buffers))]
        for copy in copies:
            copy.start()
        for i, buf in zip(moved, buffers):
            ins[i] = buf

        def ready():
            for copy in copies:
                copy.wait()

        if late:
            kernel(*ins, *outs, *scratch, ready)
        else:
            ready()
            kernel(*ins, *outs, *scratch)
    return run


def call(kernel, outs, args, scalars=0, raw=(), scratch=(), cost=(1e8, 4e6), late=False, loose=(), limit=VMEM_LIMIT):
    smem, anywhere = pl.BlockSpec(memory_space=pltpu.SMEM), pl.BlockSpec(memory_space=pl.ANY)
    moved = [x for i, x in enumerate(args) if i >= scalars and i not in raw]
    return pl.pallas_call(
        staged(kernel, scalars, raw, len(args), len(outs), late),
        out_shape=[jax.ShapeDtypeStruct(s, d) for s, d in outs],
        in_specs=[smem if i < scalars else anywhere for i in range(len(args))],
        out_specs=[anywhere if i in loose else pl.BlockSpec(memory_space=pltpu.VMEM) for i in range(len(outs))],
        scratch_shapes=[pltpu.VMEM(x.shape, x.dtype) for x in moved] + list(scratch)
        + [pltpu.SemaphoreType.DMA((max(len(moved), 1),))],
        compiler_params=pltpu.CompilerParams(vmem_limit_bytes=limit),
        cost_estimate=pl.CostEstimate(flops=int(cost[0]), bytes_accessed=int(cost[1]), transcendentals=0),
    )(*args)


def over(block, link):
    return lax.ppermute(block, "dom", [(i, i ^ link) for i in range(DOMAINS)])


def to_group(code):
    pairs = [(i, i ^ code) for i in range(GROUPS)]
    return lambda block: lax.ppermute(block, "grp", pairs)


def switched(block, code):
    return lax.switch(code - 1, [to_group(c) for c in range(1, GROUPS)], block)


def halfway_first(rows, at):
    return jnp.stack([
        sum(jnp.where(at == m, rows[m], 0) for m in range(MATCH)),
        *(jnp.where(m - 1 < at, rows[m - 1], rows[m]) for m in range(1, MATCH)),
    ])


def body(query, key, value, cotangent, tile_index, tile_mask, tile_count, partner, pair_edges):
    tied = lax.optimization_barrier
    node = ((ROWS, WIDTH), BF16)
    half = ((4, ROWS, HALF), BF16)
    slots = ((SLOTS, TILE, HALF), BF16)
    block = ((EDGES, 2 * WIDTH), BF16)

    tail = jnp.concatenate([tile_index[0], jnp.broadcast_to(tile_count[:, None], (SLOTS, 1))], axis=1)
    tail = jnp.pad(tail.astype(BF16), ((0, TAIL - SLOTS), (0, WIDTH - 4)))
    keys, values = (jnp.concatenate([x, tail], axis=0) for x in (key, value))
    ring_k = [over(keys, link) for link in (8, 4, 12)]
    ring_v = [over(values, link) for link in (2, 1, 3)]

    codes = jnp.bitwise_xor(partner[0] // DOMAINS, lax.axis_index("grp"))
    slot4 = jnp.arange(MATCH, dtype=jnp.int32)
    at = jnp.sum(jnp.where(codes == GROUPS // 2, slot4, 0))
    codes = halfway_first(codes, at)
    near = halfway_first(pair_edges[0, :, :, 0], at).reshape(-1)
    near_col, near_row = near.reshape(-1, 1), near.reshape(1, -1)
    sent = call(pick_kernel, [block] * MATCH, (near_col, key, value), limit=WHOLE_VMEM)

    far0 = to_group(GROUPS // 2)(sent[0])

    me = lax.axis_index("dom").reshape(1, 1)
    *held, info = call(
        split_kernel, [half] * 4 + [((5 * LIST, TILE), jnp.int32)],
        (me, tail, keys, ring_k[1], ring_k[2], ring_k[0], values, ring_v[1], ring_v[2], ring_v[0]),
        scalars=1, raw=range(2, 10), limit=WHOLE_VMEM,
        scratch=[pltpu.VMEM((4, TAIL, TILE), BF16), pltpu.SemaphoreType.DMA((20,))])
    held, info, sent, far0 = tied((held, info, sent, far0))
    got = [over(x, link) for x, link in zip(held, THIRD)]
    far1 = switched(sent[1], codes[1])
    got, far1, sent2, sent3 = tied((got, far1, sent[2], sent[3]))
    packs = call(
        pack_kernel, [slots] * 4, (info, *held, *got), scalars=1, raw=range(1, 9),
        scratch=[pltpu.SemaphoreType.DMA((4, SLOTS))])
    packs, sent2, sent3 = tied((packs, sent2, sent3))
    packed = [over(x, link) for x, link in zip(packs, FOURTH)]
    far = [far0, far1, switched(sent2, codes[2]), switched(sent3, codes[3])]
    near_q, near_g, stats = call(
        pair_kernel, [node, node, ((96, ROWS), F32)], (near_col, near_row, query, key, value, cotangent, *far),
        scratch=[pltpu.VMEM((16, ROWS), F32)])

    acc = ((2, PAIRS, TILE, 2 * TILE), F32)
    row_stat = pltpu.VMEM((SLOTS, 8, 2 * TILE), F32)
    block_stat = pltpu.VMEM((2, 8, 2 * TILE), F32)
    by_col = pltpu.VMEM((2, PAIRS, TILE, 2 * TILE), BF16)
    by_row = pltpu.VMEM((2, PAIRS, 2 * TILE, TILE), BF16)
    tiles_b = pltpu.VMEM((SLOTS, TILE, WIDTH), BF16)
    tiles_f = pltpu.VMEM((SLOTS, TILE, WIDTH), F32)
    *terms, out_acc, gq_acc, grads = call(
        tile_kernel,
        [slots] * 4 + [acc, acc, ((64, ROWS), F32)],
        (info, near_col, near_row, *held, *got, *packed, tile_mask[0], query, cotangent, stats),
        scalars=1, raw=range(3, 16), cost=(1e9, 2e7), late=True,
        scratch=[
            tiles_b, tiles_b, pltpu.VMEM((SLOTS, PAIRS, TILE, 2 * TILE), F32),
            row_stat, row_stat, row_stat, block_stat, block_stat, block_stat,
            tiles_f, tiles_f,
            by_col, by_col, by_row, by_row, pltpu.VMEM((SLOTS, TILE, TILE), jnp.int32),
            pltpu.SemaphoreType.DMA((4, SLOTS)), pltpu.SemaphoreType.DMA((SLOTS,)),
        ],
    )

    theirs = [over(x, link) for x, link in zip(terms, FOURTH)]
    attended, grad_query, own, *back = call(
        rest_kernel,
        [node, node, ((2 * ROWS, WIDTH), F32)] + [block] * MATCH,
        (near_row, query, key, value, cotangent, *far, near_q, near_g, out_acc, gq_acc, grads))
    back0 = to_group(GROUPS // 2)(back[0])
    back1, back2 = switched(back[1], codes[1]), switched(back[2], codes[2])
    theirs, back1, back2, back3 = tied((theirs, back1, back2, back[3]))
    sums = call(second_kernel, [half] * 4, (info, *terms, *theirs), scalars=1)
    sums, back3 = tied((sums, back3))
    more = [over(x, link) for x, link in zip(sums, THIRD)]
    back3 = switched(back3, codes[3])
    more, back3 = tied((more, back3))
    *ring, kept_k, kept_v = call(
        third_kernel, [node] * 6 + [((ROWS, WIDTH), F32)] * 2, (info, *terms, *theirs, *more), scalars=1,
        scratch=[pltpu.VMEM((4, 4, ROWS, HALF), F32)])
    ring, back0 = tied((ring, back0))
    order = ((2, 8), (5, 2), (0, 4), (3, 1), (1, 12), (4, 3))
    arrived = {i: over(ring[i], link) for i, link in order}
    grad_key, grad_value = call(
        last_kernel, [node, node],
        (near_row, kept_k, kept_v, *(arrived[i] for i in range(6)), own, back0, back1, back2, back3))
    return attended, grad_query, grad_key, grad_value


def solution(mesh):
    rows = P(("grp", "dom"), None)
    return jax.shard_map(
        body,
        mesh=mesh,
        in_specs=(
            rows, rows, rows, rows,
            P(("grp", "dom"), None, None),
            P(("grp", "dom"), None, None, None),
            P(("grp", "dom")),
            rows,
            P(("grp", "dom"), None, None, None),
        ),
        out_specs=(rows, rows, rows, rows),
        check_vma=False,
    )
```

```python
import jax
import jax.numpy as jnp
from jax import lax
from jax.experimental import pallas as pl
from jax.experimental.pallas import tpu as pltpu
from jax.sharding import PartitionSpec as P

F32 = jnp.float32
BF16 = jnp.bfloat16
LOW = -1e30
SCALE = 0.125
ROWS = 256
WIDTH = 512
TILE = 128
PAIRS = 4
SLOTS = 8
MATCH = 4
EDGES = 64
DOMAINS = 16
GROUPS = 16
VMEM_LIMIT = 50 * 2**20
WHOLE_VMEM = 63 * 2**20
HALF = WIDTH // 2
TAIL = 16
LINKS = (1, 3, 4, 12)
THIRD = (1, 3, 4, 12)
FOURTH = (3, 1, 12, 4)
A, B, FIRST, BITS = 0, 1, 2, 3
LIST = 2 * SLOTS

def dot(a, b, da=1, db=0):
    return lax.dot_general(a, b, (((da,), (db,)), ((), ())), preferred_element_type=F32)


def one_hot(near_col):
    e, r = near_col.shape[0], ROWS
    return lax.broadcasted_iota(jnp.int32, (e, r), 1) == near_col


def one_hot_t(near_row):
    e, r = near_row.shape[1], ROWS
    return lax.broadcasted_iota(jnp.int32, (r, e), 0) == near_row


def as_bf16(flags):
    return jnp.where(flags, 1.0, 0.0).astype(BF16)


def head_rows():
    s = lax.broadcasted_iota(jnp.int32, (16, WIDTH), 0)
    c = lax.broadcasted_iota(jnp.int32, (16, WIDTH), 1)
    return as_bf16((c >> 6) == 2 * (s & 7) + (s >> 3))


def halves(x):
    hi = x.astype(BF16)
    return hi, (x - hi.astype(F32)).astype(BF16)


def thirds(x):
    hi = x.astype(BF16)
    rest = x - hi.astype(F32)
    mid = rest.astype(BF16)
    return jnp.concatenate([hi, mid, (rest - mid.astype(F32)).astype(BF16)], axis=0)


def select_sum(x, matrix):
    y = dot(thirds(x), matrix)
    return y[0:16] + y[16:32] + y[32:48]


def to_blocks(x, a):
    lanes = slice(a * TILE, (a + 1) * TILE)
    return jnp.concatenate([x[0:8, lanes], x[8:16, lanes]], axis=1)


def from_blocks(x0, x1):
    even = jnp.concatenate([x0[:, :TILE], x1[:, :TILE]], axis=1)
    odd = jnp.concatenate([x0[:, TILE:], x1[:, TILE:]], axis=1)
    return jnp.concatenate([even, odd], axis=0)


def pick_kernel(near_ref, k_ref, v_ref, *outs):
    hot = as_bf16(one_hot(near_ref[...]))
    rows_k = dot(hot, k_ref[...]).astype(BF16)
    rows_v = dot(hot, v_ref[...]).astype(BF16)
    for m, out in enumerate(outs):
        part = slice(m * EDGES, (m + 1) * EDGES)
        out[:, :WIDTH] = rows_k[part]
        out[:, WIDTH:] = rows_v[part]


def pair_kernel(nc_ref, nr_ref, q_ref, k_ref, v_ref, g_ref, f0, f1, f2, f3, nq_ref, ng_ref, st_ref, top_ref):
    hot = one_hot(nc_ref[...])
    hot_b = as_bf16(hot)
    hot_t = as_bf16(one_hot_t(nr_ref[...]))
    heads = head_rows()
    qs = q_ref[...].astype(F32) * SCALE
    g = g_ref[...].astype(F32)

    far = jnp.concatenate([f0[...], f1[...], f2[...], f3[...]], axis=0).astype(F32)
    far_k, far_v = far[:, :WIDTH], far[:, WIDTH:]
    near_q = dot(hot_b, qs.astype(BF16))
    near_g = dot(hot_b, g_ref[...])
    nq_ref[...] = near_q.astype(BF16)
    ng_ref[...] = near_g.astype(BF16)

    def head_sum(x):
        hi, lo = halves(x)
        return dot(heads, hi, 1, 1) + dot(heads, lo, 1, 1)

    self_score = head_sum(qs * k_ref[...].astype(F32))
    self_drop = head_sum(g * v_ref[...].astype(F32))
    product = near_q * far_k
    hi, lo = halves(product)
    pair_score = dot(heads, hi, 1, 1) + dot(heads, lo, 1, 1)
    by_edge = dot(hi, heads, 1, 1) + dot(lo, heads, 1, 1)
    pair_drop = head_sum(near_g * far_v)
    top_ref[...] = self_score
    for s in (0, 1, 2, 3, 8, 9, 10, 11):
        best = jnp.max(jnp.where(hot, by_edge[:, s:s + 1], LOW), axis=0, keepdims=True)
        top_ref[s:s + 1, :] = jnp.maximum(top_ref[s:s + 1, :], best)
    top = top_ref[...]
    self_exp = jnp.exp(self_score - top)
    pair_exp = jnp.exp(pair_score - select_sum(top, hot_t))
    st_ref[0:16] = top
    st_ref[16:32] = self_exp + select_sum(pair_exp, hot_b)
    st_ref[32:48] = self_exp
    st_ref[48:64] = pair_exp
    st_ref[64:80] = self_drop
    st_ref[80:96] = pair_drop


def bit(info, row, link):
    return info[row, BITS + LINKS.index(link)]


def ring_index(info, row, part):
    low, high = ((4, 12), (1, 3))[part]
    return bit(info, row, low) + 2 * bit(info, row, high)


def split_kernel(me, tail_ref, k0, k1, k2, k3, v0, v1, v2, v3, ka, kb, va, vb, info_ref, tails, sem):
    copies = []
    for p, (sources, outs) in enumerate((((k0, k1, k2, k3), (ka, kb)), ((v0, v1, v2, v3), (va, vb)))):
        for i, source in enumerate(sources):
            for h, out in enumerate(outs):
                copies.append(pltpu.make_async_copy(
                    source.at[0:ROWS, h * HALF:(h + 1) * HALF], out.at[i], sem.at[p * 8 + i * 2 + h]))
    for i, source in enumerate((v1, v2, k1, k2)):
        copies.append(pltpu.make_async_copy(source.at[ROWS:ROWS + TAIL, 0:TILE], tails.at[i], sem.at[16 + i]))
    for copy in copies:
        copy.start()
    for copy in copies[16:]:
        copy.wait()
    lane = lax.broadcasted_iota(jnp.int32, (SLOTS, TILE), 1)
    for i in range(5):
        tail = tail_ref[:, 0:TILE] if i == 0 else tails[i - 1]
        tail = tail[0:SLOTS].astype(F32).astype(jnp.int32)
        block, owner, rows, count = (tail[:, c:c + 1] for c in range(4))
        place = owner * 2 + rows
        first = jnp.full((SLOTS, 1), SLOTS, jnp.int32)
        for t in range(SLOTS):
            first = jnp.minimum(first, jnp.where(place == place[t:t + 1], t, SLOTS))
        apart = owner ^ me[0, 0]
        x, y = apart >> 2, apart & 3
        columns = (block, rows, first, (y ^ (y >> 1)) & 1, y >> 1, (x ^ (x >> 1)) & 1, x >> 1)
        table = jnp.zeros((SLOTS, TILE), jnp.int32)
        for c, column in enumerate(columns):
            table = jnp.where(lane == c, column, table)
        info_ref[i * LIST:i * LIST + SLOTS] = table
        info_ref[i * LIST + SLOTS:(i + 1) * LIST] = jnp.where(lane == 0, count, 0)
    for copy in copies[:16]:
        copy.wait()


def pack_kernel(info, h0, h1, h2, h3, g0, g1, g2, g3, o0, o1, o2, o3, sem):
    held, got, outs = (h0, h1, h2, h3), (g0, g1, g2, g3), (o0, o1, o2, o3)

    def copies(act):
        for q in range(4):
            base = (1 + LINKS.index(FOURTH[q])) * LIST

            @pl.loop(0, info[base + SLOTS, 0])
            def _(t):
                row = base + t
                index = ring_index(info, row, q // 2)
                rows = pl.ds(pl.multiple_of(info[row, B] * TILE, TILE), TILE)
                here = bit(info, row, FOURTH[q]) == 0
                for other, source in enumerate((held[q], got[q])):
                    @pl.when(here & (bit(info, row, THIRD[q]) == other))
                    def _():
                        act(pltpu.make_async_copy(source.at[index, rows], outs[q].at[t], sem.at[q, t]))

    copies(lambda copy: copy.start())
    copies(lambda copy: copy.wait())


def tile_kernel(info, nc_ref, nr_ref, h0, h1, h2, h3, g0, g1, g2, g3, p0, p1, p2, p3,
                mask_ref, q_ref, g_ref, st_ref,
                s0, s1, s2, s3, out_ref, gq_ref, wd_ref,
                kb, vb, eb, mt, lt, ft, top2, sum2, del2, dk, dv,
                qs_ref, gs_ref, qt_ref, gt_ref, mask_buf, in_sem, mask_sem, ready):
    count = info[SLOTS, 0]
    held, got, packed = (h0, h1, h2, h3), (g0, g1, g2, g3), (p0, p1, p2, p3)

    def mask_copy(t):
        return pltpu.make_async_copy(mask_ref.at[t], mask_buf.at[t], mask_sem.at[t])

    def into(t, q):
        return (kb, kb, vb, vb)[q].at[t, :, pl.ds((q % 2) * HALF, HALF)]

    @pl.loop(0, count)
    def _(t):
        mask_copy(t).start()
        rows = pl.ds(pl.multiple_of(info[t, B] * TILE, TILE), TILE)
        for q in range(4):
            index = ring_index(info, t, q // 2)
            third, fourth = bit(info, t, THIRD[q]), bit(info, t, FOURTH[q])

            def fetch(source):
                pltpu.make_async_copy(source, into(t, q), in_sem.at[q, t]).start()

            @pl.when(fourth == 1)
            def _():
                fetch(packed[q].at[t])

            @pl.when((fourth == 0) & (third == 1))
            def _():
                fetch(got[q].at[index, rows])

            @pl.when((fourth == 0) & (third == 0))
            def _():
                fetch(held[q].at[index, rows])

    def arrived(t, part):
        for q in (2 * part, 2 * part + 1):
            pltpu.make_async_copy(packed[q].at[0], into(t, q), in_sem.at[q, t]).wait()

    ready()
    low_rows = lax.broadcasted_iota(jnp.int32, (TILE, TILE), 0) < 64
    low_lanes = lax.broadcasted_iota(jnp.int32, (TILE, TILE), 1) < 64
    qs = q_ref[...].astype(F32) * SCALE
    g = g_ref[...].astype(F32)
    for source, by_col, by_row in ((qs, qs_ref, qt_ref), (g, gs_ref, gt_ref)):
        for a in range(2):
            for p in range(PAIRS):
                x = source[a * TILE:(a + 1) * TILE, p * TILE:(p + 1) * TILE]
                xt = x.T
                by_col[a, p] = jnp.concatenate(
                    [jnp.where(low_rows, xt, 0.0), jnp.where(low_rows, 0.0, xt)], axis=1).astype(BF16)
                by_row[a, p] = jnp.concatenate(
                    [jnp.where(low_lanes, x, 0.0), jnp.where(low_lanes, 0.0, x)], axis=0).astype(BF16)

    top1, sum1 = st_ref[0:16], st_ref[16:32]
    self_exp, pair_exp = st_ref[32:48], st_ref[48:64]
    self_drop, pair_drop = st_ref[64:80], st_ref[80:96]
    hot_b = as_bf16(one_hot(nc_ref[...]))
    hot_t = as_bf16(one_hot_t(nr_ref[...]))
    for a in range(2):
        top2[a] = to_blocks(top1, a)

    @pl.loop(0, count)
    def _(t):
        a = info[t, 0]
        arrived(t, 0)
        mask_copy(t).wait()
        bias = jnp.where(mask_buf[t].astype(F32).T != 0, 0.0, LOW)
        bias = jnp.concatenate([bias, bias], axis=1)
        for p in range(PAIRS):
            s = dot(kb[t, :, p * TILE:(p + 1) * TILE], qs_ref[a, p]) + bias
            m = jnp.max(s, axis=0, keepdims=True)
            e = jnp.exp(s - m)
            eb[t, p] = e
            mt[t, p:p + 1] = m
            lt[t, p:p + 1] = jnp.sum(e, axis=0, keepdims=True)
        top2[a, 0:PAIRS] = jnp.maximum(top2[a, 0:PAIRS], mt[t, 0:PAIRS])

    for a in range(2):
        sum2[a] = to_blocks(sum1, a) * jnp.exp(to_blocks(top1, a) - top2[a])

    @pl.loop(0, count)
    def _(t):
        a = info[t, 0]
        shrink = jnp.exp(mt[t, 0:PAIRS] - top2[a, 0:PAIRS])
        ft[t, 0:PAIRS] = shrink
        sum2[a, 0:PAIRS] += lt[t, 0:PAIRS] * shrink

    @pl.loop(0, count)
    def _(t):
        a = info[t, 0]
        ft[t, 0:PAIRS] = ft[t, 0:PAIRS] / sum2[a, 0:PAIRS]

    factor = jnp.exp(top1 - from_blocks(top2[0], top2[1])) / from_blocks(sum2[0], sum2[1])
    self_w = self_exp * factor
    pair_w = pair_exp * select_sum(factor, hot_t)
    self_wb = self_w.astype(BF16).astype(F32)
    pair_wb = pair_w.astype(BF16).astype(F32)
    wd_ref[0:16] = self_wb
    wd_ref[16:32] = pair_wb
    delta = self_wb * self_drop + select_sum(pair_wb * pair_drop, hot_b)

    out_ref[...] = jnp.zeros_like(out_ref)
    gq_ref[...] = jnp.zeros_like(gq_ref)

    def add_term(acc, t, p, term):
        f = info[t, FIRST]
        cols = slice(p * TILE, (p + 1) * TILE)
        acc[f, :, cols] = jnp.where(f == t, 0.0, acc[f, :, cols]) + term

    @pl.loop(0, count)
    def _(t):
        a = info[t, 0]
        arrived(t, 1)
        for p in range(PAIRS):
            wb = (eb[t, p] * ft[t, p:p + 1]).astype(BF16)
            out_ref[a, p] += dot(vb[t, :, p * TILE:(p + 1) * TILE], wb, 0, 0)
            add_term(dv, t, p, dot(wb, gt_ref[a, p]))

    for a in range(2):
        base = to_blocks(delta, a)
        for p in range(PAIRS):
            del2[a, p:p + 1] = base[p:p + 1] + jnp.sum(
                gs_ref[a, p].astype(F32) * out_ref[a, p], axis=0, keepdims=True)
        del2[a, PAIRS:8] = jnp.zeros((8 - PAIRS, 2 * TILE), F32)
    delta = from_blocks(del2[0], del2[1])
    wd_ref[32:48] = self_w * (self_drop - delta)
    wd_ref[48:64] = pair_w * (pair_drop - select_sum(delta, hot_t))

    @pl.loop(0, count)
    def _(t):
        a = info[t, 0]
        for p in range(PAIRS):
            cols = slice(p * TILE, (p + 1) * TILE)
            drop = dot(vb[t, :, cols], gs_ref[a, p])
            ds = (eb[t, p] * ft[t, p:p + 1] * (drop - del2[a, p:p + 1])).astype(BF16)
            gq_ref[a, p] += dot(kb[t, :, cols], ds, 0, 0)
            add_term(dk, t, p, dot(ds, qt_ref[a, p]))

    @pl.loop(0, count)
    def _(t):
        @pl.when(info[t, FIRST] == t)
        def _():
            s0[t] = dk[t, :, 0:HALF].astype(BF16)
            s1[t] = dk[t, :, HALF:WIDTH].astype(BF16)
            s2[t] = dv[t, :, 0:HALF].astype(BF16)
            s3[t] = dv[t, :, HALF:WIDTH].astype(BF16)


def each_term(info, q, third, mine, theirs, add):
    for base, terms in ((0, mine), ((1 + LINKS.index(FOURTH[q])) * LIST, theirs)):
        @pl.loop(0, info[base + SLOTS, 0])
        def _(t):
            row = base + t

            @pl.when((info[row, FIRST] == t) & (bit(info, row, FOURTH[q]) == 0) & (bit(info, row, THIRD[q]) == third))
            def _():
                rows = pl.ds(pl.multiple_of(info[row, B] * TILE, TILE), TILE)
                add(ring_index(info, row, q // 2), rows, terms[t].astype(F32))


def second_kernel(info, m0, m1, m2, m3, g0, g1, g2, g3, o0, o1, o2, o3):
    for q, (mine, theirs, out) in enumerate(zip((m0, m1, m2, m3), (g0, g1, g2, g3), (o0, o1, o2, o3))):
        out[...] = jnp.zeros_like(out)

        def add(index, rows, term):
            out[index, rows] = (out[index, rows].astype(F32) + term).astype(BF16)

        each_term(info, q, 1, mine, theirs, add)


def third_kernel(info, m0, m1, m2, m3, g0, g1, g2, g3, n0, n1, n2, n3,
                 k1, k2, k3, v1, v2, v3, kk, kv, total):
    got = (n0, n1, n2, n3)
    for q, (mine, theirs) in enumerate(zip((m0, m1, m2, m3), (g0, g1, g2, g3))):
        total[q] = got[q][...].astype(F32)

        def add(index, rows, term):
            total[q, index, rows] += term

        each_term(info, q, 0, mine, theirs, add)
        cols = slice((q % 2) * HALF, (q % 2 + 1) * HALF)
        (kk, kv)[q // 2][:, cols] = total[q, 0]
        for i, out in enumerate(((k1, k2, k3), (v1, v2, v3))[q // 2]):
            out[:, cols] = total[q, i + 1].astype(BF16)


def rest_kernel(nr_ref, q_ref, k_ref, v_ref, g_ref, f0, f1, f2, f3, nq_ref, ng_ref, acc_ref, gacc_ref, wd_ref,
                out_ref, gq_ref, own_ref, b0, b1, b2, b3):
    hot_t = as_bf16(one_hot_t(nr_ref[...]))
    heads = head_rows()

    def expand(x):
        return dot(x.astype(BF16), heads, 0, 0)

    far = jnp.concatenate([f0[...], f1[...], f2[...], f3[...]], axis=0).astype(F32)
    self_wb, pair_wb = expand(wd_ref[0:16]), expand(wd_ref[16:32])
    self_ds, pair_ds = expand(wd_ref[32:48]), expand(wd_ref[48:64])
    back_k = (pair_ds * nq_ref[...].astype(F32)).astype(BF16)
    back_v = (pair_wb * ng_ref[...].astype(F32)).astype(BF16)
    for m, out in enumerate((b0, b1, b2, b3)):
        part = slice(m * EDGES, (m + 1) * EDGES)
        out[:, :WIDTH] = back_k[part]
        out[:, WIDTH:] = back_v[part]
    own_ref[0:ROWS] = self_ds * (q_ref[...].astype(F32) * SCALE)
    own_ref[ROWS:2 * ROWS] = self_wb * g_ref[...].astype(F32)

    def finish(own, pair, acc, scale, out):
        hi, lo = halves(pair)
        total = own + dot(hot_t, hi) + dot(hot_t, lo)
        for a in range(2):
            for p in range(PAIRS):
                x = acc[a, p]
                x = jnp.concatenate([x[0:64, :TILE], x[64:TILE, TILE:]], axis=0).T
                rows, cols = slice(a * TILE, (a + 1) * TILE), slice(p * TILE, (p + 1) * TILE)
                out[rows, cols] = ((total[rows, cols] + x) * scale).astype(BF16)

    finish(self_wb * v_ref[...].astype(F32), pair_wb * far[:, WIDTH:], acc_ref, 1.0, out_ref)
    finish(self_ds * k_ref[...].astype(F32), pair_ds * far[:, :WIDTH], gacc_ref, SCALE, gq_ref)


def last_kernel(nr_ref, kk, kv, k1, k2, k3, v1, v2, v3, own_ref, b0, b1, b2, b3, gk_ref, gv_ref):
    hot_t = as_bf16(one_hot_t(nr_ref[...]))
    back = jnp.concatenate([b0[...], b1[...], b2[...], b3[...]], axis=0)
    for part, (kept, terms, out) in enumerate(((kk, (k1, k2, k3), gk_ref), (kv, (v1, v2, v3), gv_ref))):
        total = kept[...] + own_ref[part * ROWS:(part + 1) * ROWS]
        for term in terms:
            total += term[...].astype(F32)
        out[...] = (total + dot(hot_t, back[:, part * WIDTH:(part + 1) * WIDTH])).astype(BF16)


def staged(kernel, scalars, raw, n_in, n_out, late):
    def run(*refs):
        *refs, sem = refs
        moved = [i for i in range(scalars, n_in) if i not in raw]
        ins, outs = list(refs[:n_in]), refs[n_in:n_in + n_out]
        buffers, scratch = refs[n_in + n_out:n_in + n_out + len(moved)], refs[n_in + n_out + len(moved):]
        copies = [pltpu.make_async_copy(ins[i], buf, sem.at[j]) for j, (i, buf) in enumerate(zip(moved, buffers))]
        for copy in copies:
            copy.start()
        for i, buf in zip(moved, buffers):
            ins[i] = buf

        def ready():
            for copy in copies:
                copy.wait()

        if late:
            kernel(*ins, *outs, *scratch, ready)
        else:
            ready()
            kernel(*ins, *outs, *scratch)
    return run


def call(kernel, outs, args, scalars=0, raw=(), scratch=(), cost=(1e8, 4e6), late=False, loose=(), limit=VMEM_LIMIT):
    smem, anywhere = pl.BlockSpec(memory_space=pltpu.SMEM), pl.BlockSpec(memory_space=pl.ANY)
    moved = [x for i, x in enumerate(args) if i >= scalars and i not in raw]
    return pl.pallas_call(
        staged(kernel, scalars, raw, len(args), len(outs), late),
        out_shape=[jax.ShapeDtypeStruct(s, d) for s, d in outs],
        in_specs=[smem if i < scalars else anywhere for i in range(len(args))],
        out_specs=[anywhere if i in loose else pl.BlockSpec(memory_space=pltpu.VMEM) for i in range(len(outs))],
        scratch_shapes=[pltpu.VMEM(x.shape, x.dtype) for x in moved] + list(scratch)
        + [pltpu.SemaphoreType.DMA((max(len(moved), 1),))],
        compiler_params=pltpu.CompilerParams(vmem_limit_bytes=limit),
        cost_estimate=pl.CostEstimate(flops=int(cost[0]), bytes_accessed=int(cost[1]), transcendentals=0),
    )(*args)


def over(block, link):
    return lax.ppermute(block, "dom", [(i, i ^ link) for i in range(DOMAINS)])


def to_group(code):
    pairs = [(i, i ^ code) for i in range(GROUPS)]
    return lambda block: lax.ppermute(block, "grp", pairs)


def switched(block, code):
    return lax.switch(code - 1, [to_group(c) for c in range(1, GROUPS)], block)


def halfway_first(rows, at):
    return jnp.stack([
        sum(jnp.where(at == m, rows[m], 0) for m in range(MATCH)),
        *(jnp.where(m - 1 < at, rows[m - 1], rows[m]) for m in range(1, MATCH)),
    ])


def body(query, key, value, cotangent, tile_index, tile_mask, tile_count, partner, pair_edges):
    tied = lax.optimization_barrier
    node = ((ROWS, WIDTH), BF16)
    half = ((4, ROWS, HALF), BF16)
    slots = ((SLOTS, TILE, HALF), BF16)
    block = ((EDGES, 2 * WIDTH), BF16)

    tail = jnp.concatenate([tile_index[0], jnp.broadcast_to(tile_count[:, None], (SLOTS, 1))], axis=1)
    tail = jnp.pad(tail.astype(BF16), ((0, TAIL - SLOTS), (0, WIDTH - 4)))
    keys, values = (jnp.concatenate([x, tail], axis=0) for x in (key, value))
    ring_k = [over(keys, link) for link in (8, 4, 12)]
    ring_v = [over(values, link) for link in (2, 1, 3)]

    codes = jnp.bitwise_xor(partner[0] // DOMAINS, lax.axis_index("grp"))
    slot4 = jnp.arange(MATCH, dtype=jnp.int32)
    at = jnp.sum(jnp.where(codes == GROUPS // 2, slot4, 0))
    codes = halfway_first(codes, at)
    near = halfway_first(pair_edges[0, :, :, 0], at).reshape(-1)
    near_col, near_row = near.reshape(-1, 1), near.reshape(1, -1)
    sent = call(pick_kernel, [block] * MATCH, (near_col, key, value), limit=WHOLE_VMEM)

    far0 = to_group(GROUPS // 2)(sent[0])

    me = lax.axis_index("dom").reshape(1, 1)
    *held, info = call(
        split_kernel, [half] * 4 + [((5 * LIST, TILE), jnp.int32)],
        (me, tail, keys, ring_k[1], ring_k[2], ring_k[0], values, ring_v[1], ring_v[2], ring_v[0]),
        scalars=1, raw=range(2, 10),
        scratch=[pltpu.VMEM((4, TAIL, TILE), BF16), pltpu.SemaphoreType.DMA((20,))])
    held, info, sent, far0 = tied((held, info, sent, far0))
    got = [over(x, link) for x, link in zip(held, THIRD)]
    far1 = switched(sent[1], codes[1])
    got, far1, sent2, sent3 = tied((got, far1, sent[2], sent[3]))
    packs = call(
        pack_kernel, [slots] * 4, (info, *held, *got), scalars=1, raw=range(1, 9),
        scratch=[pltpu.SemaphoreType.DMA((4, SLOTS))])
    packs, sent2, sent3 = tied((packs, sent2, sent3))
    packed = [over(x, link) for x, link in zip(packs, FOURTH)]
    far = [far0, far1, switched(sent2, codes[2]), switched(sent3, codes[3])]
    near_q, near_g, stats = call(
        pair_kernel, [node, node, ((96, ROWS), F32)], (near_col, near_row, query, key, value, cotangent, *far),
        scratch=[pltpu.VMEM((16, ROWS), F32)])

    acc = ((2, PAIRS, TILE, 2 * TILE), F32)
    row_stat = pltpu.VMEM((SLOTS, 8, 2 * TILE), F32)
    block_stat = pltpu.VMEM((2, 8, 2 * TILE), F32)
    by_col = pltpu.VMEM((2, PAIRS, TILE, 2 * TILE), BF16)
    by_row = pltpu.VMEM((2, PAIRS, 2 * TILE, TILE), BF16)
    tiles_b = pltpu.VMEM((SLOTS, TILE, WIDTH), BF16)
    tiles_f = pltpu.VMEM((SLOTS, TILE, WIDTH), F32)
    *terms, out_acc, gq_acc, grads = call(
        tile_kernel,
        [slots] * 4 + [acc, acc, ((64, ROWS), F32)],
        (info, near_col, near_row, *held, *got, *packed, tile_mask[0], query, cotangent, stats),
        scalars=1, raw=range(3, 16), cost=(1e9, 2e7), late=True,
        scratch=[
            tiles_b, tiles_b, pltpu.VMEM((SLOTS, PAIRS, TILE, 2 * TILE), F32),
            row_stat, row_stat, row_stat, block_stat, block_stat, block_stat,
            tiles_f, tiles_f,
            by_col, by_col, by_row, by_row, pltpu.VMEM((SLOTS, TILE, TILE), jnp.int32),
            pltpu.SemaphoreType.DMA((4, SLOTS)), pltpu.SemaphoreType.DMA((SLOTS,)),
        ],
    )

    theirs = [over(x, link) for x, link in zip(terms, FOURTH)]
    attended, grad_query, own, *back = call(
        rest_kernel,
        [node, node, ((2 * ROWS, WIDTH), F32)] + [block] * MATCH,
        (near_row, query, key, value, cotangent, *far, near_q, near_g, out_acc, gq_acc, grads))
    back0 = to_group(GROUPS // 2)(back[0])
    back1, back2 = switched(back[1], codes[1]), switched(back[2], codes[2])
    theirs, back1, back2, back3 = tied((theirs, back1, back2, back[3]))
    sums = call(second_kernel, [half] * 4, (info, *terms, *theirs), scalars=1)
    sums, back3 = tied((sums, back3))
    more = [over(x, link) for x, link in zip(sums, THIRD)]
    back3 = switched(back3, codes[3])
    more, back3 = tied((more, back3))
    *ring, kept_k, kept_v = call(
        third_kernel, [node] * 6 + [((ROWS, WIDTH), F32)] * 2, (info, *terms, *theirs, *more), scalars=1,
        scratch=[pltpu.VMEM((4, 4, ROWS, HALF), F32)])
    ring, back0 = tied((ring, back0))
    order = ((2, 8), (5, 2), (0, 4), (3, 1), (1, 12), (4, 3))
    arrived = {i: over(ring[i], link) for i, link in order}
    grad_key, grad_value = call(
        last_kernel, [node, node],
        (near_row, kept_k, kept_v, *(arrived[i] for i in range(6)), own, back0, back1, back2, back3))
    return attended, grad_query, grad_key, grad_value


def solution(mesh):
    rows = P(("grp", "dom"), None)
    return jax.shard_map(
        body,
        mesh=mesh,
        in_specs=(
            rows, rows, rows, rows,
            P(("grp", "dom"), None, None),
            P(("grp", "dom"), None, None, None),
            P(("grp", "dom")),
            rows,
            P(("grp", "dom"), None, None, None),
        ),
        out_specs=(rows, rows, rows, rows),
        check_vma=False,
    )
```

```python
import jax
import jax.numpy as jnp
from jax import lax
from jax.experimental import pallas as pl
from jax.experimental.pallas import tpu as pltpu
from jax.sharding import PartitionSpec as P

F32 = jnp.float32
BF16 = jnp.bfloat16
LOW = -1e30
SCALE = 0.125
ROWS = 256
WIDTH = 512
TILE = 128
PAIRS = 4
SLOTS = 8
MATCH = 4
EDGES = 64
DOMAINS = 16
GROUPS = 16
VMEM_LIMIT = 50 * 2**20
WHOLE_VMEM = 63 * 2**20
HALF = WIDTH // 2
TAIL = 16
LINKS = (1, 3, 4, 12)
THIRD = (1, 3, 4, 12)
FOURTH = (3, 1, 12, 4)
A, B, FIRST, BITS = 0, 1, 2, 3
LIST = 2 * SLOTS

def dot(a, b, da=1, db=0):
    return lax.dot_general(a, b, (((da,), (db,)), ((), ())), preferred_element_type=F32)


def one_hot(near_col):
    e, r = near_col.shape[0], ROWS
    return lax.broadcasted_iota(jnp.int32, (e, r), 1) == near_col


def one_hot_t(near_row):
    e, r = near_row.shape[1], ROWS
    return lax.broadcasted_iota(jnp.int32, (r, e), 0) == near_row


def as_bf16(flags):
    return jnp.where(flags, 1.0, 0.0).astype(BF16)


def head_rows():
    s = lax.broadcasted_iota(jnp.int32, (16, WIDTH), 0)
    c = lax.broadcasted_iota(jnp.int32, (16, WIDTH), 1)
    return as_bf16((c >> 6) == 2 * (s & 7) + (s >> 3))


def halves(x):
    hi = x.astype(BF16)
    return hi, (x - hi.astype(F32)).astype(BF16)


def thirds(x):
    hi = x.astype(BF16)
    rest = x - hi.astype(F32)
    mid = rest.astype(BF16)
    return jnp.concatenate([hi, mid, (rest - mid.astype(F32)).astype(BF16)], axis=0)


def select_sum(x, matrix):
    y = dot(thirds(x), matrix)
    return y[0:16] + y[16:32] + y[32:48]


def to_blocks(x, a):
    lanes = slice(a * TILE, (a + 1) * TILE)
    return jnp.concatenate([x[0:8, lanes], x[8:16, lanes]], axis=1)


def from_blocks(x0, x1):
    even = jnp.concatenate([x0[:, :TILE], x1[:, :TILE]], axis=1)
    odd = jnp.concatenate([x0[:, TILE:], x1[:, TILE:]], axis=1)
    return jnp.concatenate([even, odd], axis=0)


def pick_kernel(near_ref, k_ref, v_ref, *outs):
    hot = as_bf16(one_hot(near_ref[...]))
    rows_k = dot(hot, k_ref[...]).astype(BF16)
    rows_v = dot(hot, v_ref[...]).astype(BF16)
    for m, out in enumerate(outs):
        part = slice(m * EDGES, (m + 1) * EDGES)
        out[:, :WIDTH] = rows_k[part]
        out[:, WIDTH:] = rows_v[part]


def pair_kernel(nc_ref, nr_ref, q_ref, k_ref, v_ref, g_ref, f0, f1, f2, f3, nq_ref, ng_ref, st_ref, top_ref):
    hot = one_hot(nc_ref[...])
    hot_b = as_bf16(hot)
    hot_t = as_bf16(one_hot_t(nr_ref[...]))
    heads = head_rows()
    qs = q_ref[...].astype(F32) * SCALE
    g = g_ref[...].astype(F32)

    far = jnp.concatenate([f0[...], f1[...], f2[...], f3[...]], axis=0).astype(F32)
    far_k, far_v = far[:, :WIDTH], far[:, WIDTH:]
    near_q = dot(hot_b, qs.astype(BF16))
    near_g = dot(hot_b, g_ref[...])
    nq_ref[...] = near_q.astype(BF16)
    ng_ref[...] = near_g.astype(BF16)

    def head_sum(x):
        hi, lo = halves(x)
        return dot(heads, hi, 1, 1) + dot(heads, lo, 1, 1)

    self_score = head_sum(qs * k_ref[...].astype(F32))
    self_drop = head_sum(g * v_ref[...].astype(F32))
    product = near_q * far_k
    hi, lo = halves(product)
    pair_score = dot(heads, hi, 1, 1) + dot(heads, lo, 1, 1)
    by_edge = dot(hi, heads, 1, 1) + dot(lo, heads, 1, 1)
    pair_drop = head_sum(near_g * far_v)
    top_ref[...] = self_score
    for s in (0, 1, 2, 3, 8, 9, 10, 11):
        best = jnp.max(jnp.where(hot, by_edge[:, s:s + 1], LOW), axis=0, keepdims=True)
        top_ref[s:s + 1, :] = jnp.maximum(top_ref[s:s + 1, :], best)
    top = top_ref[...]
    self_exp = jnp.exp(self_score - top)
    pair_exp = jnp.exp(pair_score - select_sum(top, hot_t))
    st_ref[0:16] = top
    st_ref[16:32] = self_exp + select_sum(pair_exp, hot_b)
    st_ref[32:48] = self_exp
    st_ref[48:64] = pair_exp
    st_ref[64:80] = self_drop
    st_ref[80:96] = pair_drop


def bit(info, row, link):
    return info[row, BITS + LINKS.index(link)]


def ring_index(info, row, part):
    low, high = ((4, 12), (1, 3))[part]
    return bit(info, row, low) + 2 * bit(info, row, high)


def split_kernel(me, tail_ref, k0, k1, k2, k3, v0, v1, v2, v3, ka, kb, va, vb, info_ref, tails, sem):
    copies = []
    for p, (sources, outs) in enumerate((((k0, k1, k2, k3), (ka, kb)), ((v0, v1, v2, v3), (va, vb)))):
        for i, source in enumerate(sources):
            for h, out in enumerate(outs):
                copies.append(pltpu.make_async_copy(
                    source.at[0:ROWS, h * HALF:(h + 1) * HALF], out.at[i], sem.at[p * 8 + i * 2 + h]))
    for i, source in enumerate((v1, v2, k1, k2)):
        copies.append(pltpu.make_async_copy(source.at[ROWS:ROWS + TAIL, 0:TILE], tails.at[i], sem.at[16 + i]))
    for copy in copies:
        copy.start()
    for copy in copies[16:]:
        copy.wait()
    lane = lax.broadcasted_iota(jnp.int32, (SLOTS, TILE), 1)
    for i in range(5):
        tail = tail_ref[:, 0:TILE] if i == 0 else tails[i - 1]
        tail = tail[0:SLOTS].astype(F32).astype(jnp.int32)
        block, owner, rows, count = (tail[:, c:c + 1] for c in range(4))
        place = owner * 2 + rows
        first = jnp.full((SLOTS, 1), SLOTS, jnp.int32)
        for t in range(SLOTS):
            first = jnp.minimum(first, jnp.where(place == place[t:t + 1], t, SLOTS))
        apart = owner ^ me[0, 0]
        x, y = apart >> 2, apart & 3
        columns = (block, rows, first, (y ^ (y >> 1)) & 1, y >> 1, (x ^ (x >> 1)) & 1, x >> 1)
        table = jnp.zeros((SLOTS, TILE), jnp.int32)
        for c, column in enumerate(columns):
            table = jnp.where(lane == c, column, table)
        info_ref[i * LIST:i * LIST + SLOTS] = table
        info_ref[i * LIST + SLOTS:(i + 1) * LIST] = jnp.where(lane == 0, count, 0)
    for copy in copies[:16]:
        copy.wait()


def pack_kernel(info, h0, h1, h2, h3, g0, g1, g2, g3, o0, o1, o2, o3, sem):
    held, got, outs = (h0, h1, h2, h3), (g0, g1, g2, g3), (o0, o1, o2, o3)

    def copies(act):
        for q in range(4):
            base = (1 + LINKS.index(FOURTH[q])) * LIST

            @pl.loop(0, info[base + SLOTS, 0])
            def _(t):
                row = base + t
                index = ring_index(info, row, q // 2)
                rows = pl.ds(pl.multiple_of(info[row, B] * TILE, TILE), TILE)
                here = bit(info, row, FOURTH[q]) == 0
                for other, source in enumerate((held[q], got[q])):
                    @pl.when(here & (bit(info, row, THIRD[q]) == other))
                    def _():
                        act(pltpu.make_async_copy(source.at[index, rows], outs[q].at[t], sem.at[q, t]))

    copies(lambda copy: copy.start())
    copies(lambda copy: copy.wait())


def tile_kernel(info, nc_ref, nr_ref, h0, h1, h2, h3, g0, g1, g2, g3, p0, p1, p2, p3,
                mask_ref, q_ref, g_ref, st_ref,
                s0, s1, s2, s3, out_ref, gq_ref, wd_ref,
                kb, vb, eb, mt, lt, ft, top2, sum2, del2, dk, dv,
                qs_ref, gs_ref, qt_ref, gt_ref, mask_buf, in_sem, mask_sem, ready):
    count = info[SLOTS, 0]
    held, got, packed = (h0, h1, h2, h3), (g0, g1, g2, g3), (p0, p1, p2, p3)

    def mask_copy(t):
        return pltpu.make_async_copy(mask_ref.at[t], mask_buf.at[t], mask_sem.at[t])

    def into(t, q):
        return (kb, kb, vb, vb)[q].at[t, :, pl.ds((q % 2) * HALF, HALF)]

    @pl.loop(0, count)
    def _(t):
        mask_copy(t).start()
        rows = pl.ds(pl.multiple_of(info[t, B] * TILE, TILE), TILE)
        for q in range(4):
            index = ring_index(info, t, q // 2)
            third, fourth = bit(info, t, THIRD[q]), bit(info, t, FOURTH[q])

            def fetch(source):
                pltpu.make_async_copy(source, into(t, q), in_sem.at[q, t]).start()

            @pl.when(fourth == 1)
            def _():
                fetch(packed[q].at[t])

            @pl.when((fourth == 0) & (third == 1))
            def _():
                fetch(got[q].at[index, rows])

            @pl.when((fourth == 0) & (third == 0))
            def _():
                fetch(held[q].at[index, rows])

    def arrived(t, part):
        for q in (2 * part, 2 * part + 1):
            pltpu.make_async_copy(packed[q].at[0], into(t, q), in_sem.at[q, t]).wait()

    ready()
    low_rows = lax.broadcasted_iota(jnp.int32, (TILE, TILE), 0) < 64
    low_lanes = lax.broadcasted_iota(jnp.int32, (TILE, TILE), 1) < 64
    qs = q_ref[...].astype(F32) * SCALE
    g = g_ref[...].astype(F32)
    for source, by_col, by_row in ((qs, qs_ref, qt_ref), (g, gs_ref, gt_ref)):
        for a in range(2):
            for p in range(PAIRS):
                x = source[a * TILE:(a + 1) * TILE, p * TILE:(p + 1) * TILE]
                xt = x.T
                by_col[a, p] = jnp.concatenate(
                    [jnp.where(low_rows, xt, 0.0), jnp.where(low_rows, 0.0, xt)], axis=1).astype(BF16)
                by_row[a, p] = jnp.concatenate(
                    [jnp.where(low_lanes, x, 0.0), jnp.where(low_lanes, 0.0, x)], axis=0).astype(BF16)

    top1, sum1 = st_ref[0:16], st_ref[16:32]
    self_exp, pair_exp = st_ref[32:48], st_ref[48:64]
    self_drop, pair_drop = st_ref[64:80], st_ref[80:96]
    hot_b = as_bf16(one_hot(nc_ref[...]))
    hot_t = as_bf16(one_hot_t(nr_ref[...]))
    for a in range(2):
        top2[a] = to_blocks(top1, a)

    @pl.loop(0, count)
    def _(t):
        a = info[t, 0]
        arrived(t, 0)
        mask_copy(t).wait()
        bias = jnp.where(mask_buf[t].astype(F32).T != 0, 0.0, LOW)
        bias = jnp.concatenate([bias, bias], axis=1)
        for p in range(PAIRS):
            s = dot(kb[t, :, p * TILE:(p + 1) * TILE], qs_ref[a, p]) + bias
            m = jnp.max(s, axis=0, keepdims=True)
            e = jnp.exp(s - m)
            eb[t, p] = e
            mt[t, p:p + 1] = m
            lt[t, p:p + 1] = jnp.sum(e, axis=0, keepdims=True)
        top2[a, 0:PAIRS] = jnp.maximum(top2[a, 0:PAIRS], mt[t, 0:PAIRS])

    for a in range(2):
        sum2[a] = to_blocks(sum1, a) * jnp.exp(to_blocks(top1, a) - top2[a])

    @pl.loop(0, count)
    def _(t):
        a = info[t, 0]
        shrink = jnp.exp(mt[t, 0:PAIRS] - top2[a, 0:PAIRS])
        ft[t, 0:PAIRS] = shrink
        sum2[a, 0:PAIRS] += lt[t, 0:PAIRS] * shrink

    @pl.loop(0, count)
    def _(t):
        a = info[t, 0]
        ft[t, 0:PAIRS] = ft[t, 0:PAIRS] / sum2[a, 0:PAIRS]

    factor = jnp.exp(top1 - from_blocks(top2[0], top2[1])) / from_blocks(sum2[0], sum2[1])
    self_w = self_exp * factor
    pair_w = pair_exp * select_sum(factor, hot_t)
    self_wb = self_w.astype(BF16).astype(F32)
    pair_wb = pair_w.astype(BF16).astype(F32)
    wd_ref[0:16] = self_wb
    wd_ref[16:32] = pair_wb
    delta = self_wb * self_drop + select_sum(pair_wb * pair_drop, hot_b)

    out_ref[...] = jnp.zeros_like(out_ref)
    gq_ref[...] = jnp.zeros_like(gq_ref)

    def add_term(acc, t, p, term):
        f = info[t, FIRST]
        cols = slice(p * TILE, (p + 1) * TILE)
        acc[f, :, cols] = jnp.where(f == t, 0.0, acc[f, :, cols]) + term

    @pl.loop(0, count)
    def _(t):
        a = info[t, 0]
        arrived(t, 1)
        for p in range(PAIRS):
            wb = (eb[t, p] * ft[t, p:p + 1]).astype(BF16)
            out_ref[a, p] += dot(vb[t, :, p * TILE:(p + 1) * TILE], wb, 0, 0)
            add_term(dv, t, p, dot(wb, gt_ref[a, p]))

    for a in range(2):
        base = to_blocks(delta, a)
        for p in range(PAIRS):
            del2[a, p:p + 1] = base[p:p + 1] + jnp.sum(
                gs_ref[a, p].astype(F32) * out_ref[a, p], axis=0, keepdims=True)
        del2[a, PAIRS:8] = jnp.zeros((8 - PAIRS, 2 * TILE), F32)
    delta = from_blocks(del2[0], del2[1])
    wd_ref[32:48] = self_w * (self_drop - delta)
    wd_ref[48:64] = pair_w * (pair_drop - select_sum(delta, hot_t))

    @pl.loop(0, count)
    def _(t):
        a = info[t, 0]
        for p in range(PAIRS):
            cols = slice(p * TILE, (p + 1) * TILE)
            drop = dot(vb[t, :, cols], gs_ref[a, p])
            ds = (eb[t, p] * ft[t, p:p + 1] * (drop - del2[a, p:p + 1])).astype(BF16)
            gq_ref[a, p] += dot(kb[t, :, cols], ds, 0, 0)
            add_term(dk, t, p, dot(ds, qt_ref[a, p]))

    @pl.loop(0, count)
    def _(t):
        @pl.when(info[t, FIRST] == t)
        def _():
            s0[t] = dk[t, :, 0:HALF].astype(BF16)
            s1[t] = dk[t, :, HALF:WIDTH].astype(BF16)
            s2[t] = dv[t, :, 0:HALF].astype(BF16)
            s3[t] = dv[t, :, HALF:WIDTH].astype(BF16)


def each_term(info, q, third, mine, theirs, add):
    for base, terms in ((0, mine), ((1 + LINKS.index(FOURTH[q])) * LIST, theirs)):
        @pl.loop(0, info[base + SLOTS, 0])
        def _(t):
            row = base + t

            @pl.when((info[row, FIRST] == t) & (bit(info, row, FOURTH[q]) == 0) & (bit(info, row, THIRD[q]) == third))
            def _():
                rows = pl.ds(pl.multiple_of(info[row, B] * TILE, TILE), TILE)
                add(ring_index(info, row, q // 2), rows, terms[t].astype(F32))


def second_kernel(info, m0, m1, m2, m3, g0, g1, g2, g3, o0, o1, o2, o3, ready):
    for out in (o0, o1, o2, o3):
        out[...] = jnp.zeros_like(out)
    for q, (mine, theirs, out) in enumerate(zip((m0, m1, m2, m3), (g0, g1, g2, g3), (o0, o1, o2, o3))):
        ready((1 + q, 5 + q))

        def add(index, rows, term):
            out[index, rows] = (out[index, rows].astype(F32) + term).astype(BF16)

        each_term(info, q, 1, mine, theirs, add)


def third_kernel(info, m0, m1, m2, m3, g0, g1, g2, g3, n0, n1, n2, n3,
                 k1, k2, k3, v1, v2, v3, kk, kv, total, ready):
    got = (n0, n1, n2, n3)
    for q, (mine, theirs) in enumerate(zip((m0, m1, m2, m3), (g0, g1, g2, g3))):
        ready((1 + q, 5 + q, 9 + q))
        total[q] = got[q][...].astype(F32)

        def add(index, rows, term):
            total[q, index, rows] += term

        each_term(info, q, 0, mine, theirs, add)
        cols = slice((q % 2) * HALF, (q % 2 + 1) * HALF)
        (kk, kv)[q // 2][:, cols] = total[q, 0]
        for i, out in enumerate(((k1, k2, k3), (v1, v2, v3))[q // 2]):
            out[:, cols] = total[q, i + 1].astype(BF16)


def rest_kernel(nr_ref, q_ref, k_ref, v_ref, g_ref, f0, f1, f2, f3, nq_ref, ng_ref, acc_ref, gacc_ref, wd_ref,
                out_ref, gq_ref, own_ref, b0, b1, b2, b3):
    hot_t = as_bf16(one_hot_t(nr_ref[...]))
    heads = head_rows()

    def expand(x):
        return dot(x.astype(BF16), heads, 0, 0)

    far = jnp.concatenate([f0[...], f1[...], f2[...], f3[...]], axis=0).astype(F32)
    self_wb, pair_wb = expand(wd_ref[0:16]), expand(wd_ref[16:32])
    self_ds, pair_ds = expand(wd_ref[32:48]), expand(wd_ref[48:64])
    back_k = (pair_ds * nq_ref[...].astype(F32)).astype(BF16)
    back_v = (pair_wb * ng_ref[...].astype(F32)).astype(BF16)
    for m, out in enumerate((b0, b1, b2, b3)):
        part = slice(m * EDGES, (m + 1) * EDGES)
        out[:, :WIDTH] = back_k[part]
        out[:, WIDTH:] = back_v[part]
    own_ref[0:ROWS] = self_ds * (q_ref[...].astype(F32) * SCALE)
    own_ref[ROWS:2 * ROWS] = self_wb * g_ref[...].astype(F32)

    def finish(own, pair, acc, scale, out):
        hi, lo = halves(pair)
        total = own + dot(hot_t, hi) + dot(hot_t, lo)
        for a in range(2):
            for p in range(PAIRS):
                x = acc[a, p]
                x = jnp.concatenate([x[0:64, :TILE], x[64:TILE, TILE:]], axis=0).T
                rows, cols = slice(a * TILE, (a + 1) * TILE), slice(p * TILE, (p + 1) * TILE)
                out[rows, cols] = ((total[rows, cols] + x) * scale).astype(BF16)

    finish(self_wb * v_ref[...].astype(F32), pair_wb * far[:, WIDTH:], acc_ref, 1.0, out_ref)
    finish(self_ds * k_ref[...].astype(F32), pair_ds * far[:, :WIDTH], gacc_ref, SCALE, gq_ref)


def last_kernel(nr_ref, kk, kv, k1, k2, k3, v1, v2, v3, own_ref, b0, b1, b2, b3, gk_ref, gv_ref):
    hot_t = as_bf16(one_hot_t(nr_ref[...]))
    back = jnp.concatenate([b0[...], b1[...], b2[...], b3[...]], axis=0)
    for part, (kept, terms, out) in enumerate(((kk, (k1, k2, k3), gk_ref), (kv, (v1, v2, v3), gv_ref))):
        total = kept[...] + own_ref[part * ROWS:(part + 1) * ROWS]
        for term in terms:
            total += term[...].astype(F32)
        out[...] = (total + dot(hot_t, back[:, part * WIDTH:(part + 1) * WIDTH])).astype(BF16)


def staged(kernel, scalars, raw, n_in, n_out, late):
    def run(*refs):
        *refs, sem = refs
        moved = [i for i in range(scalars, n_in) if i not in raw]
        ins, outs = list(refs[:n_in]), refs[n_in:n_in + n_out]
        buffers, scratch = refs[n_in + n_out:n_in + n_out + len(moved)], refs[n_in + n_out + len(moved):]
        copies = [pltpu.make_async_copy(ins[i], buf, sem.at[j]) for j, (i, buf) in enumerate(zip(moved, buffers))]
        for copy in copies:
            copy.start()
        for i, buf in zip(moved, buffers):
            ins[i] = buf

        def ready(only=None):
            for i, copy in zip(moved, copies):
                if only is None or i in only:
                    copy.wait()

        if late:
            kernel(*ins, *outs, *scratch, ready)
        else:
            ready()
            kernel(*ins, *outs, *scratch)
    return run


def call(kernel, outs, args, scalars=0, raw=(), scratch=(), cost=(1e8, 4e6), late=False, loose=(), limit=VMEM_LIMIT):
    smem, anywhere = pl.BlockSpec(memory_space=pltpu.SMEM), pl.BlockSpec(memory_space=pl.ANY)
    moved = [x for i, x in enumerate(args) if i >= scalars and i not in raw]
    return pl.pallas_call(
        staged(kernel, scalars, raw, len(args), len(outs), late),
        out_shape=[jax.ShapeDtypeStruct(s, d) for s, d in outs],
        in_specs=[smem if i < scalars else anywhere for i in range(len(args))],
        out_specs=[anywhere if i in loose else pl.BlockSpec(memory_space=pltpu.VMEM) for i in range(len(outs))],
        scratch_shapes=[pltpu.VMEM(x.shape, x.dtype) for x in moved] + list(scratch)
        + [pltpu.SemaphoreType.DMA((max(len(moved), 1),))],
        compiler_params=pltpu.CompilerParams(vmem_limit_bytes=limit),
        cost_estimate=pl.CostEstimate(flops=int(cost[0]), bytes_accessed=int(cost[1]), transcendentals=0),
    )(*args)


def over(block, link):
    return lax.ppermute(block, "dom", [(i, i ^ link) for i in range(DOMAINS)])


def to_group(code):
    pairs = [(i, i ^ code) for i in range(GROUPS)]
    return lambda block: lax.ppermute(block, "grp", pairs)


def switched(block, code):
    return lax.switch(code - 1, [to_group(c) for c in range(1, GROUPS)], block)


def halfway_first(rows, at):
    return jnp.stack([
        sum(jnp.where(at == m, rows[m], 0) for m in range(MATCH)),
        *(jnp.where(m - 1 < at, rows[m - 1], rows[m]) for m in range(1, MATCH)),
    ])


def body(query, key, value, cotangent, tile_index, tile_mask, tile_count, partner, pair_edges):
    tied = lax.optimization_barrier
    node = ((ROWS, WIDTH), BF16)
    half = ((4, ROWS, HALF), BF16)
    slots = ((SLOTS, TILE, HALF), BF16)
    block = ((EDGES, 2 * WIDTH), BF16)

    tail = jnp.concatenate([tile_index[0], jnp.broadcast_to(tile_count[:, None], (SLOTS, 1))], axis=1)
    tail = jnp.pad(tail.astype(BF16), ((0, TAIL - SLOTS), (0, WIDTH - 4)))
    keys, values = (jnp.concatenate([x, tail], axis=0) for x in (key, value))
    ring_k = [over(keys, link) for link in (8, 4, 12)]
    ring_v = [over(values, link) for link in (2, 1, 3)]

    codes = jnp.bitwise_xor(partner[0] // DOMAINS, lax.axis_index("grp"))
    slot4 = jnp.arange(MATCH, dtype=jnp.int32)
    at = jnp.sum(jnp.where(codes == GROUPS // 2, slot4, 0))
    codes = halfway_first(codes, at)
    near = halfway_first(pair_edges[0, :, :, 0], at).reshape(-1)
    near_col, near_row = near.reshape(-1, 1), near.reshape(1, -1)
    sent = call(pick_kernel, [block] * MATCH, (near_col, key, value), limit=WHOLE_VMEM)

    far0 = to_group(GROUPS // 2)(sent[0])

    me = lax.axis_index("dom").reshape(1, 1)
    *held, info = call(
        split_kernel, [half] * 4 + [((5 * LIST, TILE), jnp.int32)],
        (me, tail, keys, ring_k[1], ring_k[2], ring_k[0], values, ring_v[1], ring_v[2], ring_v[0]),
        scalars=1, raw=range(2, 10),
        scratch=[pltpu.VMEM((4, TAIL, TILE), BF16), pltpu.SemaphoreType.DMA((20,))])
    held, info, sent = tied((held, info, sent))
    got = [over(x, link) for x, link in zip(held, THIRD)]
    far1 = switched(sent[1], codes[1])
    got, far1, sent2, sent3 = tied((got, far1, sent[2], sent[3]))
    packs = call(
        pack_kernel, [slots] * 4, (info, *held, *got), scalars=1, raw=range(1, 9),
        scratch=[pltpu.SemaphoreType.DMA((4, SLOTS))])
    packs, far0, sent2, sent3 = tied((packs, far0, sent2, sent3))
    packed = [over(x, link) for x, link in zip(packs, FOURTH)]
    far = [far0, far1, switched(sent2, codes[2]), switched(sent3, codes[3])]
    near_q, near_g, stats = call(
        pair_kernel, [node, node, ((96, ROWS), F32)], (near_col, near_row, query, key, value, cotangent, *far),
        scratch=[pltpu.VMEM((16, ROWS), F32)])

    acc = ((2, PAIRS, TILE, 2 * TILE), F32)
    row_stat = pltpu.VMEM((SLOTS, 8, 2 * TILE), F32)
    block_stat = pltpu.VMEM((2, 8, 2 * TILE), F32)
    by_col = pltpu.VMEM((2, PAIRS, TILE, 2 * TILE), BF16)
    by_row = pltpu.VMEM((2, PAIRS, 2 * TILE, TILE), BF16)
    tiles_b = pltpu.VMEM((SLOTS, TILE, WIDTH), BF16)
    tiles_f = pltpu.VMEM((SLOTS, TILE, WIDTH), F32)
    *terms, out_acc, gq_acc, grads = call(
        tile_kernel,
        [slots] * 4 + [acc, acc, ((64, ROWS), F32)],
        (info, near_col, near_row, *held, *got, *packed, tile_mask[0], query, cotangent, stats),
        scalars=1, raw=range(3, 16), cost=(1e9, 2e7), late=True,
        scratch=[
            tiles_b, tiles_b, pltpu.VMEM((SLOTS, PAIRS, TILE, 2 * TILE), F32),
            row_stat, row_stat, row_stat, block_stat, block_stat, block_stat,
            tiles_f, tiles_f,
            by_col, by_col, by_row, by_row, pltpu.VMEM((SLOTS, TILE, TILE), jnp.int32),
            pltpu.SemaphoreType.DMA((4, SLOTS)), pltpu.SemaphoreType.DMA((SLOTS,)),
        ],
    )

    theirs = [over(x, link) for x, link in zip(terms, FOURTH)]
    attended, grad_query, own, *back = call(
        rest_kernel,
        [node, node, ((2 * ROWS, WIDTH), F32)] + [block] * MATCH,
        (near_row, query, key, value, cotangent, *far, near_q, near_g, out_acc, gq_acc, grads))
    back0 = to_group(GROUPS // 2)(back[0])
    back1, back2 = switched(back[1], codes[1]), switched(back[2], codes[2])
    theirs, back1, back2, back3 = tied((theirs, back1, back2, back[3]))
    sums = call(second_kernel, [half] * 4, (info, *terms, *theirs), scalars=1, late=True)
    sums, back3 = tied((sums, back3))
    more = [over(x, link) for x, link in zip(sums, THIRD)]
    back3 = switched(back3, codes[3])
    more, back3 = tied((more, back3))
    *ring, kept_k, kept_v = call(
        third_kernel, [node] * 6 + [((ROWS, WIDTH), F32)] * 2, (info, *terms, *theirs, *more), scalars=1, late=True,
        scratch=[pltpu.VMEM((4, 4, ROWS, HALF), F32)])
    ring, back0 = tied((ring, back0))
    order = ((2, 8), (5, 2), (0, 4), (3, 1), (1, 12), (4, 3))
    arrived = {i: over(ring[i], link) for i, link in order}
    grad_key, grad_value = call(
        last_kernel, [node, node],
        (near_row, kept_k, kept_v, *(arrived[i] for i in range(6)), own, back0, back1, back2, back3))
    return attended, grad_query, grad_key, grad_value


def solution(mesh):
    rows = P(("grp", "dom"), None)
    return jax.shard_map(
        body,
        mesh=mesh,
        in_specs=(
            rows, rows, rows, rows,
            P(("grp", "dom"), None, None),
            P(("grp", "dom"), None, None, None),
            P(("grp", "dom")),
            rows,
            P(("grp", "dom"), None, None, None),
        ),
        out_specs=(rows, rows, rows, rows),
        check_vma=False,
    )
```
